32 devices in a mesh: groups: 2 (over y), acq: 8 (over z, x), rng: 2 (over core).
Axes of the slice: x: 2, y: 2, z: 4, core: 2. Of those that a mesh axis runs over, the one named last changes fastest.
Arguments:
- slc: bfloat16 [2, 16, 64, 2048], P(None, ('groups', 'acq'), None, 'rng'), parts along dimension 1, may hold values from -32 to 32, as said below
- map_cell: int32 [16, 256], P('groups', 'rng'), parts along dimension 0, may hold values from 0 to 16383, as said below
Outputs:
- geocoded: float32 [3, 8, 2, 16384], P(None, 'groups', None, ('acq', 'rng')), parts along dimension 1
The draws below stay inside these ranges and needn't reach their ends.
There are 2 independent parts, one for each index of `groups`. The reference program is written for one: setup_inputs(seed, part) draws one part's arguments, and reference() takes and returns one part's arrays. A program takes and returns all parts, laid end to end along the dimension named above; each array names one. Nothing has to cross between parts.
Inputs may be any that keep to these rules, and one draw needn't show every extreme that they name: `slc`: samples of an acquisition share a scene phase with the others, up to a per-sample phase drift. `map_cell`: A map cell is row * 128 + column on a grid of 128 rows; several radar cells may share one, and some map cells receive none. Nothing more is promised about where a radar cell lands.
All inputs are finite; a program needn't handle non-finite values.
Results may differ from the reference program's by a relative error of at most 0.0003.
Values may be sent and summed in bfloat16 or wider, within the bound.
No kernel may reach another device: no remote copies, remote signals or barrier semaphores. Data moves between devices by JAX's collectives and lax.ppermute only.
A program may use at most 128 MiB of HBM per device.

```python
import math
import jax
import jax.numpy as jnp
from jax import lax

LINES = 64
LOOK_A = 8
LOOK_R = 8
HALF_W = 4
ROUNDS = 3
MAPC = 16384
MAPROW = 128
MAPCOL = 128
ACQ = 8
PAIRS = 4
NRNG = 2048
MLL = 8
MLR = 256


def draw_slc(key, part):
    key_list = jax.random.split(jax.random.fold_in(key, 11), 4)
    grid_shape = (ACQ, LINES, NRNG)
    amplitude = jnp.exp(jax.random.uniform(key_list[0], (1, LINES, NRNG), minval=0.0, maxval=math.log(10.0)))
    spread = 0.8
    jitter_terms = 0.4 * jnp.clip(jax.random.normal(key_list[3], (2,) + grid_shape), -4.0, 4.0)
    scene_phase = jax.random.uniform(key_list[1], (1, LINES, NRNG), minval=-math.pi, maxval=math.pi)
    drift_phase = spread * jax.random.normal(key_list[2], grid_shape)
    full_phase = scene_phase + drift_phase
    real_part = amplitude * (jnp.cos(full_phase) + jitter_terms[0])
    imag_part = amplitude * (jnp.sin(full_phase) + jitter_terms[1])
    return jnp.clip(jnp.stack([real_part, imag_part]), -32.0, 32.0).astype(jnp.bfloat16)


def draw_map_cell(key, part):
    key_list = jax.random.split(jax.random.fold_in(key, 23), 4)
    line_ids = jnp.arange(MLL, dtype=jnp.int32)[:, None]
    col_ids = jnp.arange(MLR, dtype=jnp.int32)[None, :]
    row_step = MAPROW // MLL
    coarse_rows = MLL // 4 + 1
    coarse_cols = MLR // 8 + 1
    terrain_col = jax.random.randint(key_list[0], (coarse_rows, coarse_cols), 0, 4, dtype=jnp.int32)
    terrain_row = jax.random.randint(key_list[1], (coarse_rows, coarse_cols), 0, 2, dtype=jnp.int32)
    coarse_line = jnp.broadcast_to(line_ids // 4, (MLL, MLR))
    coarse_col = jnp.broadcast_to(col_ids // 8, (MLL, MLR))
    shift_col = terrain_col[coarse_line, coarse_col]
    shift_row = terrain_row[coarse_line, coarse_col]
    fine_row = jax.random.randint(key_list[2], (MLL, MLR), 0, max(row_step, 1), dtype=jnp.int32)
    fine_col = jax.random.randint(key_list[3], (MLL, MLR), 0, 2, dtype=jnp.int32)
    map_row = jnp.clip(line_ids * MAPROW // MLL + fine_row + shift_row, 0, MAPROW - 1)
    map_col = jnp.clip(col_ids * MAPCOL // MLR + fine_col + shift_col - 2, 0, MAPCOL - 1)
    cells = (map_row * MAPCOL + map_col).astype(jnp.int32)
    cells = cells.at[0, 0].set(0)
    cells = cells.at[MLL - 1, MLR - 1].set(MAPC - 1)
    return cells


def setup_inputs(seed: int = 0, part: int = 0) -> dict:
    key_of = jax.random.split(jax.random.key(seed), 3)
    part_keys = jax.random.split(jax.random.fold_in(key_of[2], part), 3)
    slc = draw_slc(jax.random.fold_in(jax.random.fold_in(key_of[2], part), 71), part)
    map_cell = draw_map_cell(jax.random.fold_in(jax.random.fold_in(key_of[2], part), 71), part)
    return {"slc": slc, "map_cell": map_cell}


def look_sum(values_in):
    line_count, col_count = values_in.shape
    return values_in.reshape(line_count // LOOK_A, LOOK_A, col_count // LOOK_R, LOOK_R).sum(axis=(1, 3))

def smooth_range(values_in):
    rim_width = HALF_W
    col_count = values_in.shape[-1]
    padded = jnp.pad(values_in, [(0, 0)] * (values_in.ndim - 1) + [(rim_width, rim_width)])
    summed = jnp.zeros_like(values_in)
    for offset in range(-rim_width, rim_width + 1):
        weight = (rim_width + 1 - abs(offset)) / float((rim_width + 1) ** 2)
        summed = summed + weight * padded[..., rim_width + offset:rim_width + offset + col_count]
    return summed

def filter_pair(lower_slc, upper_slc):
    real_part = lower_slc[0] * upper_slc[0] + lower_slc[1] * upper_slc[1]
    imag_part = lower_slc[1] * upper_slc[0] - lower_slc[0] * upper_slc[1]
    power_low = look_sum(lower_slc[0] * lower_slc[0] + lower_slc[1] * lower_slc[1])
    power_up = look_sum(upper_slc[0] * upper_slc[0] + upper_slc[1] * upper_slc[1])
    inverse = 1.0 / jnp.sqrt(power_low * power_up + 1e-06)
    gamma = jnp.stack([look_sum(real_part) * inverse, look_sum(imag_part) * inverse])
    smooth = smooth_range(gamma)
    gain_term = (smooth[0] * smooth[0] + smooth[1] * smooth[1] + 0.01) ** (-0.25)
    return smooth * gain_term[None]

def reference(slc, map_cell):
    flat_cells = map_cell.reshape(-1).astype(jnp.int32)
    counts = jax.ops.segment_sum(jnp.ones(flat_cells.shape, jnp.float32), flat_cells, MAPC)
    divisor = jnp.maximum(counts, 1.0)
    results = []
    for round_index in range(ROUNDS):
        stride = 2 ** round_index
        pair_ids = jnp.arange(PAIRS, dtype=jnp.int32)
        lower_ids = pair_ids // stride * (2 * stride) + pair_ids % stride

        def one_pair(lower_index):
            lower_slc = lax.dynamic_index_in_dim(slc, lower_index, 1, keepdims=False).astype(jnp.float32)
            upper_slc = lax.dynamic_index_in_dim(slc, lower_index + stride, 1, keepdims=False).astype(jnp.float32)
            filtered = filter_pair(lower_slc, upper_slc)
            cell_sums = jnp.zeros((2, MAPC), jnp.float32).at[:, flat_cells].add(filtered.reshape(2, -1))
            return cell_sums / divisor[None]
        results.append(lax.map(one_pair, lower_ids))
    return jnp.stack(results)
```

```python
import functools

import jax
import jax.numpy as jnp
from jax import lax
from jax.experimental import pallas as pl
from jax.experimental.pallas import tpu as pltpu
from jax.sharding import PartitionSpec as P

LOOK_A = 8
LOOK_R = 8
HALF_W = 4
ROUNDS = 3
BLOCK = 2**ROUNDS
MAPC = 16384
WIDE = 256
F32 = jnp.float32
BF16 = jnp.bfloat16

VMEM = pl.BlockSpec(memory_space=pltpu.VMEM)
SMEM = pl.BlockSpec(memory_space=pltpu.SMEM)


def in_two(value):
    high = value.astype(BF16)
    return high, (value - high.astype(F32)).astype(BF16)


def dot(left, right):
    return jnp.dot(left, right, preferred_element_type=F32)


def coherence_kernel(round_index, ids, own, other, out):
    half, width = other.shape[1:]
    looks, cells = half // LOOK_A, width // LOOK_R
    upper = (ids[0] >> round_index) & 1
    rows = pl.ds(pl.multiple_of(upper * half, half), half)
    mine_re, mine_im = own[0, rows, :].astype(F32), own[1, rows, :].astype(F32)
    their_re, their_im = other[0].astype(F32), other[1].astype(F32)
    terms = jnp.concatenate(
        [
            mine_re * their_re + mine_im * their_im,
            mine_im * their_re - mine_re * their_im,
            mine_re * mine_re + mine_im * mine_im,
            their_re * their_re + their_im * their_im,
        ],
        axis=0,
    )
    sample = lax.broadcasted_iota(jnp.int32, (width, cells), 0) // LOOK_R
    cell = lax.broadcasted_iota(jnp.int32, (width, cells), 1)
    take = (sample == cell).astype(F32).astype(BF16)
    high, low = in_two(terms)
    sums = dot(high, take) + dot(low, take)
    sums = sums.reshape(4 * looks, LOOK_A, cells).sum(axis=1)
    power = sums[2 * looks : 3 * looks] * sums[3 * looks :]
    inverse = lax.rsqrt(power + 1e-06)
    sign = (1 - 2 * upper).astype(F32)
    out[...] = sums[: 2 * looks] * jnp.concatenate([inverse, inverse * sign], axis=0)


def coherence(round_index, ids, own, other):
    looks, cells = other.shape[1] // LOOK_A, other.shape[2] // LOOK_R
    return pl.pallas_call(
        functools.partial(coherence_kernel, round_index),
        out_shape=jax.ShapeDtypeStruct((2 * looks, cells), F32),
        in_specs=[SMEM, VMEM, VMEM],
        out_specs=VMEM,
        name=f"coherence_{round_index}",
        cost_estimate=pl.CostEstimate(flops=2 * 2**20, bytes_accessed=2**18, transcendentals=0),
    )(ids, own, other)


def select_kernel(blocks, ids, own_cells, other_cells, band, onehot, masks, scale):
    lines, cols = own_cells.shape
    first = (2 * ids[0] + ids[1]) * blocks
    own, other = own_cells[...], other_cells[...]
    left_core = ids[1] == 0
    halves = [jnp.where(left_core, own, other), jnp.where(left_core, other, own)]
    lane = lax.broadcasted_iota(jnp.int32, (cols, WIDE), 1).astype(F32)
    for side, cells in enumerate(halves):
        low = (cells & (WIDE - 1)).astype(F32)
        tall = jnp.concatenate([low] * (cols // lines), axis=0).T
        for line in range(lines):
            hit = tall[:, line : line + 1] == lane
            start = (line * 2 + side) * cols
            onehot[start : start + cols, :] = hit.astype(F32).astype(BF16)
    wide = jnp.concatenate(halves, axis=1) // WIDE
    mine = [(wide == first + block).astype(F32) for block in range(blocks)]
    for line in range(lines):
        for block in range(blocks):
            masks[line * blocks + block : line * blocks + block + 1, :] = mine[block][line : line + 1]
    count = jnp.zeros((blocks * lines, WIDE), F32)
    for line in range(lines):
        rows = masks[line * blocks : (line + 1) * blocks, :]
        rows = jnp.concatenate([rows] * lines, axis=0).astype(BF16)
        count = count + dot(rows, onehot[line * 2 * cols : (line + 1) * 2 * cols, :])
    scale[...] = 1.0 / jnp.maximum(count[:blocks], 1.0)
    shift = lax.broadcasted_iota(jnp.int32, (2 * cols, 2 * cols), 0)
    shift = jnp.abs(shift - lax.broadcasted_iota(jnp.int32, (2 * cols, 2 * cols), 1))
    band[...] = jnp.maximum(HALF_W + 1 - shift, 0).astype(F32).astype(BF16)


def select(blocks, ids, own_cells, other_cells):
    lines, cols = own_cells.shape
    return pl.pallas_call(
        functools.partial(select_kernel, blocks),
        out_shape=(
            jax.ShapeDtypeStruct((2 * cols, 2 * cols), BF16),
            jax.ShapeDtypeStruct((lines * 2 * cols, WIDE), BF16),
            jax.ShapeDtypeStruct((lines * blocks, 2 * cols), F32),
            jax.ShapeDtypeStruct((blocks, WIDE), F32),
        ),
        in_specs=[SMEM, VMEM, VMEM],
        out_specs=(VMEM,) * 4,
        name="select",
        cost_estimate=pl.CostEstimate(flops=2 * 2**20, bytes_accessed=2**20, transcendentals=0),
    )(ids, own_cells, other_cells)


def geocode_kernel(ids, near, far, near_sent, far_sent, band, onehot, masks, scale, out, by_acq, grid, filt):
    pairs = BLOCK // 2
    looks = near.shape[2] // (2 * ROUNDS)
    lines, cols = 2 * looks, near.shape[3]
    planes = ROUNDS * pairs * 2
    blocks = scale.shape[0]

    def keep(first_half, second_half):
        for other in range(BLOCK):
            half = second_half if other & 1 else first_half
            by_acq[ids[0] ^ other] = half[other >> 1]

    @pl.when(ids[1] == 1)
    def _():
        keep(near, far)

    @pl.when(ids[1] == 0)
    def _():
        keep(near_sent, far_sent)

    for acq in range(BLOCK):
        for side in range(2):
            for r in range(ROUNDS):
                upper = acq >> r & 1
                pair = (acq >> (r + 1) << r) | (acq & (2**r - 1))
                for part in range(2):
                    row = ((r * pairs + pair) * 2 + part) * lines + upper * looks
                    start = (r * 2 + part) * looks
                    grid[row : row + looks, side * cols : (side + 1) * cols] = by_acq[
                        acq, side, start : start + looks, :
                    ]
    high, low = in_two(grid[...])
    smooth = (dot(high, band[...]) + dot(low, band[...])) * (1.0 / (HALF_W + 1) ** 2)
    smooth = smooth.reshape(planes // 2, 2, lines, 2 * cols)
    real, imag = smooth[:, 0], smooth[:, 1]
    gain = lax.rsqrt(jnp.sqrt(real * real + imag * imag + 0.01))
    filtered = (smooth * gain[:, None]).reshape(planes * lines, 2 * cols)
    for side in range(2):
        filt[side] = filtered[:, side * cols : (side + 1) * cols]
    left = []
    for line in range(lines):
        value = [filt[side, pl.ds(line, planes, stride=lines), :] for side in range(2)]
        value = jnp.concatenate(value, axis=1)
        top = value.astype(BF16).astype(F32)
        both = jnp.concatenate([top, value - top], axis=0)
        rows = [both * masks[line * blocks + block : line * blocks + block + 1, :] for block in range(blocks)]
        left.append(jnp.concatenate(rows, axis=0).astype(BF16))
    sums = dot(jnp.concatenate(left, axis=1), onehot[...])
    for block in range(blocks):
        start = block * 2 * planes
        total = sums[start : start + planes] + sums[start + planes : start + 2 * planes]
        total = total * scale[block : block + 1, :]
        for plane in range(0, planes, 2):
            r, pair = plane // (2 * pairs), plane // 2 % pairs
            out[r, pair, :, block * WIDE : (block + 1) * WIDE] = total[plane : plane + 2]


def geocode(ids, near, far, near_sent, far_sent, band, onehot, masks, scale):
    pairs, blocks = BLOCK // 2, scale.shape[0]
    _, _, rows, cols = near.shape
    lines = rows // ROUNDS
    return pl.pallas_call(
        geocode_kernel,
        out_shape=jax.ShapeDtypeStruct((ROUNDS, pairs, 2, blocks * WIDE), F32),
        in_specs=[SMEM] + [VMEM] * 8,
        out_specs=VMEM,
        scratch_shapes=[
            pltpu.VMEM((BLOCK, 2, rows, cols), F32),
            pltpu.VMEM((ROUNDS * pairs * 2 * lines, 2 * cols), F32),
            pltpu.VMEM((2, ROUNDS * pairs * 2 * lines, cols), F32),
        ],
        name="geocode",
        cost_estimate=pl.CostEstimate(flops=2**28, bytes_accessed=2**21, transcendentals=2**16),
    )(ids, near, far, near_sent, far_sent, band, onehot, masks, scale)


def over_cores(value, pairs):
    return lax.ppermute(value, "rng", pairs)


def over_chips(value, mask):
    count = lax.axis_size("acq")
    pairs = [(2 * a + 1, 2 * (a ^ mask) + 1) for a in range(count)]
    return lax.ppermute(value, ("acq", "rng"), pairs)


def gather_small(ids, packed, map_cell):
    piece = MAPC // (lax.axis_size("acq") * lax.axis_size("rng"))
    other_cells = over_cores(map_cell, [(0, 1), (1, 0)])
    chosen = select(piece // WIDE, ids, map_cell, other_cells)
    held = jnp.stack([over_cores(packed, [(0, 1)]), packed])[None]
    for bit in range(ROUNDS - 1, 0, -1):
        held = jnp.concatenate([held, over_chips(held, 2**bit)], axis=0)
    order = [0] * held.shape[0]
    for slot in range(held.shape[0]):
        index = 0
        for place, bit in enumerate(range(ROUNDS - 1, 0, -1)):
            index |= (slot >> place & 1) << (bit - 1)
        order[index] = slot
    held = jnp.stack([held[slot] for slot in order])
    far = over_chips(held, 1)
    near_sent, far_sent = over_cores(held, [(1, 0)]), over_cores(far, [(1, 0)])
    return geocode(ids, held, far, near_sent, far_sent, *chosen)


def gather_large(packed, map_cell):
    acq_count, rng_count = lax.axis_size("acq"), lax.axis_size("rng")
    pairs, piece = acq_count // 2, MAPC // (acq_count * rng_count)
    rows, cols = packed.shape
    looks = rows // (2 * ROUNDS)
    whole = lax.all_gather(packed, ("acq", "rng"))
    whole = whole.reshape(acq_count, rng_count, ROUNDS, 2, looks, cols)
    whole = whole.transpose(2, 0, 3, 4, 1, 5).reshape(ROUNDS, acq_count, 2, looks, rng_count * cols)
    grids = []
    for r in range(ROUNDS):
        split = whole[r].reshape(acq_count // 2 ** (r + 1), 2, 2**r, 2, looks, rng_count * cols)
        grids.append(
            split.transpose(0, 2, 3, 1, 4, 5).reshape(pairs, 2, 2 * looks, rng_count * cols)
        )
    gamma = jnp.stack(grids)
    width = gamma.shape[-1]
    padded = jnp.pad(gamma, [(0, 0)] * 4 + [(HALF_W, HALF_W)])
    smooth = jnp.zeros_like(gamma)
    for offset in range(-HALF_W, HALF_W + 1):
        weight = (HALF_W + 1 - abs(offset)) / float((HALF_W + 1) ** 2)
        smooth = smooth + weight * padded[..., HALF_W + offset : HALF_W + offset + width]
    power = smooth[:, :, 0] ** 2 + smooth[:, :, 1] ** 2 + 0.01
    filtered = smooth * (power ** (-0.25))[:, :, None]
    cells = lax.all_gather(map_cell, "rng", axis=1, tiled=True).reshape(-1, 1)
    first = (lax.axis_index("acq") * rng_count + lax.axis_index("rng")) * piece
    onehot = (cells == first + jnp.arange(piece, dtype=jnp.int32)).astype(F32)
    count = onehot.sum(axis=0)
    sums = jnp.dot(
        filtered.reshape(-1, cells.shape[0]), onehot, precision=lax.Precision.HIGHEST
    ).reshape(ROUNDS, pairs, 2, piece)
    return sums / jnp.maximum(count, 1.0)


def per_device(slc, map_cell):
    acq_count = lax.axis_size("acq")
    acq_rank = lax.axis_index("acq")
    ids = jnp.stack([acq_rank, lax.axis_index("rng")]).astype(jnp.int32)
    own = slc[:, 0]
    half = own.shape[1] // 2
    received = [None] * ROUNDS
    for r in range(ROUNDS - 1, -1, -1):
        start = (1 - (acq_rank >> r & 1)) * half
        partner_rows = lax.dynamic_slice_in_dim(own, start, half, 1)
        pairs = [(a, a ^ 2**r) for a in range(acq_count)]
        received[r] = lax.ppermute(partner_rows, "acq", pairs)
    packed = jnp.concatenate([coherence(r, ids, own, received[r]) for r in range(ROUNDS)], axis=0)
    if acq_count == BLOCK:
        return gather_small(ids, packed, map_cell)
    return gather_large(packed, map_cell)


def solution(mesh):
    in_specs = (P(None, ("groups", "acq"), None, "rng"), P("groups", "rng"))
    out_specs = P(None, "groups", None, ("acq", "rng"))
    return jax.shard_map(
        per_device, mesh=mesh, in_specs=in_specs, out_specs=out_specs, check_vma=False
    )
```

```python
import functools

import jax
import jax.numpy as jnp
from jax import lax
from jax.experimental import pallas as pl
from jax.experimental.pallas import tpu as pltpu
from jax.sharding import PartitionSpec as P

LOOK_A = 8
LOOK_R = 8
HALF_W = 4
ROUNDS = 3
BLOCK = 2**ROUNDS
STEPS = (4, 2, 1)
MAPC = 16384
WIDE = 256
F32 = jnp.float32
BF16 = jnp.bfloat16

VMEM = pl.BlockSpec(memory_space=pltpu.VMEM)


def in_two(value):
    high = value.astype(BF16)
    return high, (value - high.astype(F32)).astype(BF16)


def dot(left, right):
    return jnp.dot(left, right, preferred_element_type=F32)


def coherence_kernel(round_index, own, other, out):
    half, width = other.shape[1:]
    looks, cells = half // LOOK_A, width // LOOK_R
    upper = (lax.axis_index("acq") >> round_index) & 1
    rows = pl.ds(pl.multiple_of(upper * half, half), half)
    mine_re, mine_im = own[0, rows, :].astype(F32), own[1, rows, :].astype(F32)
    their_re, their_im = other[0].astype(F32), other[1].astype(F32)
    terms = jnp.concatenate(
        [
            mine_re * their_re + mine_im * their_im,
            mine_im * their_re - mine_re * their_im,
            mine_re * mine_re + mine_im * mine_im,
            their_re * their_re + their_im * their_im,
        ],
        axis=0,
    )
    sample = lax.broadcasted_iota(jnp.int32, (width, cells), 0) // LOOK_R
    cell = lax.broadcasted_iota(jnp.int32, (width, cells), 1)
    take = (sample == cell).astype(F32).astype(BF16)
    high, low = in_two(terms)
    sums = dot(high, take) + dot(low, take)
    sums = sums.reshape(4 * looks, LOOK_A, cells).sum(axis=1)
    power = sums[2 * looks : 3 * looks] * sums[3 * looks :]
    inverse = lax.rsqrt(power + 1e-06)
    sign = (1 - 2 * upper).astype(F32)
    out[...] = sums[: 2 * looks] * jnp.concatenate([inverse, inverse * sign], axis=0)


def coherence(round_index, own, other):
    looks, cells = other.shape[1] // LOOK_A, other.shape[2] // LOOK_R
    return pl.pallas_call(
        functools.partial(coherence_kernel, round_index),
        out_shape=jax.ShapeDtypeStruct((2 * looks, cells), F32),
        in_specs=[VMEM, VMEM],
        out_specs=VMEM,
        name=f"coherence_{round_index}",
        compiler_params=pltpu.CompilerParams(vmem_limit_bytes=4 * 2**20),
        cost_estimate=pl.CostEstimate(flops=2 * 2**20, bytes_accessed=2**18, transcendentals=0),
    )(own, other)


def select_kernel(blocks, own_cells, other_cells, band, onehot, masks, scale):
    lines, cols = own_cells.shape
    core = lax.axis_index("rng")
    first = (2 * lax.axis_index("acq") + core) * blocks
    own, other = own_cells[...], other_cells[...]
    left_core = core == 0
    halves = [jnp.where(left_core, own, other), jnp.where(left_core, other, own)]
    lane = lax.broadcasted_iota(jnp.int32, (cols, WIDE), 1).astype(F32)
    for side, cells in enumerate(halves):
        low = (cells & (WIDE - 1)).astype(F32)
        tall = jnp.concatenate([low] * (cols // lines), axis=0).T
        for line in range(lines):
            hit = tall[:, line : line + 1] == lane
            start = (line * 2 + side) * cols
            onehot[start : start + cols, :] = hit.astype(F32).astype(BF16)
    wide = jnp.concatenate(halves, axis=1) // WIDE
    mine = [(wide == first + block).astype(F32) for block in range(blocks)]
    for line in range(lines):
        for block in range(blocks):
            masks[line * blocks + block : line * blocks + block + 1, :] = mine[block][line : line + 1]
    count = jnp.zeros((blocks * lines, WIDE), F32)
    for line in range(lines):
        rows = masks[line * blocks : (line + 1) * blocks, :]
        rows = jnp.concatenate([rows] * lines, axis=0).astype(BF16)
        count = count + dot(rows, onehot[line * 2 * cols : (line + 1) * 2 * cols, :])
    scale[...] = 1.0 / jnp.maximum(count[:blocks], 1.0)
    shift = lax.broadcasted_iota(jnp.int32, (2 * cols, 2 * cols), 0)
    shift = jnp.abs(shift - lax.broadcasted_iota(jnp.int32, (2 * cols, 2 * cols), 1))
    band[...] = jnp.maximum(HALF_W + 1 - shift, 0).astype(F32).astype(BF16)


def select(blocks, own_cells, other_cells):
    lines, cols = own_cells.shape
    return pl.pallas_call(
        functools.partial(select_kernel, blocks),
        out_shape=(
            jax.ShapeDtypeStruct((2 * cols, 2 * cols), BF16),
            jax.ShapeDtypeStruct((lines * 2 * cols, WIDE), BF16),
            jax.ShapeDtypeStruct((lines * blocks, 2 * cols), F32),
            jax.ShapeDtypeStruct((blocks, WIDE), F32),
        ),
        in_specs=[VMEM, VMEM],
        out_specs=(VMEM,) * 4,
        name="select",
        compiler_params=pltpu.CompilerParams(vmem_limit_bytes=8 * 2**20),
        cost_estimate=pl.CostEstimate(flops=2 * 2**20, bytes_accessed=2**20, transcendentals=0),
    )(own_cells, other_cells)


def geocode_kernel(held, sent, band, onehot, masks, scale, out, by_acq, grid, filt):
    pairs = BLOCK // 2
    looks = held.shape[1] // (2 * ROUNDS)
    lines, cols = 2 * looks, held.shape[2]
    planes = ROUNDS * pairs * 2
    blocks = scale.shape[0]
    rank, core = lax.axis_index("acq"), lax.axis_index("rng")

    for slot in range(BLOCK):
        steps = [mask for i, mask in enumerate(STEPS) if slot >> i & 1]
        acq, side = rank ^ sum(steps), core ^ (len(steps) % 2)
        by_acq[acq, side] = held[slot]
        by_acq[acq, 1 - side] = sent[slot]
    for acq in range(BLOCK):
        for side in range(2):
            for r in range(ROUNDS):
                upper = acq >> r & 1
                pair = (acq >> (r + 1) << r) | (acq & (2**r - 1))
                for part in range(2):
                    row = ((r * pairs + pair) * 2 + part) * lines + upper * looks
                    start = (r * 2 + part) * looks
                    grid[row : row + looks, side * cols : (side + 1) * cols] = by_acq[
                        acq, side, start : start + looks, :
                    ]
    high, low = in_two(grid[...])
    smooth = (dot(high, band[...]) + dot(low, band[...])) * (1.0 / (HALF_W + 1) ** 2)
    smooth = smooth.reshape(planes // 2, 2, lines, 2 * cols)
    real, imag = smooth[:, 0], smooth[:, 1]
    gain = lax.rsqrt(jnp.sqrt(real * real + imag * imag + 0.01))
    filtered = (smooth * gain[:, None]).reshape(planes * lines, 2 * cols)
    for side in range(2):
        filt[side] = filtered[:, side * cols : (side + 1) * cols]
    left = []
    for line in range(lines):
        value = [filt[side, pl.ds(line, planes, stride=lines), :] for side in range(2)]
        value = jnp.concatenate(value, axis=1)
        top = value.astype(BF16).astype(F32)
        both = jnp.concatenate([top, value - top], axis=0)
        rows = [both * masks[line * blocks + block : line * blocks + block + 1, :] for block in range(blocks)]
        left.append(jnp.concatenate(rows, axis=0).astype(BF16))
    sums = dot(jnp.concatenate(left, axis=1), onehot[...])
    for block in range(blocks):
        start = block * 2 * planes
        total = sums[start : start + planes] + sums[start + planes : start + 2 * planes]
        total = total * scale[block : block + 1, :]
        for plane in range(0, planes, 2):
            r, pair = plane // (2 * pairs), plane // 2 % pairs
            out[r, pair, :, block * WIDE : (block + 1) * WIDE] = total[plane : plane + 2]


def geocode(held, sent, band, onehot, masks, scale):
    pairs, blocks = BLOCK // 2, scale.shape[0]
    _, rows, cols = held.shape
    lines = rows // ROUNDS
    return pl.pallas_call(
        geocode_kernel,
        out_shape=jax.ShapeDtypeStruct((ROUNDS, pairs, 2, blocks * WIDE), F32),
        in_specs=[VMEM] * 6,
        out_specs=VMEM,
        scratch_shapes=[
            pltpu.VMEM((BLOCK, 2, rows, cols), F32),
            pltpu.VMEM((ROUNDS * pairs * 2 * lines, 2 * cols), F32),
            pltpu.VMEM((2, ROUNDS * pairs * 2 * lines, cols), F32),
        ],
        name="geocode",
        compiler_params=pltpu.CompilerParams(vmem_limit_bytes=8 * 2**20),
        cost_estimate=pl.CostEstimate(flops=2**28, bytes_accessed=2**21, transcendentals=2**16),
    )(held, sent, band, onehot, masks, scale)


def gather_small(packed, chosen):
    held = packed[None]
    for mask in STEPS:
        pairs = [(2 * a + c, 2 * (a ^ mask) + 1 - c) for a in range(BLOCK) for c in range(2)]
        held = jnp.concatenate([held, lax.ppermute(held, ("acq", "rng"), pairs)], axis=0)
    return geocode(held, lax.ppermute(held, "rng", [(0, 1), (1, 0)]), *chosen)


def gather_large(packed, map_cell):
    acq_count, rng_count = lax.axis_size("acq"), lax.axis_size("rng")
    pairs, piece = acq_count // 2, MAPC // (acq_count * rng_count)
    rows, cols = packed.shape
    looks = rows // (2 * ROUNDS)
    whole = lax.all_gather(packed, ("acq", "rng"))
    whole = whole.reshape(acq_count, rng_count, ROUNDS, 2, looks, cols)
    whole = whole.transpose(2, 0, 3, 4, 1, 5).reshape(ROUNDS, acq_count, 2, looks, rng_count * cols)
    grids = []
    for r in range(ROUNDS):
        split = whole[r].reshape(acq_count // 2 ** (r + 1), 2, 2**r, 2, looks, rng_count * cols)
        grids.append(
            split.transpose(0, 2, 3, 1, 4, 5).reshape(pairs, 2, 2 * looks, rng_count * cols)
        )
    gamma = jnp.stack(grids)
    width = gamma.shape[-1]
    padded = jnp.pad(gamma, [(0, 0)] * 4 + [(HALF_W, HALF_W)])
    smooth = jnp.zeros_like(gamma)
    for offset in range(-HALF_W, HALF_W + 1):
        weight = (HALF_W + 1 - abs(offset)) / float((HALF_W + 1) ** 2)
        smooth = smooth + weight * padded[..., HALF_W + offset : HALF_W + offset + width]
    power = smooth[:, :, 0] ** 2 + smooth[:, :, 1] ** 2 + 0.01
    filtered = smooth * (power ** (-0.25))[:, :, None]
    cells = lax.all_gather(map_cell, "rng", axis=1, tiled=True).reshape(-1, 1)
    first = (lax.axis_index("acq") * rng_count + lax.axis_index("rng")) * piece
    onehot = (cells == first + jnp.arange(piece, dtype=jnp.int32)).astype(F32)
    count = onehot.sum(axis=0)
    sums = jnp.dot(
        filtered.reshape(-1, cells.shape[0]), onehot, precision=lax.Precision.HIGHEST
    ).reshape(ROUNDS, pairs, 2, piece)
    return sums / jnp.maximum(count, 1.0)


def per_device(slc, map_cell):
    acq_count = lax.axis_size("acq")
    acq_rank = lax.axis_index("acq")
    own = slc[:, 0]
    half = own.shape[1] // 2
    received = [None] * ROUNDS
    source = own
    for r in range(ROUNDS - 1, -1, -1):
        start = (1 - (acq_rank >> r & 1)) * half
        partner_rows = lax.dynamic_slice_in_dim(source, start, half, 1)
        pairs = [(a, a ^ 2**r) for a in range(acq_count)]
        received[r] = lax.ppermute(partner_rows, "acq", pairs)
        if r == ROUNDS - 1:
            source, _ = lax.optimization_barrier((own, partner_rows))
    small = acq_count == BLOCK
    if small:
        blocks = MAPC // (acq_count * lax.axis_size("rng")) // WIDE
        chosen = select(blocks, map_cell, lax.ppermute(map_cell, "rng", [(0, 1), (1, 0)]))
        own, chosen = lax.optimization_barrier((own, chosen))
    grids = []
    for r in range(ROUNDS):
        grids.append(coherence(r, own, received[r]))
        own, grids[r] = lax.optimization_barrier((own, grids[r]))
    packed = jnp.concatenate(grids, axis=0)
    return gather_small(packed, chosen) if small else gather_large(packed, map_cell)


def solution(mesh):
    in_specs = (P(None, ("groups", "acq"), None, "rng"), P("groups", "rng"))
    out_specs = P(None, "groups", None, ("acq", "rng"))
    return jax.shard_map(
        per_device, mesh=mesh, in_specs=in_specs, out_specs=out_specs, check_vma=False
    )
```

```python
import functools

import jax
import jax.numpy as jnp
from jax import lax
from jax.experimental import pallas as pl
from jax.experimental.pallas import tpu as pltpu
from jax.sharding import PartitionSpec as P

LOOK_A = 8
LOOK_R = 8
HALF_W = 4
ROUNDS = 3
BLOCK = 2**ROUNDS
STEPS = (4, 2, 1)
MAPC = 16384
WIDE = 256
F32 = jnp.float32
BF16 = jnp.bfloat16

VMEM = pl.BlockSpec(memory_space=pltpu.VMEM)


def in_two(value):
    high = value.astype(BF16)
    return high, (value - high.astype(F32)).astype(BF16)


def dot(left, right):
    return jnp.dot(left, right, preferred_element_type=F32)


def coherence_kernel(own, *refs):
    others, out = refs[:-1], refs[-1]
    half, width = others[0].shape[1:]
    looks, cells = half // LOOK_A, width // LOOK_R
    sample = lax.broadcasted_iota(jnp.int32, (width, cells), 0) // LOOK_R
    cell = lax.broadcasted_iota(jnp.int32, (width, cells), 1)
    take = (sample == cell).astype(F32).astype(BF16)
    for r, other in enumerate(others):
        upper = (lax.axis_index("acq") >> r) & 1
        rows = pl.ds(pl.multiple_of(upper * half, half), half)
        mine_re, mine_im = own[0, rows, :].astype(F32), own[1, rows, :].astype(F32)
        their_re, their_im = other[0].astype(F32), other[1].astype(F32)
        terms = jnp.concatenate(
            [
                mine_re * their_re + mine_im * their_im,
                mine_im * their_re - mine_re * their_im,
                mine_re * mine_re + mine_im * mine_im,
                their_re * their_re + their_im * their_im,
            ],
            axis=0,
        )
        high, low = in_two(terms)
        sums = dot(high, take) + dot(low, take)
        sums = sums.reshape(4 * looks, LOOK_A, cells).sum(axis=1)
        power = sums[2 * looks : 3 * looks] * sums[3 * looks :]
        inverse = lax.rsqrt(power + 1e-06)
        sign = (1 - 2 * upper).astype(F32)
        scale = jnp.concatenate([inverse, inverse * sign], axis=0)
        out[2 * looks * r : 2 * looks * (r + 1)] = sums[: 2 * looks] * scale


def coherence(own, others):
    looks, cells = others[0].shape[1] // LOOK_A, others[0].shape[2] // LOOK_R
    return pl.pallas_call(
        coherence_kernel,
        out_shape=jax.ShapeDtypeStruct((2 * ROUNDS * looks, cells), F32),
        in_specs=[VMEM] * (1 + ROUNDS),
        out_specs=VMEM,
        name="coherence",
        compiler_params=pltpu.CompilerParams(vmem_limit_bytes=4 * 2**20),
        cost_estimate=pl.CostEstimate(flops=6 * 2**20, bytes_accessed=2**18, transcendentals=0),
    )(own, *others)


def select_kernel(blocks, own_cells, other_cells, band, onehot, masks, scale):
    lines, cols = own_cells.shape
    core = lax.axis_index("rng")
    first = (2 * lax.axis_index("acq") + core) * blocks
    own, other = own_cells[...], other_cells[...]
    left_core = core == 0
    halves = [jnp.where(left_core, own, other), jnp.where(left_core, other, own)]
    lane = lax.broadcasted_iota(jnp.int32, (cols, WIDE), 1).astype(F32)
    for side, cells in enumerate(halves):
        low = (cells & (WIDE - 1)).astype(F32)
        tall = jnp.concatenate([low] * (cols // lines), axis=0).T
        for line in range(lines):
            hit = tall[:, line : line + 1] == lane
            start = (line * 2 + side) * cols
            onehot[start : start + cols, :] = hit.astype(F32).astype(BF16)
    wide = jnp.concatenate(halves, axis=1) // WIDE
    mine = [(wide == first + block).astype(F32) for block in range(blocks)]
    for line in range(lines):
        for block in range(blocks):
            masks[line * blocks + block : line * blocks + block + 1, :] = mine[block][line : line + 1]
    count = jnp.zeros((blocks * lines, WIDE), F32)
    for line in range(lines):
        rows = masks[line * blocks : (line + 1) * blocks, :]
        rows = jnp.concatenate([rows] * lines, axis=0).astype(BF16)
        count = count + dot(rows, onehot[line * 2 * cols : (line + 1) * 2 * cols, :])
    scale[...] = 1.0 / jnp.maximum(count[:blocks], 1.0)
    shift = lax.broadcasted_iota(jnp.int32, (2 * cols, 2 * cols), 0)
    shift = jnp.abs(shift - lax.broadcasted_iota(jnp.int32, (2 * cols, 2 * cols), 1))
    band[...] = jnp.maximum(HALF_W + 1 - shift, 0).astype(F32).astype(BF16)


def select(blocks, own_cells, other_cells):
    lines, cols = own_cells.shape
    return pl.pallas_call(
        functools.partial(select_kernel, blocks),
        out_shape=(
            jax.ShapeDtypeStruct((2 * cols, 2 * cols), BF16),
            jax.ShapeDtypeStruct((lines * 2 * cols, WIDE), BF16),
            jax.ShapeDtypeStruct((lines * blocks, 2 * cols), F32),
            jax.ShapeDtypeStruct((blocks, WIDE), F32),
        ),
        in_specs=[VMEM, VMEM],
        out_specs=(VMEM,) * 4,
        name="select",
        compiler_params=pltpu.CompilerParams(vmem_limit_bytes=8 * 2**20),
        cost_estimate=pl.CostEstimate(flops=2 * 2**20, bytes_accessed=2**20, transcendentals=0),
    )(own_cells, other_cells)


def geocode_kernel(held, sent, band, onehot, masks, scale, out, by_acq, grid, filt):
    pairs = BLOCK // 2
    looks = held.shape[1] // (2 * ROUNDS)
    lines, cols = 2 * looks, held.shape[2]
    planes = ROUNDS * pairs * 2
    blocks = scale.shape[0]
    rank, core = lax.axis_index("acq"), lax.axis_index("rng")

    for slot in range(BLOCK):
        steps = [mask for i, mask in enumerate(STEPS) if slot >> i & 1]
        acq, side = rank ^ sum(steps), core ^ (len(steps) % 2)
        by_acq[acq, side] = held[slot]
        by_acq[acq, 1 - side] = sent[slot]
    for acq in range(BLOCK):
        for side in range(2):
            for r in range(ROUNDS):
                upper = acq >> r & 1
                pair = (acq >> (r + 1) << r) | (acq & (2**r - 1))
                for part in range(2):
                    row = ((r * pairs + pair) * 2 + part) * lines + upper * looks
                    start = (r * 2 + part) * looks
                    grid[row : row + looks, side * cols : (side + 1) * cols] = by_acq[
                        acq, side, start : start + looks, :
                    ]
    high, low = in_two(grid[...])
    smooth = (dot(high, band[...]) + dot(low, band[...])) * (1.0 / (HALF_W + 1) ** 2)
    smooth = smooth.reshape(planes // 2, 2, lines, 2 * cols)
    real, imag = smooth[:, 0], smooth[:, 1]
    gain = lax.rsqrt(jnp.sqrt(real * real + imag * imag + 0.01))
    filtered = (smooth * gain[:, None]).reshape(planes * lines, 2 * cols)
    for side in range(2):
        filt[side] = filtered[:, side * cols : (side + 1) * cols]
    left = []
    for line in range(lines):
        value = [filt[side, pl.ds(line, planes, stride=lines), :] for side in range(2)]
        value = jnp.concatenate(value, axis=1)
        top = value.astype(BF16).astype(F32)
        both = jnp.concatenate([top, value - top], axis=0)
        rows = [both * masks[line * blocks + block : line * blocks + block + 1, :] for block in range(blocks)]
        left.append(jnp.concatenate(rows, axis=0).astype(BF16))
    sums = dot(jnp.concatenate(left, axis=1), onehot[...])
    for block in range(blocks):
        start = block * 2 * planes
        total = sums[start : start + planes] + sums[start + planes : start + 2 * planes]
        total = total * scale[block : block + 1, :]
        for plane in range(0, planes, 2):
            r, pair = plane // (2 * pairs), plane // 2 % pairs
            out[r, pair, :, block * WIDE : (block + 1) * WIDE] = total[plane : plane + 2]


def geocode(held, sent, band, onehot, masks, scale):
    pairs, blocks = BLOCK // 2, scale.shape[0]
    _, rows, cols = held.shape
    lines = rows // ROUNDS
    return pl.pallas_call(
        geocode_kernel,
        out_shape=jax.ShapeDtypeStruct((ROUNDS, pairs, 2, blocks * WIDE), F32),
        in_specs=[VMEM] * 6,
        out_specs=VMEM,
        scratch_shapes=[
            pltpu.VMEM((BLOCK, 2, rows, cols), F32),
            pltpu.VMEM((ROUNDS * pairs * 2 * lines, 2 * cols), F32),
            pltpu.VMEM((2, ROUNDS * pairs * 2 * lines, cols), F32),
        ],
        name="geocode",
        compiler_params=pltpu.CompilerParams(vmem_limit_bytes=8 * 2**20),
        cost_estimate=pl.CostEstimate(flops=2**28, bytes_accessed=2**21, transcendentals=2**16),
    )(held, sent, band, onehot, masks, scale)


def gather_small(packed, chosen):
    held = packed[None]
    for mask in STEPS:
        pairs = [(2 * a + c, 2 * (a ^ mask) + 1 - c) for a in range(BLOCK) for c in range(2)]
        held = jnp.concatenate([held, lax.ppermute(held, ("acq", "rng"), pairs)], axis=0)
    return geocode(held, lax.ppermute(held, "rng", [(0, 1), (1, 0)]), *chosen)


def gather_large(packed, map_cell):
    acq_count, rng_count = lax.axis_size("acq"), lax.axis_size("rng")
    pairs, piece = acq_count // 2, MAPC // (acq_count * rng_count)
    rows, cols = packed.shape
    looks = rows // (2 * ROUNDS)
    whole = lax.all_gather(packed, ("acq", "rng"))
    whole = whole.reshape(acq_count, rng_count, ROUNDS, 2, looks, cols)
    whole = whole.transpose(2, 0, 3, 4, 1, 5).reshape(ROUNDS, acq_count, 2, looks, rng_count * cols)
    grids = []
    for r in range(ROUNDS):
        split = whole[r].reshape(acq_count // 2 ** (r + 1), 2, 2**r, 2, looks, rng_count * cols)
        grids.append(
            split.transpose(0, 2, 3, 1, 4, 5).reshape(pairs, 2, 2 * looks, rng_count * cols)
        )
    gamma = jnp.stack(grids)
    width = gamma.shape[-1]
    padded = jnp.pad(gamma, [(0, 0)] * 4 + [(HALF_W, HALF_W)])
    smooth = jnp.zeros_like(gamma)
    for offset in range(-HALF_W, HALF_W + 1):
        weight = (HALF_W + 1 - abs(offset)) / float((HALF_W + 1) ** 2)
        smooth = smooth + weight * padded[..., HALF_W + offset : HALF_W + offset + width]
    power = smooth[:, :, 0] ** 2 + smooth[:, :, 1] ** 2 + 0.01
    filtered = smooth * (power ** (-0.25))[:, :, None]
    cells = lax.all_gather(map_cell, "rng", axis=1, tiled=True).reshape(-1, 1)
    first = (lax.axis_index("acq") * rng_count + lax.axis_index("rng")) * piece
    onehot = (cells == first + jnp.arange(piece, dtype=jnp.int32)).astype(F32)
    count = onehot.sum(axis=0)
    sums = jnp.dot(
        filtered.reshape(-1, cells.shape[0]), onehot, precision=lax.Precision.HIGHEST
    ).reshape(ROUNDS, pairs, 2, piece)
    return sums / jnp.maximum(count, 1.0)


def per_device(slc, map_cell):
    acq_count = lax.axis_size("acq")
    acq_rank = lax.axis_index("acq")
    own = slc[:, 0]
    half = own.shape[1] // 2
    received = [None] * ROUNDS
    source = own
    for r in range(ROUNDS - 1, -1, -1):
        start = (1 - (acq_rank >> r & 1)) * half
        partner_rows = lax.dynamic_slice_in_dim(source, start, half, 1)
        pairs = [(a, a ^ 2**r) for a in range(acq_count)]
        received[r] = lax.ppermute(partner_rows, "acq", pairs)
        if r == ROUNDS - 1:
            source, _ = lax.optimization_barrier((own, partner_rows))
    small = acq_count == BLOCK
    if small:
        blocks = MAPC // (acq_count * lax.axis_size("rng")) // WIDE
        chosen = select(blocks, map_cell, lax.ppermute(map_cell, "rng", [(0, 1), (1, 0)]))
        own, chosen = lax.optimization_barrier((own, chosen))
    packed = coherence(own, received)
    return gather_small(packed, chosen) if small else gather_large(packed, map_cell)


def solution(mesh):
    in_specs = (P(None, ("groups", "acq"), None, "rng"), P("groups", "rng"))
    out_specs = P(None, "groups", None, ("acq", "rng"))
    return jax.shard_map(
        per_device, mesh=mesh, in_specs=in_specs, out_specs=out_specs, check_vma=False
    )
```

```python
import functools

import jax
import jax.numpy as jnp
from jax import lax
from jax.experimental import pallas as pl
from jax.experimental.pallas import tpu as pltpu
from jax.sharding import PartitionSpec as P

LOOK_A = 8
LOOK_R = 8
HALF_W = 4
ROUNDS = 3
BLOCK = 2**ROUNDS
STEPS = (4, 2, 1)
SEND = (2, 0, 3, 1)
WHOLE = ((1, 0), (2, 2), (2, 0), (1, 2))
MAPC = 16384
WIDE = 256
F32 = jnp.float32
BF16 = jnp.bfloat16

VMEM = pl.BlockSpec(memory_space=pltpu.VMEM)


def in_two(value):
    high = value.astype(BF16)
    return high, (value - high.astype(F32)).astype(BF16)


def dot(left, right):
    return jnp.dot(left, right, preferred_element_type=F32)


def coherence_kernel(bit, own, other, out):
    lines, width = own.shape[1:]
    count = other.shape[1]
    cells, looks = width // LOOK_R, count // LOOK_A
    upper = (lax.axis_index("acq") >> bit) & 1
    rows = pl.ds(pl.multiple_of(upper * count, count), count) if count < lines else slice(None)
    mine_re, mine_im = own[0, rows, :].astype(F32), own[1, rows, :].astype(F32)
    their_re, their_im = other[0].astype(F32), other[1].astype(F32)
    terms = jnp.concatenate(
        [
            mine_re * their_re + mine_im * their_im,
            mine_im * their_re - mine_re * their_im,
            mine_re * mine_re + mine_im * mine_im,
            their_re * their_re + their_im * their_im,
        ],
        axis=0,
    )
    sample = lax.broadcasted_iota(jnp.int32, (width, cells), 0) // LOOK_R
    cell = lax.broadcasted_iota(jnp.int32, (width, cells), 1)
    take = (sample == cell).astype(F32).astype(BF16)
    high, low = in_two(terms)
    sums = dot(high, take) + dot(low, take)
    sums = sums.reshape(4 * looks, LOOK_A, cells).sum(axis=1)
    power = sums[2 * looks : 3 * looks] * sums[3 * looks :]
    inverse = lax.rsqrt(power + 1e-06)
    sign = (1 - 2 * upper).astype(F32)
    out[...] = sums[: 2 * looks] * jnp.concatenate([inverse, inverse * sign], axis=0)


def coherence(bit, own, other):
    looks, cells = other.shape[1] // LOOK_A, own.shape[2] // LOOK_R
    return pl.pallas_call(
        functools.partial(coherence_kernel, bit),
        out_shape=jax.ShapeDtypeStruct((2 * looks, cells), F32),
        in_specs=[VMEM, VMEM],
        out_specs=VMEM,
        name=f"coherence_{bit}",
        compiler_params=pltpu.CompilerParams(vmem_limit_bytes=4 * 2**20),
        cost_estimate=pl.CostEstimate(flops=2 * 2**20, bytes_accessed=2**18, transcendentals=0),
    )(own, other)


def select_kernel(blocks, own_cells, other_cells, band, onehot, masks, scale):
    lines, cols = own_cells.shape
    core = lax.axis_index("rng")
    first = (2 * lax.axis_index("acq") + core) * blocks
    own, other = own_cells[...], other_cells[...]
    left_core = core == 0
    halves = [jnp.where(left_core, own, other), jnp.where(left_core, other, own)]
    lane = lax.broadcasted_iota(jnp.int32, (cols, WIDE), 1).astype(F32)
    for side, cells in enumerate(halves):
        low = (cells & (WIDE - 1)).astype(F32)
        tall = jnp.concatenate([low] * (cols // lines), axis=0).T
        for line in range(lines):
            hit = tall[:, line : line + 1] == lane
            start = (line * 2 + side) * cols
            onehot[start : start + cols, :] = hit.astype(F32).astype(BF16)
    wide = jnp.concatenate(halves, axis=1) // WIDE
    mine = [(wide == first + block).astype(F32) for block in range(blocks)]
    for line in range(lines):
        for block in range(blocks):
            masks[line * blocks + block : line * blocks + block + 1, :] = mine[block][line : line + 1]
    count = jnp.zeros((blocks * lines, WIDE), F32)
    for line in range(lines):
        rows = masks[line * blocks : (line + 1) * blocks, :]
        rows = jnp.concatenate([rows] * lines, axis=0).astype(BF16)
        count = count + dot(rows, onehot[line * 2 * cols : (line + 1) * 2 * cols, :])
    scale[...] = 1.0 / jnp.maximum(count[:blocks], 1.0)
    shift = lax.broadcasted_iota(jnp.int32, (2 * cols, 2 * cols), 0)
    shift = jnp.abs(shift - lax.broadcasted_iota(jnp.int32, (2 * cols, 2 * cols), 1))
    band[...] = jnp.maximum(HALF_W + 1 - shift, 0).astype(F32).astype(BF16)


def select(blocks, own_cells, other_cells):
    lines, cols = own_cells.shape
    return pl.pallas_call(
        functools.partial(select_kernel, blocks),
        out_shape=(
            jax.ShapeDtypeStruct((2 * cols, 2 * cols), BF16),
            jax.ShapeDtypeStruct((lines * 2 * cols, WIDE), BF16),
            jax.ShapeDtypeStruct((lines * blocks, 2 * cols), F32),
            jax.ShapeDtypeStruct((blocks, WIDE), F32),
        ),
        in_specs=[VMEM, VMEM],
        out_specs=(VMEM,) * 4,
        name="select",
        compiler_params=pltpu.CompilerParams(vmem_limit_bytes=8 * 2**20),
        cost_estimate=pl.CostEstimate(flops=2 * 2**20, bytes_accessed=2**20, transcendentals=0),
    )(own_cells, other_cells)


def geocode_kernel(held, sent, band, onehot, masks, scale, out, by_acq, grid, filt):
    pairs = BLOCK // 2
    looks = held.shape[1] // 6
    lines, cols = 2 * looks, held.shape[2]
    planes = ROUNDS * pairs * 2
    blocks = scale.shape[0]
    rank, core = lax.axis_index("acq"), lax.axis_index("rng")
    for slot in range(BLOCK):
        steps = [mask for i, mask in enumerate(STEPS) if slot >> i & 1]
        acq, side = rank ^ sum(steps), core ^ (len(steps) % 2)
        by_acq[acq, side] = held[slot]
        by_acq[acq, 1 - side] = sent[slot]
    for side in range(2):
        columns = slice(side * cols, (side + 1) * cols)
        for acq in range(BLOCK):
            for part in range(2):
                row = (acq // 2 * 2 + part) * lines + (acq & 1) * looks
                grid[row : row + looks, columns] = by_acq[acq, side, part * looks : (part + 1) * looks, :]
            r, pair = WHOLE[acq >> 1]
            row = (r * pairs + pair + (acq & 1)) * 2 * lines
            grid[row : row + 2 * lines, columns] = by_acq[acq, side, lines:, :]
    high, low = in_two(grid[...])
    smooth = (dot(high, band[...]) + dot(low, band[...])) * (1.0 / (HALF_W + 1) ** 2)
    smooth = smooth.reshape(planes // 2, 2, lines, 2 * cols)
    real, imag = smooth[:, 0], smooth[:, 1]
    gain = lax.rsqrt(jnp.sqrt(real * real + imag * imag + 0.01))
    filtered = (smooth * gain[:, None]).reshape(planes * lines, 2 * cols)
    for side in range(2):
        filt[side] = filtered[:, side * cols : (side + 1) * cols]
    left = []
    for line in range(lines):
        value = [filt[side, pl.ds(line, planes, stride=lines), :] for side in range(2)]
        value = jnp.concatenate(value, axis=1)
        top = value.astype(BF16).astype(F32)
        both = jnp.concatenate([top, value - top], axis=0)
        rows = [both * masks[line * blocks + block : line * blocks + block + 1, :] for block in range(blocks)]
        left.append(jnp.concatenate(rows, axis=0).astype(BF16))
    sums = dot(jnp.concatenate(left, axis=1), onehot[...])
    for block in range(blocks):
        start = block * 2 * planes
        total = sums[start : start + planes] + sums[start + planes : start + 2 * planes]
        total = total * scale[block : block + 1, :]
        for plane in range(0, planes, 2):
            r, pair = plane // (2 * pairs), plane // 2 % pairs
            out[r, pair, :, block * WIDE : (block + 1) * WIDE] = total[plane : plane + 2]


def geocode(held, sent, band, onehot, masks, scale):
    pairs, blocks = BLOCK // 2, scale.shape[0]
    _, rows, cols = held.shape
    lines = rows // 3
    return pl.pallas_call(
        geocode_kernel,
        out_shape=jax.ShapeDtypeStruct((ROUNDS, pairs, 2, blocks * WIDE), F32),
        in_specs=[VMEM] * 6,
        out_specs=VMEM,
        scratch_shapes=[
            pltpu.VMEM((BLOCK, 2, rows, cols), F32),
            pltpu.VMEM((ROUNDS * pairs * 2 * lines, 2 * cols), F32),
            pltpu.VMEM((2, ROUNDS * pairs * 2 * lines, cols), F32),
        ],
        name="geocode",
        compiler_params=pltpu.CompilerParams(vmem_limit_bytes=8 * 2**20),
        cost_estimate=pl.CostEstimate(flops=2**28, bytes_accessed=2**21, transcendentals=2**16),
    )(held, sent, band, onehot, masks, scale)


def across(value, mask):
    pairs = [(2 * a + c, 2 * (a ^ mask) + 1 - c) for a in range(BLOCK) for c in range(2)]
    return lax.ppermute(value, ("acq", "rng"), pairs)


def gather_small(packed, chosen):
    held = packed[None]
    for mask in STEPS:
        held = jnp.concatenate([held, across(held, mask)], axis=0)
    return geocode(held, lax.ppermute(held, "rng", [(0, 1), (1, 0)]), *chosen)


def gather_large(packed, map_cell):
    acq_count, rng_count = lax.axis_size("acq"), lax.axis_size("rng")
    pairs, piece = acq_count // 2, MAPC // (acq_count * rng_count)
    rows, cols = packed.shape
    lines, looks, width = rows // 3, rows // 6, rng_count * cols
    whole = lax.all_gather(packed, ("acq", "rng")).reshape(acq_count, rng_count, rows, cols)
    whole = whole.transpose(0, 2, 1, 3).reshape(acq_count, rows, width)
    halves = whole[:, :lines].reshape(pairs, 2, 2, looks, width)
    grids = [halves.transpose(0, 2, 1, 3, 4).reshape(pairs, 2, lines, width)]
    planes = whole[:, lines:].reshape(acq_count // BLOCK, 4, 2, 2, lines, width)
    for r in range(1, ROUNDS):
        quads = sorted((pair, quad) for quad, (found, pair) in enumerate(WHOLE) if found == r)
        grid = jnp.stack([planes[:, quad] for _, quad in quads], axis=1)
        grids.append(grid.reshape(pairs, 2, lines, width))
    gamma = jnp.stack(grids)
    padded = jnp.pad(gamma, [(0, 0)] * 4 + [(HALF_W, HALF_W)])
    smooth = jnp.zeros_like(gamma)
    for offset in range(-HALF_W, HALF_W + 1):
        weight = (HALF_W + 1 - abs(offset)) / float((HALF_W + 1) ** 2)
        smooth = smooth + weight * padded[..., HALF_W + offset : HALF_W + offset + width]
    power = smooth[:, :, 0] ** 2 + smooth[:, :, 1] ** 2 + 0.01
    filtered = smooth * (power ** (-0.25))[:, :, None]
    cells = lax.all_gather(map_cell, "rng", axis=1, tiled=True).reshape(-1, 1)
    first = (lax.axis_index("acq") * rng_count + lax.axis_index("rng")) * piece
    onehot = (cells == first + jnp.arange(piece, dtype=jnp.int32)).astype(F32)
    count = onehot.sum(axis=0)
    sums = jnp.dot(
        filtered.reshape(-1, cells.shape[0]), onehot, precision=lax.Precision.HIGHEST
    ).reshape(ROUNDS, pairs, 2, piece)
    return sums / jnp.maximum(count, 1.0)


def per_device(slc, map_cell):
    acq_count = lax.axis_size("acq")
    acq_rank = lax.axis_index("acq")
    own = slc[:, 0]
    half = own.shape[1] // 2
    quarter = [(a & -BLOCK) + 2 * SEND[a % BLOCK // 2] + a % 2 for a in range(acq_count)]
    whole = lax.ppermute(own, "acq", list(enumerate(quarter)))
    part = lax.dynamic_slice_in_dim(own, (1 - acq_rank % 2) * half, half, 1)
    part = lax.ppermute(part, "acq", [(a, a ^ 1) for a in range(acq_count)])
    small = acq_count == BLOCK
    if small:
        blocks = MAPC // (acq_count * lax.axis_size("rng")) // WIDE
        chosen = select(blocks, map_cell, lax.ppermute(map_cell, "rng", [(0, 1), (1, 0)]))
        own, chosen = lax.optimization_barrier((own, chosen))
    packed = jnp.concatenate([coherence(0, own, part), coherence(2, own, whole)], axis=0)
    return gather_small(packed, chosen) if small else gather_large(packed, map_cell)


def solution(mesh):
    in_specs = (P(None, ("groups", "acq"), None, "rng"), P("groups", "rng"))
    out_specs = P(None, "groups", None, ("acq", "rng"))
    return jax.shard_map(
        per_device, mesh=mesh, in_specs=in_specs, out_specs=out_specs, check_vma=False
    )
```

```python
import functools

import jax
import jax.numpy as jnp
from jax import lax
from jax.experimental import pallas as pl
from jax.experimental.pallas import tpu as pltpu
from jax.sharding import PartitionSpec as P

LOOK_A = 8
LOOK_R = 8
HALF_W = 4
ROUNDS = 3
BLOCK = 2**ROUNDS
STEPS = (4, 2, 1)
SEND = (2, 0, 3, 1)
WHOLE = ((1, 0), (2, 2), (2, 0), (1, 2))
MAPC = 16384
WIDE = 256
UNIT = 32760.0
F32 = jnp.float32
BF16 = jnp.bfloat16

VMEM = pl.BlockSpec(memory_space=pltpu.VMEM)


def in_two(value):
    high = value.astype(BF16)
    return high, (value - high.astype(F32)).astype(BF16)


def squared(root):
    root = root.astype(F32)
    return root * jnp.abs(root)


def dot(left, right):
    return jnp.dot(left, right, preferred_element_type=F32)


def pick_kernel(own, out):
    half = out.shape[1]
    upper = lax.axis_index("acq") & 1
    out[...] = own[:, pl.ds(pl.multiple_of((1 - upper) * half, half), half), :]


def pick(own):
    parts, lines, width = own.shape
    return pl.pallas_call(
        pick_kernel,
        out_shape=jax.ShapeDtypeStruct((parts, lines // 2, width), own.dtype),
        in_specs=[VMEM],
        out_specs=VMEM,
        name="pick",
        compiler_params=pltpu.CompilerParams(vmem_limit_bytes=2 * 2**20),
        cost_estimate=pl.CostEstimate(flops=2**10, bytes_accessed=2**18, transcendentals=0),
    )(own)


def look_sums(terms, take):
    high, low = in_two(terms)
    sums = dot(high, take) + dot(low, take)
    return sums.reshape(terms.shape[0] // LOOK_A, LOOK_A, take.shape[1]).sum(axis=1)


def products(mine_re, mine_im, their_re, their_im):
    return [
        mine_re * their_re + mine_im * their_im,
        mine_im * their_re - mine_re * their_im,
        their_re * their_re + their_im * their_im,
    ]


def normalised(sums, power, sign):
    looks = power.shape[0]
    inverse = lax.rsqrt(power * sums[2 * looks :] + 1e-06)
    return sums[: 2 * looks] * jnp.concatenate([inverse, inverse * sign], axis=0)


def first_kernel(own, other, take, out, power):
    half = other.shape[1]
    looks = half // LOOK_A
    mine_re, mine_im = own[0].astype(F32), own[1].astype(F32)
    power[...] = look_sums(mine_re * mine_re + mine_im * mine_im, take[...])
    upper = lax.axis_index("acq") & 1
    rows = pl.ds(pl.multiple_of(upper * half, half), half)
    terms = products(own[0, rows, :].astype(F32), own[1, rows, :].astype(F32), other[0].astype(F32), other[1].astype(F32))
    sums = look_sums(jnp.concatenate(terms, axis=0), take[...])
    mine = jnp.where(upper == 1, power[looks:], power[:looks])
    out[...] = normalised(sums, mine, (1 - 2 * upper).astype(F32))


def first_matching(own, other, take):
    looks, cells = other.shape[1] // LOOK_A, own.shape[2] // LOOK_R
    shape = jax.ShapeDtypeStruct((2 * looks, cells), F32)
    return pl.pallas_call(
        first_kernel,
        out_shape=(shape, shape),
        in_specs=[VMEM] * 3,
        out_specs=(VMEM, VMEM),
        name="first_matching",
        compiler_params=pltpu.CompilerParams(vmem_limit_bytes=4 * 2**20),
        cost_estimate=pl.CostEstimate(flops=2 * 2**20, bytes_accessed=2**18, transcendentals=0),
    )(own, other, take)


def whole_kernel(own, other, take, power, first, out):
    upper = (lax.axis_index("acq") >> 2) & 1
    terms = products(own[0].astype(F32), own[1].astype(F32), other[0].astype(F32), other[1].astype(F32))
    sums = look_sums(jnp.concatenate(terms, axis=0), take[...])
    whole = normalised(sums, power[...], (1 - 2 * upper).astype(F32))
    packed = jnp.concatenate([first[...], whole], axis=0)
    root = jnp.sqrt(jnp.abs(packed)) * UNIT
    out[...] = jnp.round(jnp.where(packed < 0, -root, root)).astype(jnp.int32).astype(jnp.int16)


def whole_pair(own, other, take, power, first):
    rows, cells = first.shape
    return pl.pallas_call(
        whole_kernel,
        out_shape=jax.ShapeDtypeStruct((3 * rows, cells), jnp.int16),
        in_specs=[VMEM] * 5,
        out_specs=VMEM,
        name="whole_pair",
        compiler_params=pltpu.CompilerParams(vmem_limit_bytes=4 * 2**20),
        cost_estimate=pl.CostEstimate(flops=2 * 2**20, bytes_accessed=2**18, transcendentals=0),
    )(own, other, take, power, first)


def take_kernel(take):
    sample = lax.broadcasted_iota(jnp.int32, take.shape, 0) // LOOK_R
    cell = lax.broadcasted_iota(jnp.int32, take.shape, 1)
    take[...] = (sample == cell).astype(F32).astype(BF16)


def taking(width):
    return pl.pallas_call(
        take_kernel,
        out_shape=jax.ShapeDtypeStruct((width, width // LOOK_R), BF16),
        out_specs=VMEM,
        name="taking",
        compiler_params=pltpu.CompilerParams(vmem_limit_bytes=2 * 2**20),
        cost_estimate=pl.CostEstimate(flops=2**17, bytes_accessed=2**18, transcendentals=0),
    )()


def select_kernel(blocks, own_cells, other_cells, band, onehot, masks, scale):
    lines, cols = own_cells.shape
    core = lax.axis_index("rng")
    first = (2 * lax.axis_index("acq") + core) * blocks
    own, other = own_cells[...], other_cells[...]
    left_core = core == 0
    halves = [jnp.where(left_core, own, other), jnp.where(left_core, other, own)]
    lane = lax.broadcasted_iota(jnp.int32, (cols, WIDE), 1).astype(F32)
    for side, cells in enumerate(halves):
        low = (cells & (WIDE - 1)).astype(F32)
        tall = jnp.concatenate([low] * (cols // lines), axis=0).T
        for line in range(lines):
            hit = tall[:, line : line + 1] == lane
            start = (line * 2 + side) * cols
            onehot[start : start + cols, :] = hit.astype(F32).astype(BF16)
    wide = jnp.concatenate(halves, axis=1) // WIDE
    mine = [(wide == first + block).astype(F32) for block in range(blocks)]
    for line in range(lines):
        for block in range(blocks):
            masks[line * blocks + block : line * blocks + block + 1, :] = mine[block][line : line + 1]
    count = jnp.zeros((blocks * lines, WIDE), F32)
    for line in range(lines):
        rows = masks[line * blocks : (line + 1) * blocks, :]
        rows = jnp.concatenate([rows] * lines, axis=0).astype(BF16)
        count = count + dot(rows, onehot[line * 2 * cols : (line + 1) * 2 * cols, :])
    scale[...] = 1.0 / jnp.maximum(count[:blocks], 1.0)
    shift = lax.broadcasted_iota(jnp.int32, (2 * cols, 2 * cols), 0)
    shift = jnp.abs(shift - lax.broadcasted_iota(jnp.int32, (2 * cols, 2 * cols), 1))
    band[...] = jnp.maximum(HALF_W + 1 - shift, 0).astype(F32).astype(BF16)


def select(blocks, own_cells, other_cells):
    lines, cols = own_cells.shape
    return pl.pallas_call(
        functools.partial(select_kernel, blocks),
        out_shape=(
            jax.ShapeDtypeStruct((2 * cols, 2 * cols), BF16),
            jax.ShapeDtypeStruct((lines * 2 * cols, WIDE), BF16),
            jax.ShapeDtypeStruct((lines * blocks, 2 * cols), F32),
            jax.ShapeDtypeStruct((blocks, WIDE), F32),
        ),
        in_specs=[VMEM, VMEM],
        out_specs=(VMEM,) * 4,
        name="select",
        compiler_params=pltpu.CompilerParams(vmem_limit_bytes=8 * 2**20),
        cost_estimate=pl.CostEstimate(flops=2 * 2**20, bytes_accessed=2**20, transcendentals=0),
    )(own_cells, other_cells)


def geocode_kernel(held, sent, band, onehot, masks, scale, out, by_acq, grid, filt):
    pairs = BLOCK // 2
    looks = held.shape[1] // 6
    lines, cols = 2 * looks, held.shape[2]
    planes = ROUNDS * pairs * 2
    blocks = scale.shape[0]
    rank, core = lax.axis_index("acq"), lax.axis_index("rng")
    for slot in range(BLOCK):
        steps = [mask for i, mask in enumerate(STEPS) if slot >> i & 1]
        acq, side = rank ^ sum(steps), core ^ (len(steps) % 2)
        by_acq[acq, side] = squared(held[slot].astype(jnp.int32))
        by_acq[acq, 1 - side] = squared(sent[slot].astype(jnp.int32))
    for side in range(2):
        columns = slice(side * cols, (side + 1) * cols)
        for acq in range(BLOCK):
            for part in range(2):
                row = (acq // 2 * 2 + part) * lines + (acq & 1) * looks
                grid[row : row + looks, columns] = by_acq[acq, side, part * looks : (part + 1) * looks, :]
            r, pair = WHOLE[acq >> 1]
            row = (r * pairs + pair + (acq & 1)) * 2 * lines
            grid[row : row + 2 * lines, columns] = by_acq[acq, side, lines:, :]
    high, low = in_two(grid[...])
    smooth = (dot(high, band[...]) + dot(low, band[...])) * (1.0 / (UNIT * (HALF_W + 1)) ** 2)
    smooth = smooth.reshape(planes // 2, 2, lines, 2 * cols)
    real, imag = smooth[:, 0], smooth[:, 1]
    gain = lax.rsqrt(jnp.sqrt(real * real + imag * imag + 0.01))
    filtered = (smooth * gain[:, None]).reshape(planes * lines, 2 * cols)
    for side in range(2):
        filt[side] = filtered[:, side * cols : (side + 1) * cols]
    left = []
    for line in range(lines):
        value = [filt[side, pl.ds(line, planes, stride=lines), :] for side in range(2)]
        value = jnp.concatenate(value, axis=1)
        top = value.astype(BF16).astype(F32)
        both = jnp.concatenate([top, value - top], axis=0)
        rows = [both * masks[line * blocks + block : line * blocks + block + 1, :] for block in range(blocks)]
        left.append(jnp.concatenate(rows, axis=0).astype(BF16))
    sums = dot(jnp.concatenate(left, axis=1), onehot[...])
    for block in range(blocks):
        start = block * 2 * planes
        total = sums[start : start + planes] + sums[start + planes : start + 2 * planes]
        total = total * scale[block : block + 1, :]
        for plane in range(0, planes, 2):
            r, pair = plane // (2 * pairs), plane // 2 % pairs
            out[r, pair, :, block * WIDE : (block + 1) * WIDE] = total[plane : plane + 2]


def geocode(held, sent, band, onehot, masks, scale):
    pairs, blocks = BLOCK // 2, scale.shape[0]
    _, rows, cols = held.shape
    lines = rows // 3
    return pl.pallas_call(
        geocode_kernel,
        out_shape=jax.ShapeDtypeStruct((ROUNDS, pairs, 2, blocks * WIDE), F32),
        in_specs=[VMEM] * 6,
        out_specs=VMEM,
        scratch_shapes=[
            pltpu.VMEM((BLOCK, 2, rows, cols), F32),
            pltpu.VMEM((ROUNDS * pairs * 2 * lines, 2 * cols), F32),
            pltpu.VMEM((2, ROUNDS * pairs * 2 * lines, cols), F32),
        ],
        name="geocode",
        compiler_params=pltpu.CompilerParams(vmem_limit_bytes=8 * 2**20),
        cost_estimate=pl.CostEstimate(flops=2**28, bytes_accessed=2**21, transcendentals=2**16),
    )(held, sent, band, onehot, masks, scale)


def across(value, mask):
    pairs = [(2 * a + c, 2 * (a ^ mask) + 1 - c) for a in range(BLOCK) for c in range(2)]
    return lax.ppermute(value, ("acq", "rng"), pairs)


def gather_small(packed, chosen):
    held = packed[None]
    for mask in STEPS:
        held = jnp.concatenate([held, across(held, mask)], axis=0)
    return geocode(held, lax.ppermute(held, "rng", [(0, 1), (1, 0)]), *chosen)


def gather_large(packed, map_cell):
    acq_count, rng_count = lax.axis_size("acq"), lax.axis_size("rng")
    pairs, piece = acq_count // 2, MAPC // (acq_count * rng_count)
    rows, cols = packed.shape
    lines, looks, width = rows // 3, rows // 6, rng_count * cols
    whole = lax.all_gather(packed, ("acq", "rng")).reshape(acq_count, rng_count, rows, cols)
    whole = whole.transpose(0, 2, 1, 3).reshape(acq_count, rows, width)
    whole = squared(whole) / UNIT**2
    halves = whole[:, :lines].reshape(pairs, 2, 2, looks, width)
    grids = [halves.transpose(0, 2, 1, 3, 4).reshape(pairs, 2, lines, width)]
    planes = whole[:, lines:].reshape(acq_count // BLOCK, 4, 2, 2, lines, width)
    for r in range(1, ROUNDS):
        quads = sorted((pair, quad) for quad, (found, pair) in enumerate(WHOLE) if found == r)
        grid = jnp.stack([planes[:, quad] for _, quad in quads], axis=1)
        grids.append(grid.reshape(pairs, 2, lines, width))
    gamma = jnp.stack(grids)
    padded = jnp.pad(gamma, [(0, 0)] * 4 + [(HALF_W, HALF_W)])
    smooth = jnp.zeros_like(gamma)
    for offset in range(-HALF_W, HALF_W + 1):
        weight = (HALF_W + 1 - abs(offset)) / float((HALF_W + 1) ** 2)
        smooth = smooth + weight * padded[..., HALF_W + offset : HALF_W + offset + width]
    power = smooth[:, :, 0] ** 2 + smooth[:, :, 1] ** 2 + 0.01
    filtered = smooth * (power ** (-0.25))[:, :, None]
    cells = lax.all_gather(map_cell, "rng", axis=1, tiled=True).reshape(-1, 1)
    first = (lax.axis_index("acq") * rng_count + lax.axis_index("rng")) * piece
    onehot = (cells == first + jnp.arange(piece, dtype=jnp.int32)).astype(F32)
    count = onehot.sum(axis=0)
    sums = jnp.dot(
        filtered.reshape(-1, cells.shape[0]), onehot, precision=lax.Precision.HIGHEST
    ).reshape(ROUNDS, pairs, 2, piece)
    return sums / jnp.maximum(count, 1.0)


def per_device(slc, map_cell):
    acq_count = lax.axis_size("acq")
    own = slc[:, 0]
    quarter = [(a & -BLOCK) + 2 * SEND[a % BLOCK // 2] + a % 2 for a in range(acq_count)]
    whole = lax.ppermute(own, "acq", list(enumerate(quarter)))
    half = lax.ppermute(pick(own), "acq", [(a, a ^ 1) for a in range(acq_count)])
    small = acq_count == BLOCK
    take = taking(own.shape[2])
    if small:
        blocks = MAPC // (acq_count * lax.axis_size("rng")) // WIDE
        chosen = select(blocks, map_cell, lax.ppermute(map_cell, "rng", [(0, 1), (1, 0)]))
        take, chosen = lax.optimization_barrier((take, chosen))
    first, power = first_matching(own, half, take)
    packed = whole_pair(own, whole, take, power, first)
    return gather_small(packed, chosen) if small else gather_large(packed, map_cell)


def solution(mesh):
    in_specs = (P(None, ("groups", "acq"), None, "rng"), P("groups", "rng"))
    out_specs = P(None, "groups", None, ("acq", "rng"))
    return jax.shard_map(
        per_device, mesh=mesh, in_specs=in_specs, out_specs=out_specs, check_vma=False
    )
```

```python
import functools

import jax
import jax.numpy as jnp
from jax import lax
from jax.experimental import pallas as pl
from jax.experimental.pallas import tpu as pltpu
from jax.sharding import PartitionSpec as P

LOOK_A = 8
LOOK_R = 8
HALF_W = 4
ROUNDS = 3
BLOCK = 2**ROUNDS
STEPS = ((1,), (6, 4, 2))
SEND = (2, 0, 3, 1)
WHOLE = ((1, 0), (2, 2), (2, 0), (1, 2))
MAPC = 16384
LANES = 128
WIDE = 256
UNIT = 32760.0
F32 = jnp.float32
BF16 = jnp.bfloat16

VMEM = pl.BlockSpec(memory_space=pltpu.VMEM)


def dot(left, right):
    return jnp.dot(left, right, preferred_element_type=F32)


def dot_in_two(left, right):
    rows = left.shape[0]
    high = left.astype(BF16).astype(F32)
    both = dot(jnp.concatenate([high, left - high], axis=0).astype(BF16), right)
    return both[:rows] + both[rows:]


def squared(root):
    root = root.astype(F32)
    return root * jnp.abs(root)


def pick_kernel(own, out):
    half = out.shape[1]
    upper = lax.axis_index("acq") & 1
    out[...] = own[:, pl.ds(pl.multiple_of((1 - upper) * half, half), half), :]


def pick(own):
    parts, lines, width = own.shape
    return pl.pallas_call(
        pick_kernel,
        out_shape=jax.ShapeDtypeStruct((parts, lines // 2, width), own.dtype),
        in_specs=[VMEM],
        out_specs=VMEM,
        name="pick",
        compiler_params=pltpu.CompilerParams(vmem_limit_bytes=2 * 2**20),
        cost_estimate=pl.CostEstimate(flops=2**10, bytes_accessed=2**18, transcendentals=0),
    )(own)


def look_sums(terms, take):
    sums = dot_in_two(terms, take)
    return sums.reshape(terms.shape[0] // LOOK_A, LOOK_A, take.shape[1]).sum(axis=1)


def products(mine_re, mine_im, their_re, their_im):
    return [
        mine_re * their_re + mine_im * their_im,
        mine_im * their_re - mine_re * their_im,
        their_re * their_re + their_im * their_im,
    ]


def normalised(sums, power, sign):
    looks = power.shape[0]
    inverse = lax.rsqrt(power * sums[2 * looks :] + 1e-06)
    return sums[: 2 * looks] * jnp.concatenate([inverse, inverse * sign], axis=0)


def spread(samples, part, wide, out):
    blocks, looks = wide.shape[1], out.shape[3]
    for j in range(blocks):
        wide[part, j] = samples[part, :, j * LANES : (j + 1) * LANES].astype(F32)
        for i in range(LOOK_A):
            out[part, j, i] = wide[part, j, pl.ds(i, looks, stride=LOOK_A), :]


def first_kernel(own, other, take, out, power, mine, wide):
    half = other.shape[1]
    looks = half // LOOK_A
    own_re, own_im = own[0].astype(F32), own[1].astype(F32)
    power[...] = look_sums(own_re * own_re + own_im * own_im, take[...])
    upper = lax.axis_index("acq") & 1
    rows = pl.ds(pl.multiple_of(upper * half, half), half)
    terms = products(own[0, rows, :].astype(F32), own[1, rows, :].astype(F32), other[0].astype(F32), other[1].astype(F32))
    sums = look_sums(jnp.concatenate(terms, axis=0), take[...])
    half_power = jnp.where(upper == 1, power[looks:], power[:looks])
    out[...] = normalised(sums, half_power, (1 - 2 * upper).astype(F32))
    for part in range(2):
        spread(own, part, wide, mine)


def first_matching(own, other, take):
    parts, lines, width = own.shape
    looks, cells = lines // LOOK_A, width // LOOK_R
    blocks = width // LANES
    shape = jax.ShapeDtypeStruct((looks, cells), F32)
    return pl.pallas_call(
        first_kernel,
        out_shape=(shape, shape, jax.ShapeDtypeStruct((parts, blocks, LOOK_A, looks, LANES), F32)),
        in_specs=[VMEM] * 3,
        out_specs=(VMEM,) * 3,
        scratch_shapes=[pltpu.VMEM((parts, blocks, lines, LANES), F32)],
        name="first_matching",
        compiler_params=pltpu.CompilerParams(vmem_limit_bytes=4 * 2**20),
        cost_estimate=pl.CostEstimate(flops=2 * 2**20, bytes_accessed=2**18, transcendentals=0),
    )(own, other, take)


def whole_kernel(mine, other, take, power, first, out, wide):
    upper = (lax.axis_index("acq") >> 2) & 1
    blocks, looks = mine.shape[1], mine.shape[3]
    columns = []
    for j in range(blocks):
        for part in range(2):
            wide[part, j] = other[part, :, j * LANES : (j + 1) * LANES].astype(F32)
        total = 0.0
        for i in range(LOOK_A):
            their_re, their_im = (wide[part, j, pl.ds(i, looks, stride=LOOK_A), :] for part in range(2))
            terms = products(mine[0, j, i], mine[1, j, i], their_re, their_im)
            total = total + jnp.concatenate(terms, axis=0)
        columns.append(total)
    sums = dot_in_two(jnp.concatenate(columns, axis=1), take[...])
    whole = normalised(sums, power[...], (1 - 2 * upper).astype(F32))
    packed = jnp.concatenate([first[...], whole], axis=0)
    root = jnp.sqrt(jnp.abs(packed)) * UNIT
    out[...] = jnp.round(jnp.where(packed < 0, -root, root)).astype(jnp.int32).astype(jnp.int16)


def whole_pair(mine, other, take, power, first):
    rows, cells = first.shape
    parts, lines, width = other.shape
    return pl.pallas_call(
        whole_kernel,
        out_shape=jax.ShapeDtypeStruct((3 * rows, cells), jnp.int16),
        in_specs=[VMEM] * 5,
        out_specs=VMEM,
        scratch_shapes=[pltpu.VMEM((parts, width // LANES, lines, LANES), F32)],
        name="whole_pair",
        compiler_params=pltpu.CompilerParams(vmem_limit_bytes=4 * 2**20),
        cost_estimate=pl.CostEstimate(flops=2 * 2**20, bytes_accessed=2**18, transcendentals=0),
    )(mine, other, take, power, first)


def take_kernel(take):
    sample = lax.broadcasted_iota(jnp.int32, take.shape, 0) // LOOK_R
    cell = lax.broadcasted_iota(jnp.int32, take.shape, 1)
    take[...] = (sample == cell).astype(F32).astype(BF16)


def taking(width):
    return pl.pallas_call(
        take_kernel,
        out_shape=jax.ShapeDtypeStruct((width, width // LOOK_R), BF16),
        out_specs=VMEM,
        name="taking",
        compiler_params=pltpu.CompilerParams(vmem_limit_bytes=2 * 2**20),
        cost_estimate=pl.CostEstimate(flops=2**17, bytes_accessed=2**18, transcendentals=0),
    )()


def select_kernel(blocks, own_cells, other_cells, band, onehot, masks, scale):
    lines, cols = own_cells.shape
    core = lax.axis_index("rng")
    first = (2 * lax.axis_index("acq") + core) * blocks
    own, other = own_cells[...], other_cells[...]
    left_core = core == 0
    halves = [jnp.where(left_core, own, other), jnp.where(left_core, other, own)]
    lane = lax.broadcasted_iota(jnp.int32, (cols, WIDE), 1).astype(F32)
    for side, cells in enumerate(halves):
        low = (cells & (WIDE - 1)).astype(F32)
        tall = jnp.concatenate([low] * (cols // lines), axis=0).T
        for line in range(lines):
            hit = tall[:, line : line + 1] == lane
            start = (line * 2 + side) * cols
            onehot[start : start + cols, :] = hit.astype(F32).astype(BF16)
    wide = jnp.concatenate(halves, axis=1) // WIDE
    mine = [(wide == first + block).astype(F32) for block in range(blocks)]
    for line in range(lines):
        for block in range(blocks):
            masks[line * blocks + block : line * blocks + block + 1, :] = mine[block][line : line + 1]
    count = jnp.zeros((blocks * lines, WIDE), F32)
    for line in range(lines):
        rows = masks[line * blocks : (line + 1) * blocks, :]
        rows = jnp.concatenate([rows] * lines, axis=0).astype(BF16)
        count = count + dot(rows, onehot[line * 2 * cols : (line + 1) * 2 * cols, :])
    scale[...] = 1.0 / jnp.maximum(count[:blocks], 1.0)
    shift = lax.broadcasted_iota(jnp.int32, (2 * cols, 2 * cols), 0)
    shift = jnp.abs(shift - lax.broadcasted_iota(jnp.int32, (2 * cols, 2 * cols), 1))
    band[...] = jnp.maximum(HALF_W + 1 - shift, 0).astype(F32).astype(BF16)


def select(blocks, own_cells, other_cells):
    lines, cols = own_cells.shape
    return pl.pallas_call(
        functools.partial(select_kernel, blocks),
        out_shape=(
            jax.ShapeDtypeStruct((2 * cols, 2 * cols), BF16),
            jax.ShapeDtypeStruct((lines * 2 * cols, WIDE), BF16),
            jax.ShapeDtypeStruct((lines * blocks, 2 * cols), F32),
            jax.ShapeDtypeStruct((blocks, WIDE), F32),
        ),
        in_specs=[VMEM, VMEM],
        out_specs=(VMEM,) * 4,
        name="select",
        compiler_params=pltpu.CompilerParams(vmem_limit_bytes=8 * 2**20),
        cost_estimate=pl.CostEstimate(flops=2 * 2**20, bytes_accessed=2**20, transcendentals=0),
    )(own_cells, other_cells)


def geocode_kernel(held, sent, band, onehot, masks, scale, out, by_acq, grid, filt):
    pairs = BLOCK // 2
    looks = held.shape[1] // 6
    lines, cols = 2 * looks, held.shape[2]
    planes = ROUNDS * pairs * 2
    blocks = scale.shape[0]
    rank, core = lax.axis_index("acq"), lax.axis_index("rng")
    origins = [(0, 0)]
    for step in STEPS:
        origins = origins + [(bits ^ mask, 1 - other) for mask in step for bits, other in origins]
    for slot, (bits, other) in enumerate(origins):
        acq, side = rank ^ bits, core ^ other
        by_acq[acq, side] = squared(held[slot].astype(jnp.int32))
        by_acq[acq, 1 - side] = squared(sent[slot].astype(jnp.int32))
    for side in range(2):
        columns = slice(side * cols, (side + 1) * cols)
        for acq in range(BLOCK):
            for part in range(2):
                row = (acq // 2 * 2 + part) * lines + (acq & 1) * looks
                grid[row : row + looks, columns] = by_acq[acq, side, part * looks : (part + 1) * looks, :]
            r, pair = WHOLE[acq >> 1]
            row = (r * pairs + pair + (acq & 1)) * 2 * lines
            grid[row : row + 2 * lines, columns] = by_acq[acq, side, lines:, :]
    smooth = dot_in_two(grid[...], band[...]) * (1.0 / (UNIT * (HALF_W + 1)) ** 2)
    smooth = smooth.reshape(planes // 2, 2, lines, 2 * cols)
    real, imag = smooth[:, 0], smooth[:, 1]
    gain = lax.rsqrt(jnp.sqrt(real * real + imag * imag + 0.01))
    filtered = (smooth * gain[:, None]).reshape(planes * lines, 2 * cols)
    for side in range(2):
        filt[side] = filtered[:, side * cols : (side + 1) * cols]
    left = []
    for line in range(lines):
        value = [filt[side, pl.ds(line, planes, stride=lines), :] for side in range(2)]
        value = jnp.concatenate(value, axis=1)
        top = value.astype(BF16).astype(F32)
        both = jnp.concatenate([top, value - top], axis=0)
        rows = [both * masks[line * blocks + block : line * blocks + block + 1, :] for block in range(blocks)]
        left.append(jnp.concatenate(rows, axis=0).astype(BF16))
    sums = dot(jnp.concatenate(left, axis=1), onehot[...])
    for block in range(blocks):
        start = block * 2 * planes
        total = sums[start : start + planes] + sums[start + planes : start + 2 * planes]
        total = total * scale[block : block + 1, :]
        for plane in range(0, planes, 2):
            r, pair = plane // (2 * pairs), plane // 2 % pairs
            out[r, pair, :, block * WIDE : (block + 1) * WIDE] = total[plane : plane + 2]


def geocode(held, sent, band, onehot, masks, scale):
    pairs, blocks = BLOCK // 2, scale.shape[0]
    _, rows, cols = held.shape
    lines = rows // 3
    return pl.pallas_call(
        geocode_kernel,
        out_shape=jax.ShapeDtypeStruct((ROUNDS, pairs, 2, blocks * WIDE), F32),
        in_specs=[VMEM] * 6,
        out_specs=VMEM,
        scratch_shapes=[
            pltpu.VMEM((BLOCK, 2, rows, cols), F32),
            pltpu.VMEM((ROUNDS * pairs * 2 * lines, 2 * cols), F32),
            pltpu.VMEM((2, ROUNDS * pairs * 2 * lines, cols), F32),
        ],
        name="geocode",
        compiler_params=pltpu.CompilerParams(vmem_limit_bytes=8 * 2**20),
        cost_estimate=pl.CostEstimate(flops=2**28, bytes_accessed=2**21, transcendentals=2**16),
    )(held, sent, band, onehot, masks, scale)


def across(value, mask):
    pairs = [(2 * a + c, 2 * (a ^ mask) + 1 - c) for a in range(BLOCK) for c in range(2)]
    return lax.ppermute(value, ("acq", "rng"), pairs)


def gather_small(packed, chosen):
    held = packed[None]
    for step in STEPS:
        held = jnp.concatenate([held] + [across(held, mask) for mask in step], axis=0)
    return geocode(held, lax.ppermute(held, "rng", [(0, 1), (1, 0)]), *chosen)


def gather_large(packed, map_cell):
    acq_count, rng_count = lax.axis_size("acq"), lax.axis_size("rng")
    pairs, piece = acq_count // 2, MAPC // (acq_count * rng_count)
    rows, cols = packed.shape
    lines, looks, width = rows // 3, rows // 6, rng_count * cols
    whole = lax.all_gather(packed, ("acq", "rng")).reshape(acq_count, rng_count, rows, cols)
    whole = whole.transpose(0, 2, 1, 3).reshape(acq_count, rows, width)
    whole = squared(whole) / UNIT**2
    halves = whole[:, :lines].reshape(pairs, 2, 2, looks, width)
    grids = [halves.transpose(0, 2, 1, 3, 4).reshape(pairs, 2, lines, width)]
    planes = whole[:, lines:].reshape(acq_count // BLOCK, 4, 2, 2, lines, width)
    for r in range(1, ROUNDS):
        quads = sorted((pair, quad) for quad, (found, pair) in enumerate(WHOLE) if found == r)
        grid = jnp.stack([planes[:, quad] for _, quad in quads], axis=1)
        grids.append(grid.reshape(pairs, 2, lines, width))
    gamma = jnp.stack(grids)
    padded = jnp.pad(gamma, [(0, 0)] * 4 + [(HALF_W, HALF_W)])
    smooth = jnp.zeros_like(gamma)
    for offset in range(-HALF_W, HALF_W + 1):
        weight = (HALF_W + 1 - abs(offset)) / float((HALF_W + 1) ** 2)
        smooth = smooth + weight * padded[..., HALF_W + offset : HALF_W + offset + width]
    power = smooth[:, :, 0] ** 2 + smooth[:, :, 1] ** 2 + 0.01
    filtered = smooth * (power ** (-0.25))[:, :, None]
    cells = lax.all_gather(map_cell, "rng", axis=1, tiled=True).reshape(-1, 1)
    first = (lax.axis_index("acq") * rng_count + lax.axis_index("rng")) * piece
    onehot = (cells == first + jnp.arange(piece, dtype=jnp.int32)).astype(F32)
    count = onehot.sum(axis=0)
    sums = jnp.dot(
        filtered.reshape(-1, cells.shape[0]), onehot, precision=lax.Precision.HIGHEST
    ).reshape(ROUNDS, pairs, 2, piece)
    return sums / jnp.maximum(count, 1.0)


def per_device(slc, map_cell):
    acq_count = lax.axis_size("acq")
    own = slc[:, 0]
    quarter = [(a & -BLOCK) + 2 * SEND[a % BLOCK // 2] + a % 2 for a in range(acq_count)]
    whole = lax.ppermute(own, "acq", list(enumerate(quarter)))
    half = lax.ppermute(pick(own), "acq", [(a, a ^ 1) for a in range(acq_count)])
    small = acq_count == BLOCK
    take = taking(own.shape[2])
    if small:
        blocks = MAPC // (acq_count * lax.axis_size("rng")) // WIDE
        chosen = select(blocks, map_cell, lax.ppermute(map_cell, "rng", [(0, 1), (1, 0)]))
        take, chosen = lax.optimization_barrier((take, chosen))
    first, power, mine = first_matching(own, half, take)
    packed = whole_pair(mine, whole, take, power, first)
    return gather_small(packed, chosen) if small else gather_large(packed, map_cell)


def solution(mesh):
    in_specs = (P(None, ("groups", "acq"), None, "rng"), P("groups", "rng"))
    out_specs = P(None, "groups", None, ("acq", "rng"))
    return jax.shard_map(
        per_device, mesh=mesh, in_specs=in_specs, out_specs=out_specs, check_vma=False
    )
```

```python
import functools

import jax
import jax.numpy as jnp
from jax import lax
from jax.experimental import pallas as pl
from jax.experimental.pallas import tpu as pltpu
from jax.sharding import PartitionSpec as P

LOOK_A = 8
LOOK_R = 8
HALF_W = 4
ROUNDS = 3
BLOCK = 2**ROUNDS
STEPS = ((1,), (6, 4, 2))
SEND = (2, 0, 3, 1)
WHOLE = ((1, 0), (2, 2), (2, 0), (1, 2))
MAPC = 16384
LANES = 128
WIDE = 256
UNIT = 32760.0
F32 = jnp.float32
BF16 = jnp.bfloat16

VMEM = pl.BlockSpec(memory_space=pltpu.VMEM)


def dot(left, right):
    return jnp.dot(left, right, preferred_element_type=F32)


def dot_in_two(left, right):
    rows = left.shape[0]
    high = left.astype(BF16).astype(F32)
    both = dot(jnp.concatenate([high, left - high], axis=0).astype(BF16), right)
    return both[:rows] + both[rows:]


def squared(root):
    root = root.astype(F32)
    return root * jnp.abs(root)


def pick_kernel(own, out):
    half = out.shape[1]
    upper = lax.axis_index("acq") & 1
    out[...] = own[:, pl.ds(pl.multiple_of((1 - upper) * half, half), half), :]


def pick(own):
    parts, lines, width = own.shape
    return pl.pallas_call(
        pick_kernel,
        out_shape=jax.ShapeDtypeStruct((parts, lines // 2, width), own.dtype),
        in_specs=[VMEM],
        out_specs=VMEM,
        name="pick",
        compiler_params=pltpu.CompilerParams(vmem_limit_bytes=2 * 2**20),
        cost_estimate=pl.CostEstimate(flops=2**10, bytes_accessed=2**18, transcendentals=0),
    )(own)


def look_sums(terms, take):
    sums = dot_in_two(terms, take)
    return sums.reshape(terms.shape[0] // LOOK_A, LOOK_A, take.shape[1]).sum(axis=1)


def products(mine_re, mine_im, their_re, their_im):
    return [
        mine_re * their_re + mine_im * their_im,
        mine_im * their_re - mine_re * their_im,
        their_re * their_re + their_im * their_im,
    ]


def normalised(sums, power, sign):
    looks = power.shape[0]
    inverse = lax.rsqrt(power * sums[2 * looks :] + 1e-06)
    return sums[: 2 * looks] * jnp.concatenate([inverse, inverse * sign], axis=0)


def spread(samples, part, wide, out):
    blocks, looks = wide.shape[1], out.shape[3]
    for j in range(blocks):
        wide[part, j, : samples.shape[1]] = samples[part, :, j * LANES : (j + 1) * LANES].astype(F32)
        for i in range(LOOK_A):
            out[part, j, i] = wide[part, j, pl.ds(i, looks, stride=LOOK_A), :]


def first_kernel(own, other, take, out, power, mine, wide):
    half = other.shape[1]
    looks = half // LOOK_A
    own_re, own_im = own[0].astype(F32), own[1].astype(F32)
    power[...] = look_sums(own_re * own_re + own_im * own_im, take[...])
    upper = lax.axis_index("acq") & 1
    rows = pl.ds(pl.multiple_of(upper * half, half), half)
    terms = products(own[0, rows, :].astype(F32), own[1, rows, :].astype(F32), other[0].astype(F32), other[1].astype(F32))
    sums = look_sums(jnp.concatenate(terms, axis=0), take[...])
    half_power = jnp.where(upper == 1, power[looks:], power[:looks])
    out[...] = normalised(sums, half_power, (1 - 2 * upper).astype(F32))
    for part in range(2):
        spread(own, part, wide, mine)


def first_matching(own, other, take):
    parts, lines, width = own.shape
    looks, cells = lines // LOOK_A, width // LOOK_R
    blocks = width // LANES
    shape = jax.ShapeDtypeStruct((looks, cells), F32)
    return pl.pallas_call(
        first_kernel,
        out_shape=(shape, shape, jax.ShapeDtypeStruct((parts, blocks, LOOK_A, looks, LANES), F32)),
        in_specs=[VMEM] * 3,
        out_specs=(VMEM,) * 3,
        scratch_shapes=[pltpu.VMEM((parts, blocks, lines + LOOK_A, LANES), F32)],
        name="first_matching",
        compiler_params=pltpu.CompilerParams(vmem_limit_bytes=4 * 2**20),
        cost_estimate=pl.CostEstimate(flops=2 * 2**20, bytes_accessed=2**18, transcendentals=0),
    )(own, other, take)


def whole_kernel(mine, other, take, power, first, out, wide):
    upper = (lax.axis_index("acq") >> 2) & 1
    blocks, looks = mine.shape[1], mine.shape[3]
    columns = []
    for j in range(blocks):
        for part in range(2):
            wide[part, j, : other.shape[1]] = other[part, :, j * LANES : (j + 1) * LANES].astype(F32)
        total = 0.0
        for i in range(LOOK_A):
            their_re, their_im = (wide[part, j, pl.ds(i, looks, stride=LOOK_A), :] for part in range(2))
            terms = products(mine[0, j, i], mine[1, j, i], their_re, their_im)
            total = total + jnp.concatenate(terms, axis=0)
        columns.append(total)
    sums = dot_in_two(jnp.concatenate(columns, axis=1), take[...])
    whole = normalised(sums, power[...], (1 - 2 * upper).astype(F32))
    packed = jnp.concatenate([first[...], whole], axis=0)
    root = jnp.sqrt(jnp.abs(packed)) * UNIT
    out[...] = jnp.round(jnp.where(packed < 0, -root, root)).astype(jnp.int32).astype(jnp.int16)


def whole_pair(mine, other, take, power, first):
    rows, cells = first.shape
    parts, lines, width = other.shape
    return pl.pallas_call(
        whole_kernel,
        out_shape=jax.ShapeDtypeStruct((3 * rows, cells), jnp.int16),
        in_specs=[VMEM] * 5,
        out_specs=VMEM,
        scratch_shapes=[pltpu.VMEM((parts, width // LANES, lines + LOOK_A, LANES), F32)],
        name="whole_pair",
        compiler_params=pltpu.CompilerParams(vmem_limit_bytes=4 * 2**20),
        cost_estimate=pl.CostEstimate(flops=2 * 2**20, bytes_accessed=2**18, transcendentals=0),
    )(mine, other, take, power, first)


def take_kernel(take):
    sample = lax.broadcasted_iota(jnp.int32, take.shape, 0) // LOOK_R
    cell = lax.broadcasted_iota(jnp.int32, take.shape, 1)
    take[...] = (sample == cell).astype(F32).astype(BF16)


def taking(width):
    return pl.pallas_call(
        take_kernel,
        out_shape=jax.ShapeDtypeStruct((width, width // LOOK_R), BF16),
        out_specs=VMEM,
        name="taking",
        compiler_params=pltpu.CompilerParams(vmem_limit_bytes=2 * 2**20),
        cost_estimate=pl.CostEstimate(flops=2**17, bytes_accessed=2**18, transcendentals=0),
    )()


def select_kernel(blocks, own_cells, other_cells, band, onehot, masks, scale):
    lines, cols = own_cells.shape
    core = lax.axis_index("rng")
    first = (2 * lax.axis_index("acq") + core) * blocks
    own, other = own_cells[...], other_cells[...]
    left_core = core == 0
    halves = [jnp.where(left_core, own, other), jnp.where(left_core, other, own)]
    lane = lax.broadcasted_iota(jnp.int32, (cols, WIDE), 1).astype(F32)
    for side, cells in enumerate(halves):
        low = (cells & (WIDE - 1)).astype(F32)
        tall = jnp.concatenate([low] * (cols // lines), axis=0).T
        for line in range(lines):
            hit = tall[:, line : line + 1] == lane
            start = (line * 2 + side) * cols
            onehot[start : start + cols, :] = hit.astype(F32).astype(BF16)
    wide = jnp.concatenate(halves, axis=1) // WIDE
    mine = [(wide == first + block).astype(F32) for block in range(blocks)]
    for line in range(lines):
        for block in range(blocks):
            masks[line * blocks + block : line * blocks + block + 1, :] = mine[block][line : line + 1]
    count = jnp.zeros((blocks * lines, WIDE), F32)
    for line in range(lines):
        rows = masks[line * blocks : (line + 1) * blocks, :]
        rows = jnp.concatenate([rows] * lines, axis=0).astype(BF16)
        count = count + dot(rows, onehot[line * 2 * cols : (line + 1) * 2 * cols, :])
    scale[...] = 1.0 / jnp.maximum(count[:blocks], 1.0)
    shift = lax.broadcasted_iota(jnp.int32, (2 * cols, 2 * cols), 0)
    shift = jnp.abs(shift - lax.broadcasted_iota(jnp.int32, (2 * cols, 2 * cols), 1))
    band[...] = jnp.maximum(HALF_W + 1 - shift, 0).astype(F32).astype(BF16)


def select(blocks, own_cells, other_cells):
    lines, cols = own_cells.shape
    return pl.pallas_call(
        functools.partial(select_kernel, blocks),
        out_shape=(
            jax.ShapeDtypeStruct((2 * cols, 2 * cols), BF16),
            jax.ShapeDtypeStruct((lines * 2 * cols, WIDE), BF16),
            jax.ShapeDtypeStruct((lines * blocks, 2 * cols), F32),
            jax.ShapeDtypeStruct((blocks, WIDE), F32),
        ),
        in_specs=[VMEM, VMEM],
        out_specs=(VMEM,) * 4,
        name="select",
        compiler_params=pltpu.CompilerParams(vmem_limit_bytes=8 * 2**20),
        cost_estimate=pl.CostEstimate(flops=2 * 2**20, bytes_accessed=2**20, transcendentals=0),
    )(own_cells, other_cells)


def geocode_kernel(held, sent, band, onehot, masks, scale, out, by_acq, grid, filt):
    pairs = BLOCK // 2
    looks = held.shape[1] // 6
    lines, cols = 2 * looks, held.shape[2]
    planes = ROUNDS * pairs * 2
    blocks = scale.shape[0]
    rank, core = lax.axis_index("acq"), lax.axis_index("rng")
    origins = [(0, 0)]
    for step in STEPS:
        origins = origins + [(bits ^ mask, 1 - other) for mask in step for bits, other in origins]
    for slot, (bits, other) in enumerate(origins):
        acq, side = rank ^ bits, core ^ other
        by_acq[acq, side] = squared(held[slot].astype(jnp.int32))
        by_acq[acq, 1 - side] = squared(sent[slot].astype(jnp.int32))
    for side in range(2):
        columns = slice(side * cols, (side + 1) * cols)
        for acq in range(BLOCK):
            for part in range(2):
                row = (acq // 2 * 2 + part) * lines + (acq & 1) * looks
                grid[row : row + looks, columns] = by_acq[acq, side, part * looks : (part + 1) * looks, :]
            r, pair = WHOLE[acq >> 1]
            row = (r * pairs + pair + (acq & 1)) * 2 * lines
            grid[row : row + 2 * lines, columns] = by_acq[acq, side, lines:, :]
    smooth = dot_in_two(grid[...], band[...]) * (1.0 / (UNIT * (HALF_W + 1)) ** 2)
    smooth = smooth.reshape(planes // 2, 2, lines, 2 * cols)
    real, imag = smooth[:, 0], smooth[:, 1]
    gain = lax.rsqrt(jnp.sqrt(real * real + imag * imag + 0.01))
    filtered = (smooth * gain[:, None]).reshape(planes * lines, 2 * cols)
    for side in range(2):
        filt[side, : planes * lines] = filtered[:, side * cols : (side + 1) * cols]
    left = []
    for line in range(lines):
        value = [filt[side, pl.ds(line, planes, stride=lines), :] for side in range(2)]
        value = jnp.concatenate(value, axis=1)
        top = value.astype(BF16).astype(F32)
        both = jnp.concatenate([top, value - top], axis=0)
        rows = [both * masks[line * blocks + block : line * blocks + block + 1, :] for block in range(blocks)]
        left.append(jnp.concatenate(rows, axis=0).astype(BF16))
    sums = dot(jnp.concatenate(left, axis=1), onehot[...])
    for block in range(blocks):
        start = block * 2 * planes
        total = sums[start : start + planes] + sums[start + planes : start + 2 * planes]
        total = total * scale[block : block + 1, :]
        for plane in range(0, planes, 2):
            r, pair = plane // (2 * pairs), plane // 2 % pairs
            out[r, pair, :, block * WIDE : (block + 1) * WIDE] = total[plane : plane + 2]


def geocode(held, sent, band, onehot, masks, scale):
    pairs, blocks = BLOCK // 2, scale.shape[0]
    _, rows, cols = held.shape
    lines = rows // 3
    return pl.pallas_call(
        geocode_kernel,
        out_shape=jax.ShapeDtypeStruct((ROUNDS, pairs, 2, blocks * WIDE), F32),
        in_specs=[VMEM] * 6,
        out_specs=VMEM,
        scratch_shapes=[
            pltpu.VMEM((BLOCK, 2, rows, cols), F32),
            pltpu.VMEM((ROUNDS * pairs * 2 * lines, 2 * cols), F32),
            pltpu.VMEM((2, (ROUNDS * pairs * 2 + 1) * lines, cols), F32),
        ],
        name="geocode",
        compiler_params=pltpu.CompilerParams(vmem_limit_bytes=8 * 2**20),
        cost_estimate=pl.CostEstimate(flops=2**28, bytes_accessed=2**21, transcendentals=2**16),
    )(held, sent, band, onehot, masks, scale)


def across(value, mask):
    pairs = [(2 * a + c, 2 * (a ^ mask) + 1 - c) for a in range(BLOCK) for c in range(2)]
    return lax.ppermute(value, ("acq", "rng"), pairs)


def gather_small(packed, chosen):
    held = packed[None]
    for step in STEPS:
        held = jnp.concatenate([held] + [across(held, mask) for mask in step], axis=0)
    return geocode(held, lax.ppermute(held, "rng", [(0, 1), (1, 0)]), *chosen)


def gather_large(packed, map_cell):
    acq_count, rng_count = lax.axis_size("acq"), lax.axis_size("rng")
    pairs, piece = acq_count // 2, MAPC // (acq_count * rng_count)
    rows, cols = packed.shape
    lines, looks, width = rows // 3, rows // 6, rng_count * cols
    whole = lax.all_gather(packed, ("acq", "rng")).reshape(acq_count, rng_count, rows, cols)
    whole = whole.transpose(0, 2, 1, 3).reshape(acq_count, rows, width)
    whole = squared(whole) / UNIT**2
    halves = whole[:, :lines].reshape(pairs, 2, 2, looks, width)
    grids = [halves.transpose(0, 2, 1, 3, 4).reshape(pairs, 2, lines, width)]
    planes = whole[:, lines:].reshape(acq_count // BLOCK, 4, 2, 2, lines, width)
    for r in range(1, ROUNDS):
        quads = sorted((pair, quad) for quad, (found, pair) in enumerate(WHOLE) if found == r)
        grid = jnp.stack([planes[:, quad] for _, quad in quads], axis=1)
        grids.append(grid.reshape(pairs, 2, lines, width))
    gamma = jnp.stack(grids)
    padded = jnp.pad(gamma, [(0, 0)] * 4 + [(HALF_W, HALF_W)])
    smooth = jnp.zeros_like(gamma)
    for offset in range(-HALF_W, HALF_W + 1):
        weight = (HALF_W + 1 - abs(offset)) / float((HALF_W + 1) ** 2)
        smooth = smooth + weight * padded[..., HALF_W + offset : HALF_W + offset + width]
    power = smooth[:, :, 0] ** 2 + smooth[:, :, 1] ** 2 + 0.01
    filtered = smooth * (power ** (-0.25))[:, :, None]
    cells = lax.all_gather(map_cell, "rng", axis=1, tiled=True).reshape(-1, 1)
    first = (lax.axis_index("acq") * rng_count + lax.axis_index("rng")) * piece
    onehot = (cells == first + jnp.arange(piece, dtype=jnp.int32)).astype(F32)
    count = onehot.sum(axis=0)
    sums = jnp.dot(
        filtered.reshape(-1, cells.shape[0]), onehot, precision=lax.Precision.HIGHEST
    ).reshape(ROUNDS, pairs, 2, piece)
    return sums / jnp.maximum(count, 1.0)


def per_device(slc, map_cell):
    acq_count = lax.axis_size("acq")
    own = slc[:, 0]
    quarter = [(a & -BLOCK) + 2 * SEND[a % BLOCK // 2] + a % 2 for a in range(acq_count)]
    whole = lax.ppermute(own, "acq", list(enumerate(quarter)))
    half = lax.ppermute(pick(own), "acq", [(a, a ^ 1) for a in range(acq_count)])
    small = acq_count == BLOCK
    take = taking(own.shape[2])
    if small:
        blocks = MAPC // (acq_count * lax.axis_size("rng")) // WIDE
        chosen = select(blocks, map_cell, lax.ppermute(map_cell, "rng", [(0, 1), (1, 0)]))
        take, chosen = lax.optimization_barrier((take, chosen))
    first, power, mine = first_matching(own, half, take)
    packed = whole_pair(mine, whole, take, power, first)
    return gather_small(packed, chosen) if small else gather_large(packed, map_cell)


def solution(mesh):
    in_specs = (P(None, ("groups", "acq"), None, "rng"), P("groups", "rng"))
    out_specs = P(None, "groups", None, ("acq", "rng"))
    return jax.shard_map(
        per_device, mesh=mesh, in_specs=in_specs, out_specs=out_specs, check_vma=False
    )
```

```python
import functools

import jax
import jax.numpy as jnp
from jax import lax
from jax.experimental import pallas as pl
from jax.experimental.pallas import tpu as pltpu
from jax.sharding import PartitionSpec as P

LOOK_A = 8
LOOK_R = 8
HALF_W = 4
ROUNDS = 3
BLOCK = 2**ROUNDS
STEPS = ((1,), (6, 4, 2))
SEND = (2, 0, 3, 1)
WHOLE = ((1, 0), (2, 2), (2, 0), (1, 2))
MAPC = 16384
LANES = 128
WIDE = 256
UNIT = 32760.0
F32 = jnp.float32
BF16 = jnp.bfloat16

VMEM = pl.BlockSpec(memory_space=pltpu.VMEM)


def dot(left, right):
    return jnp.dot(left, right, preferred_element_type=F32)


def dot_in_two(left, right):
    rows = left.shape[0]
    high = left.astype(BF16).astype(F32)
    both = dot(jnp.concatenate([high, left - high], axis=0).astype(BF16), right)
    return both[:rows] + both[rows:]


def squared(root):
    root = root.astype(F32)
    return root * jnp.abs(root)


def pick_kernel(own, out):
    half = out.shape[1]
    upper = lax.axis_index("acq") & 1
    out[...] = own[:, pl.ds(pl.multiple_of((1 - upper) * half, half), half), :]


def pick(own):
    parts, lines, width = own.shape
    return pl.pallas_call(
        pick_kernel,
        out_shape=jax.ShapeDtypeStruct((parts, lines // 2, width), own.dtype),
        in_specs=[VMEM],
        out_specs=VMEM,
        name="pick",
        compiler_params=pltpu.CompilerParams(vmem_limit_bytes=2 * 2**20),
        cost_estimate=pl.CostEstimate(flops=2**10, bytes_accessed=2**18, transcendentals=0),
    )(own)


def look_sums(terms, take):
    sums = dot_in_two(terms, take)
    return sums.reshape(terms.shape[0] // LOOK_A, LOOK_A, take.shape[1]).sum(axis=1)


def products(mine_re, mine_im, their_re, their_im):
    return [
        mine_re * their_re + mine_im * their_im,
        mine_im * their_re - mine_re * their_im,
        their_re * their_re + their_im * their_im,
    ]


def normalised(sums, power, sign):
    looks = power.shape[0]
    inverse = lax.rsqrt(power * sums[2 * looks :] + 1e-06)
    return sums[: 2 * looks] * jnp.concatenate([inverse, inverse * sign], axis=0)


def spread(samples, part, wide, out):
    blocks, looks = wide.shape[1], out.shape[3]
    for j in range(blocks):
        wide[part, j, : samples.shape[1]] = samples[part, :, j * LANES : (j + 1) * LANES].astype(F32)
        for i in range(LOOK_A):
            out[part, j, i] = wide[part, j, pl.ds(i, looks, stride=LOOK_A), :]


def first_kernel(own, other, take, out, power, mine, wide):
    half = other.shape[1]
    looks = half // LOOK_A
    own_re, own_im = own[0].astype(F32), own[1].astype(F32)
    power[...] = look_sums(own_re * own_re + own_im * own_im, take[...])
    upper = lax.axis_index("acq") & 1
    rows = pl.ds(pl.multiple_of(upper * half, half), half)
    terms = products(own[0, rows, :].astype(F32), own[1, rows, :].astype(F32), other[0].astype(F32), other[1].astype(F32))
    sums = look_sums(jnp.concatenate(terms, axis=0), take[...])
    half_power = jnp.where(upper == 1, power[looks:], power[:looks])
    out[...] = normalised(sums, half_power, (1 - 2 * upper).astype(F32))
    for part in range(2):
        spread(own, part, wide, mine)


def first_matching(own, other, take):
    parts, lines, width = own.shape
    looks, cells = lines // LOOK_A, width // LOOK_R
    blocks = width // LANES
    shape = jax.ShapeDtypeStruct((looks, cells), F32)
    return pl.pallas_call(
        first_kernel,
        out_shape=(shape, shape, jax.ShapeDtypeStruct((parts, blocks, LOOK_A, looks, LANES), F32)),
        in_specs=[VMEM] * 3,
        out_specs=(VMEM,) * 3,
        scratch_shapes=[pltpu.VMEM((parts, blocks, lines + LOOK_A, LANES), F32)],
        name="first_matching",
        compiler_params=pltpu.CompilerParams(vmem_limit_bytes=4 * 2**20),
        cost_estimate=pl.CostEstimate(flops=2 * 2**20, bytes_accessed=2**18, transcendentals=0),
    )(own, other, take)


def whole_kernel(mine, other, take, power, first, out, wide):
    upper = (lax.axis_index("acq") >> 2) & 1
    blocks, looks = mine.shape[1], mine.shape[3]
    columns = []
    for j in range(blocks):
        for part in range(2):
            wide[part, j, : other.shape[1]] = other[part, :, j * LANES : (j + 1) * LANES].astype(F32)
        total = 0.0
        for i in range(LOOK_A):
            their_re, their_im = (wide[part, j, pl.ds(i, looks, stride=LOOK_A), :] for part in range(2))
            terms = products(mine[0, j, i], mine[1, j, i], their_re, their_im)
            total = total + jnp.concatenate(terms, axis=0)
        columns.append(total)
    sums = dot_in_two(jnp.concatenate(columns, axis=1), take[...])
    whole = normalised(sums, power[...], (1 - 2 * upper).astype(F32))
    packed = jnp.concatenate([first[...], whole], axis=0)
    root = jnp.sqrt(jnp.abs(packed)) * UNIT
    out[...] = jnp.round(jnp.where(packed < 0, -root, root)).astype(jnp.int32).astype(jnp.int16)


def whole_pair(mine, other, take, power, first):
    rows, cells = first.shape
    parts, lines, width = other.shape
    return pl.pallas_call(
        whole_kernel,
        out_shape=jax.ShapeDtypeStruct((3 * rows, cells), jnp.int16),
        in_specs=[VMEM] * 5,
        out_specs=VMEM,
        scratch_shapes=[pltpu.VMEM((parts, width // LANES, lines + LOOK_A, LANES), F32)],
        name="whole_pair",
        compiler_params=pltpu.CompilerParams(vmem_limit_bytes=4 * 2**20),
        cost_estimate=pl.CostEstimate(flops=2 * 2**20, bytes_accessed=2**18, transcendentals=0),
    )(mine, other, take, power, first)


def take_kernel(take):
    sample = lax.broadcasted_iota(jnp.int32, take.shape, 0) // LOOK_R
    cell = lax.broadcasted_iota(jnp.int32, take.shape, 1)
    take[...] = (sample == cell).astype(F32).astype(BF16)


def taking(width):
    return pl.pallas_call(
        take_kernel,
        out_shape=jax.ShapeDtypeStruct((width, width // LOOK_R), BF16),
        out_specs=VMEM,
        name="taking",
        compiler_params=pltpu.CompilerParams(vmem_limit_bytes=2 * 2**20),
        cost_estimate=pl.CostEstimate(flops=2**17, bytes_accessed=2**18, transcendentals=0),
    )()


def select_kernel(blocks, own_cells, other_cells, band, onehot, masks, scale):
    lines, cols = own_cells.shape
    core = lax.axis_index("rng")
    first = (2 * lax.axis_index("acq") + core) * blocks
    own, other = own_cells[...], other_cells[...]
    left_core = core == 0
    halves = [jnp.where(left_core, own, other), jnp.where(left_core, other, own)]
    lane = lax.broadcasted_iota(jnp.int32, (cols, WIDE), 1).astype(F32)
    for side, cells in enumerate(halves):
        low = (cells & (WIDE - 1)).astype(F32)
        tall = jnp.concatenate([low] * (cols // lines), axis=0).T
        for line in range(lines):
            hit = tall[:, line : line + 1] == lane
            start = (line * 2 + side) * cols
            onehot[start : start + cols, :] = hit.astype(F32).astype(BF16)
    wide = jnp.concatenate(halves, axis=1) // WIDE
    mine = [(wide == first + block).astype(F32) for block in range(blocks)]
    for line in range(lines):
        for block in range(blocks):
            masks[line * blocks + block : line * blocks + block + 1, :] = mine[block][line : line + 1]
    count = jnp.zeros((blocks * lines, WIDE), F32)
    for line in range(lines):
        rows = masks[line * blocks : (line + 1) * blocks, :]
        rows = jnp.concatenate([rows] * lines, axis=0).astype(BF16)
        count = count + dot(rows, onehot[line * 2 * cols : (line + 1) * 2 * cols, :])
    scale[...] = 1.0 / jnp.maximum(count[:blocks], 1.0)
    shift = lax.broadcasted_iota(jnp.int32, (2 * cols, 2 * cols), 0)
    shift = jnp.abs(shift - lax.broadcasted_iota(jnp.int32, (2 * cols, 2 * cols), 1))
    band[...] = jnp.maximum(HALF_W + 1 - shift, 0).astype(F32).astype(BF16)


def select(blocks, own_cells, other_cells):
    lines, cols = own_cells.shape
    return pl.pallas_call(
        functools.partial(select_kernel, blocks),
        out_shape=(
            jax.ShapeDtypeStruct((2 * cols, 2 * cols), BF16),
            jax.ShapeDtypeStruct((lines * 2 * cols, WIDE), BF16),
            jax.ShapeDtypeStruct((lines * blocks, 2 * cols), F32),
            jax.ShapeDtypeStruct((blocks, WIDE), F32),
        ),
        in_specs=[VMEM, VMEM],
        out_specs=(VMEM,) * 4,
        name="select",
        compiler_params=pltpu.CompilerParams(vmem_limit_bytes=8 * 2**20),
        cost_estimate=pl.CostEstimate(flops=2 * 2**20, bytes_accessed=2**20, transcendentals=0),
    )(own_cells, other_cells)


def geocode_kernel(held, sent, band, onehot, masks, scale, out, by_acq, grid, filt):
    pairs = BLOCK // 2
    looks = held.shape[1] // 6
    lines, cols = 2 * looks, held.shape[2]
    planes = ROUNDS * pairs * 2
    blocks = scale.shape[0]
    rank, core = lax.axis_index("acq"), lax.axis_index("rng")
    origins = [(0, 0)]
    for step in STEPS:
        origins = origins + [(bits ^ mask, 1 - other) for mask in step for bits, other in origins]
    for slot, (bits, other) in enumerate(origins):
        acq, side = rank ^ bits, core ^ other
        by_acq[acq, side] = squared(held[slot].astype(jnp.int32))
        by_acq[acq, 1 - side] = squared(sent[slot].astype(jnp.int32))
    for side in range(2):
        columns = slice(side * cols, (side + 1) * cols)
        for acq in range(BLOCK):
            for part in range(2):
                row = (acq // 2 * 2 + part) * lines + (acq & 1) * looks
                grid[row : row + looks, columns] = by_acq[acq, side, part * looks : (part + 1) * looks, :]
            r, pair = WHOLE[acq >> 1]
            row = (r * pairs + pair + (acq & 1)) * 2 * lines
            grid[row : row + 2 * lines, columns] = by_acq[acq, side, lines:, :]
    smooth = dot_in_two(grid[...], band[...]) * (1.0 / (UNIT * (HALF_W + 1)) ** 2)
    smooth = smooth.reshape(planes // 2, 2, lines, 2 * cols)
    real, imag = smooth[:, 0], smooth[:, 1]
    gain = lax.rsqrt(jnp.sqrt(real * real + imag * imag + 0.01))
    filtered = (smooth * gain[:, None]).reshape(planes * lines, 2 * cols)
    for side in range(2):
        filt[side, : planes * lines] = filtered[:, side * cols : (side + 1) * cols]
    left = []
    for line in range(lines):
        value = [filt[side, pl.ds(line, planes, stride=lines), :] for side in range(2)]
        value = jnp.concatenate(value, axis=1)
        top = value.astype(BF16).astype(F32)
        both = jnp.concatenate([top, value - top], axis=0)
        rows = [both * masks[line * blocks + block : line * blocks + block + 1, :] for block in range(blocks)]
        left.append(jnp.concatenate(rows, axis=0).astype(BF16))
    sums = dot(jnp.concatenate(left, axis=1), onehot[...])
    for block in range(blocks):
        start = block * 2 * planes
        total = sums[start : start + planes] + sums[start + planes : start + 2 * planes]
        total = total * scale[block : block + 1, :]
        for plane in range(0, planes, 2):
            r, pair = plane // (2 * pairs), plane // 2 % pairs
            out[r, pair, :, block * WIDE : (block + 1) * WIDE] = total[plane : plane + 2]


def geocode(held, sent, band, onehot, masks, scale):
    pairs, blocks = BLOCK // 2, scale.shape[0]
    _, rows, cols = held.shape
    lines = rows // 3
    return pl.pallas_call(
        geocode_kernel,
        out_shape=jax.ShapeDtypeStruct((ROUNDS, pairs, 2, blocks * WIDE), F32),
        in_specs=[VMEM] * 6,
        out_specs=VMEM,
        scratch_shapes=[
            pltpu.VMEM((BLOCK, 2, rows, cols), F32),
            pltpu.VMEM((ROUNDS * pairs * 2 * lines, 2 * cols), F32),
            pltpu.VMEM((2, (ROUNDS * pairs * 2 + 1) * lines, cols), F32),
        ],
        name="geocode",
        compiler_params=pltpu.CompilerParams(vmem_limit_bytes=8 * 2**20),
        cost_estimate=pl.CostEstimate(flops=2**28, bytes_accessed=2**21, transcendentals=2**16),
    )(held, sent, band, onehot, masks, scale)


def across(value, mask):
    pairs = [(2 * a + c, 2 * (a ^ mask) + 1 - c) for a in range(BLOCK) for c in range(2)]
    return lax.ppermute(value, ("acq", "rng"), pairs)


def swap(value):
    return lax.ppermute(value, "rng", [(0, 1), (1, 0)])


def gather_small(packed, chosen):
    held = packed[None]
    for step in STEPS[:-1]:
        held = jnp.concatenate([held] + [across(held, mask) for mask in step], axis=0)
    last = [across(held, mask) for mask in STEPS[-1]]
    early = swap(jnp.concatenate([held] + last[:1], axis=0))
    late = swap(jnp.concatenate(last[1:], axis=0))
    return geocode(jnp.concatenate([held] + last, axis=0), jnp.concatenate([early, late], axis=0), *chosen)


def gather_large(packed, map_cell):
    acq_count, rng_count = lax.axis_size("acq"), lax.axis_size("rng")
    pairs, piece = acq_count // 2, MAPC // (acq_count * rng_count)
    rows, cols = packed.shape
    lines, looks, width = rows // 3, rows // 6, rng_count * cols
    whole = lax.all_gather(packed, ("acq", "rng")).reshape(acq_count, rng_count, rows, cols)
    whole = whole.transpose(0, 2, 1, 3).reshape(acq_count, rows, width)
    whole = squared(whole) / UNIT**2
    halves = whole[:, :lines].reshape(pairs, 2, 2, looks, width)
    grids = [halves.transpose(0, 2, 1, 3, 4).reshape(pairs, 2, lines, width)]
    planes = whole[:, lines:].reshape(acq_count // BLOCK, 4, 2, 2, lines, width)
    for r in range(1, ROUNDS):
        quads = sorted((pair, quad) for quad, (found, pair) in enumerate(WHOLE) if found == r)
        grid = jnp.stack([planes[:, quad] for _, quad in quads], axis=1)
        grids.append(grid.reshape(pairs, 2, lines, width))
    gamma = jnp.stack(grids)
    padded = jnp.pad(gamma, [(0, 0)] * 4 + [(HALF_W, HALF_W)])
    smooth = jnp.zeros_like(gamma)
    for offset in range(-HALF_W, HALF_W + 1):
        weight = (HALF_W + 1 - abs(offset)) / float((HALF_W + 1) ** 2)
        smooth = smooth + weight * padded[..., HALF_W + offset : HALF_W + offset + width]
    power = smooth[:, :, 0] ** 2 + smooth[:, :, 1] ** 2 + 0.01
    filtered = smooth * (power ** (-0.25))[:, :, None]
    cells = lax.all_gather(map_cell, "rng", axis=1, tiled=True).reshape(-1, 1)
    first = (lax.axis_index("acq") * rng_count + lax.axis_index("rng")) * piece
    onehot = (cells == first + jnp.arange(piece, dtype=jnp.int32)).astype(F32)
    count = onehot.sum(axis=0)
    sums = jnp.dot(
        filtered.reshape(-1, cells.shape[0]), onehot, precision=lax.Precision.HIGHEST
    ).reshape(ROUNDS, pairs, 2, piece)
    return sums / jnp.maximum(count, 1.0)


def per_device(slc, map_cell):
    acq_count = lax.axis_size("acq")
    own = slc[:, 0]
    quarter = [(a & -BLOCK) + 2 * SEND[a % BLOCK // 2] + a % 2 for a in range(acq_count)]
    whole = lax.ppermute(own, "acq", list(enumerate(quarter)))
    half = lax.ppermute(pick(own), "acq", [(a, a ^ 1) for a in range(acq_count)])
    small = acq_count == BLOCK
    take = taking(own.shape[2])
    if small:
        blocks = MAPC // (acq_count * lax.axis_size("rng")) // WIDE
        chosen = select(blocks, map_cell, swap(map_cell))
        take, chosen = lax.optimization_barrier((take, chosen))
    first, power, mine = first_matching(own, half, take)
    packed = whole_pair(mine, whole, take, power, first)
    return gather_small(packed, chosen) if small else gather_large(packed, map_cell)


def solution(mesh):
    in_specs = (P(None, ("groups", "acq"), None, "rng"), P("groups", "rng"))
    out_specs = P(None, "groups", None, ("acq", "rng"))
    return jax.shard_map(
        per_device, mesh=mesh, in_specs=in_specs, out_specs=out_specs, check_vma=False
    )
```

```python
import functools

import jax
import jax.numpy as jnp
from jax import lax
from jax.experimental import pallas as pl
from jax.experimental.pallas import tpu as pltpu
from jax.sharding import PartitionSpec as P

LOOK_A = 8
LOOK_R = 8
HALF_W = 4
ROUNDS = 3
BLOCK = 2**ROUNDS
STEPS = ((6, 4, 2), (1,))
SEND = (2, 0, 3, 1)
WHOLE = ((1, 0), (2, 2), (2, 0), (1, 2))
MAPC = 16384
LANES = 128
WIDE = 256
UNIT = 32760.0
F32 = jnp.float32
BF16 = jnp.bfloat16

VMEM = pl.BlockSpec(memory_space=pltpu.VMEM)


def dot(left, right):
    return jnp.dot(left, right, preferred_element_type=F32)


def dot_in_two(left, right):
    rows = left.shape[0]
    high = left.astype(BF16).astype(F32)
    both = dot(jnp.concatenate([high, left - high], axis=0).astype(BF16), right)
    return both[:rows] + both[rows:]


def squared(root):
    root = root.astype(F32)
    return root * jnp.abs(root)


def pick_kernel(own, out):
    half = out.shape[1]
    upper = lax.axis_index("acq") & 1
    out[...] = own[:, pl.ds(pl.multiple_of((1 - upper) * half, half), half), :]


def pick(own):
    parts, lines, width = own.shape
    return pl.pallas_call(
        pick_kernel,
        out_shape=jax.ShapeDtypeStruct((parts, lines // 2, width), own.dtype),
        in_specs=[VMEM],
        out_specs=VMEM,
        name="pick",
        compiler_params=pltpu.CompilerParams(vmem_limit_bytes=2 * 2**20),
        cost_estimate=pl.CostEstimate(flops=2**10, bytes_accessed=2**18, transcendentals=0),
    )(own)


def look_sums(terms, take):
    sums = dot_in_two(terms, take)
    return sums.reshape(terms.shape[0] // LOOK_A, LOOK_A, take.shape[1]).sum(axis=1)


def products(mine_re, mine_im, their_re, their_im):
    return [
        mine_re * their_re + mine_im * their_im,
        mine_im * their_re - mine_re * their_im,
        their_re * their_re + their_im * their_im,
    ]


def normalised(sums, power, sign):
    looks = power.shape[0]
    inverse = lax.rsqrt(power * sums[2 * looks :] + 1e-06)
    return sums[: 2 * looks] * jnp.concatenate([inverse, inverse * sign], axis=0)


def spread(samples, part, wide, out):
    blocks, looks = wide.shape[1], out.shape[3]
    for j in range(blocks):
        wide[part, j, : samples.shape[1]] = samples[part, :, j * LANES : (j + 1) * LANES].astype(F32)
        for i in range(LOOK_A):
            out[part, j, i] = wide[part, j, pl.ds(i, looks, stride=LOOK_A), :]


def first_kernel(own, other, take, out, power, mine, wide):
    half = other.shape[1]
    looks = half // LOOK_A
    own_re, own_im = own[0].astype(F32), own[1].astype(F32)
    power[...] = look_sums(own_re * own_re + own_im * own_im, take[...])
    upper = lax.axis_index("acq") & 1
    rows = pl.ds(pl.multiple_of(upper * half, half), half)
    terms = products(own[0, rows, :].astype(F32), own[1, rows, :].astype(F32), other[0].astype(F32), other[1].astype(F32))
    sums = look_sums(jnp.concatenate(terms, axis=0), take[...])
    half_power = jnp.where(upper == 1, power[looks:], power[:looks])
    out[...] = normalised(sums, half_power, (1 - 2 * upper).astype(F32))
    for part in range(2):
        spread(own, part, wide, mine)


def first_matching(own, other, take):
    parts, lines, width = own.shape
    looks, cells = lines // LOOK_A, width // LOOK_R
    blocks = width // LANES
    shape = jax.ShapeDtypeStruct((looks, cells), F32)
    return pl.pallas_call(
        first_kernel,
        out_shape=(shape, shape, jax.ShapeDtypeStruct((parts, blocks, LOOK_A, looks, LANES), F32)),
        in_specs=[VMEM] * 3,
        out_specs=(VMEM,) * 3,
        scratch_shapes=[pltpu.VMEM((parts, blocks, lines + LOOK_A, LANES), F32)],
        name="first_matching",
        compiler_params=pltpu.CompilerParams(vmem_limit_bytes=4 * 2**20),
        cost_estimate=pl.CostEstimate(flops=2 * 2**20, bytes_accessed=2**18, transcendentals=0),
    )(own, other, take)


def whole_kernel(mine, other, take, power, first, out, wide):
    upper = (lax.axis_index("acq") >> 2) & 1
    blocks, looks = mine.shape[1], mine.shape[3]
    columns = []
    for j in range(blocks):
        for part in range(2):
            wide[part, j, : other.shape[1]] = other[part, :, j * LANES : (j + 1) * LANES].astype(F32)
        total = 0.0
        for i in range(LOOK_A):
            their_re, their_im = (wide[part, j, pl.ds(i, looks, stride=LOOK_A), :] for part in range(2))
            terms = products(mine[0, j, i], mine[1, j, i], their_re, their_im)
            total = total + jnp.concatenate(terms, axis=0)
        columns.append(total)
    sums = dot_in_two(jnp.concatenate(columns, axis=1), take[...])
    whole = normalised(sums, power[...], (1 - 2 * upper).astype(F32))
    packed = jnp.concatenate([first[...], whole], axis=0)
    root = jnp.sqrt(jnp.abs(packed)) * UNIT
    out[...] = jnp.round(jnp.where(packed < 0, -root, root)).astype(jnp.int32).astype(jnp.int16)


def whole_pair(mine, other, take, power, first):
    rows, cells = first.shape
    parts, lines, width = other.shape
    return pl.pallas_call(
        whole_kernel,
        out_shape=jax.ShapeDtypeStruct((3 * rows, cells), jnp.int16),
        in_specs=[VMEM] * 5,
        out_specs=VMEM,
        scratch_shapes=[pltpu.VMEM((parts, width // LANES, lines + LOOK_A, LANES), F32)],
        name="whole_pair",
        compiler_params=pltpu.CompilerParams(vmem_limit_bytes=4 * 2**20),
        cost_estimate=pl.CostEstimate(flops=2 * 2**20, bytes_accessed=2**18, transcendentals=0),
    )(mine, other, take, power, first)


def take_kernel(take):
    sample = lax.broadcasted_iota(jnp.int32, take.shape, 0) // LOOK_R
    cell = lax.broadcasted_iota(jnp.int32, take.shape, 1)
    take[...] = (sample == cell).astype(F32).astype(BF16)


def taking(width):
    return pl.pallas_call(
        take_kernel,
        out_shape=jax.ShapeDtypeStruct((width, width // LOOK_R), BF16),
        out_specs=VMEM,
        name="taking",
        compiler_params=pltpu.CompilerParams(vmem_limit_bytes=2 * 2**20),
        cost_estimate=pl.CostEstimate(flops=2**17, bytes_accessed=2**18, transcendentals=0),
    )()


def select_kernel(blocks, own_cells, other_cells, band, onehot, masks, scale):
    lines, cols = own_cells.shape
    core = lax.axis_index("rng")
    first = (2 * lax.axis_index("acq") + core) * blocks
    own, other = own_cells[...], other_cells[...]
    left_core = core == 0
    halves = [jnp.where(left_core, own, other), jnp.where(left_core, other, own)]
    lane = lax.broadcasted_iota(jnp.int32, (cols, WIDE), 1).astype(F32)
    for side, cells in enumerate(halves):
        low = (cells & (WIDE - 1)).astype(F32)
        tall = jnp.concatenate([low] * (cols // lines), axis=0).T
        for line in range(lines):
            hit = tall[:, line : line + 1] == lane
            start = (line * 2 + side) * cols
            onehot[start : start + cols, :] = hit.astype(F32).astype(BF16)
    wide = jnp.concatenate(halves, axis=1) // WIDE
    mine = [(wide == first + block).astype(F32) for block in range(blocks)]
    for line in range(lines):
        for block in range(blocks):
            masks[line * blocks + block : line * blocks + block + 1, :] = mine[block][line : line + 1]
    count = jnp.zeros((blocks * lines, WIDE), F32)
    for line in range(lines):
        rows = masks[line * blocks : (line + 1) * blocks, :]
        rows = jnp.concatenate([rows] * lines, axis=0).astype(BF16)
        count = count + dot(rows, onehot[line * 2 * cols : (line + 1) * 2 * cols, :])
    scale[...] = 1.0 / jnp.maximum(count[:blocks], 1.0)
    shift = lax.broadcasted_iota(jnp.int32, (2 * cols, 2 * cols), 0)
    shift = jnp.abs(shift - lax.broadcasted_iota(jnp.int32, (2 * cols, 2 * cols), 1))
    band[...] = jnp.maximum(HALF_W + 1 - shift, 0).astype(F32).astype(BF16)


def select(blocks, own_cells, other_cells):
    lines, cols = own_cells.shape
    return pl.pallas_call(
        functools.partial(select_kernel, blocks),
        out_shape=(
            jax.ShapeDtypeStruct((2 * cols, 2 * cols), BF16),
            jax.ShapeDtypeStruct((lines * 2 * cols, WIDE), BF16),
            jax.ShapeDtypeStruct((lines * blocks, 2 * cols), F32),
            jax.ShapeDtypeStruct((blocks, WIDE), F32),
        ),
        in_specs=[VMEM, VMEM],
        out_specs=(VMEM,) * 4,
        name="select",
        compiler_params=pltpu.CompilerParams(vmem_limit_bytes=8 * 2**20),
        cost_estimate=pl.CostEstimate(flops=2 * 2**20, bytes_accessed=2**20, transcendentals=0),
    )(own_cells, other_cells)


def half_sums(held, sent, other_line, band, onehot, masks, by_quarter, grid, filt):
    looks = held.shape[1] // 6
    lines, cols = 2 * looks, held.shape[2]
    quarters = BLOCK // 2
    planes = 4 * quarters
    blocks = masks.shape[0] // lines
    rank, core = lax.axis_index("acq"), lax.axis_index("rng")
    for slot, bits in enumerate((0,) + STEPS[0]):
        quarter, side = (rank ^ bits) >> 1, core ^ (bits != 0) ^ other_line
        by_quarter[quarter, side] = squared(held[slot].astype(jnp.int32))
        by_quarter[quarter, 1 - side] = squared(sent[slot].astype(jnp.int32))
    upper = (rank & 1) ^ other_line
    none = jnp.zeros((looks, cols), F32)
    for side in range(2):
        columns = slice(side * cols, (side + 1) * cols)
        for quarter in range(quarters):
            for part in range(2):
                value = by_quarter[quarter, side, part * looks : (part + 1) * looks, :]
                row = (quarter * 2 + part) * lines
                grid[row : row + looks, columns] = jnp.where(upper == 0, value, none)
                grid[row + looks : row + lines, columns] = jnp.where(upper == 0, none, value)
            row = (planes // 2 + quarter * 2) * lines
            grid[row : row + 2 * lines, columns] = by_quarter[quarter, side, lines:, :]
    smooth = dot_in_two(grid[...], band[...]) * (1.0 / (UNIT * (HALF_W + 1)) ** 2)
    smooth = smooth.reshape(planes // 2, 2, lines, 2 * cols)
    real, imag = smooth[:, 0], smooth[:, 1]
    gain = lax.rsqrt(jnp.sqrt(real * real + imag * imag + 0.01))
    filtered = (smooth * gain[:, None]).reshape(planes * lines, 2 * cols)
    for side in range(2):
        filt[side, : planes * lines] = filtered[:, side * cols : (side + 1) * cols]
    left = []
    for line in range(lines):
        value = [filt[side, pl.ds(line, planes, stride=lines), :] for side in range(2)]
        value = jnp.concatenate(value, axis=1)
        top = value.astype(BF16).astype(F32)
        both = jnp.concatenate([top, value - top], axis=0)
        rows = [both * masks[line * blocks + block : line * blocks + block + 1, :] for block in range(blocks)]
        left.append(jnp.concatenate(rows, axis=0).astype(BF16))
    sums = dot(jnp.concatenate(left, axis=1), onehot[...])
    starts = [block * 2 * planes for block in range(blocks)]
    return [sums[start : start + planes] + sums[start + planes : start + 2 * planes] for start in starts]


def near_kernel(held, sent, band, onehot, masks, scale, out, by_quarter, grid, filt):
    for block, total in enumerate(half_sums(held, sent, 0, band, onehot, masks, by_quarter, grid, filt)):
        out[block] = total * scale[block : block + 1, :]


def far_kernel(held, sent, band, onehot, masks, scale, near, out, by_quarter, grid, filt):
    line = lax.axis_index("acq") & 1
    half = near.shape[1] // 2
    for block, total in enumerate(half_sums(held, sent, 1, band, onehot, masks, by_quarter, grid, filt)):
        total = total * scale[block : block + 1, :]
        ours = near[block]
        columns = slice(block * WIDE, (block + 1) * WIDE)
        for quarter in range(BLOCK // 2):
            rows = slice(2 * quarter, 2 * quarter + 2)
            out[0, quarter, :, columns] = ours[rows] + total[rows]
            r, pair = WHOLE[quarter]
            rows = slice(half + 2 * quarter, half + 2 * quarter + 2)
            out[r, pair + line, :, columns] = ours[rows]
            out[r, pair + 1 - line, :, columns] = total[rows]


def geocode_half(kernel, name, shape, held, sent, *rest):
    slots, rows, cols = held.shape
    lines = rows // 3
    planes = 4 * slots
    return pl.pallas_call(
        kernel,
        out_shape=jax.ShapeDtypeStruct(shape, F32),
        in_specs=[VMEM] * (2 + len(rest)),
        out_specs=VMEM,
        scratch_shapes=[
            pltpu.VMEM((slots, 2, rows, cols), F32),
            pltpu.VMEM((planes * lines, 2 * cols), F32),
            pltpu.VMEM((2, (planes + 1) * lines, cols), F32),
        ],
        name=name,
        compiler_params=pltpu.CompilerParams(vmem_limit_bytes=8 * 2**20),
        cost_estimate=pl.CostEstimate(flops=2**21, bytes_accessed=2**20, transcendentals=2**15),
    )(held, sent, *rest)


def across(value, mask):
    pairs = [(2 * a + c, 2 * (a ^ mask) + 1 - c) for a in range(BLOCK) for c in range(2)]
    return lax.ppermute(value, ("acq", "rng"), pairs)


def swap(value):
    return lax.ppermute(value, "rng", [(0, 1), (1, 0)])


def gather_small(packed, chosen):
    held = packed[None]
    held = jnp.concatenate([held] + [across(held, mask) for mask in STEPS[0]], axis=0)
    far = across(held, STEPS[1][0])
    band, onehot, masks, scale = chosen
    blocks = scale.shape[0]
    near = geocode_half(
        near_kernel, "near_line", (blocks, 2 * BLOCK, WIDE), held, swap(held), band, onehot, masks, scale
    )
    shape = (ROUNDS, BLOCK // 2, 2, blocks * WIDE)
    return geocode_half(far_kernel, "far_line", shape, far, swap(far), band, onehot, masks, scale, near)


def gather_large(packed, map_cell):
    acq_count, rng_count = lax.axis_size("acq"), lax.axis_size("rng")
    pairs, piece = acq_count // 2, MAPC // (acq_count * rng_count)
    rows, cols = packed.shape
    lines, looks, width = rows // 3, rows // 6, rng_count * cols
    whole = lax.all_gather(packed, ("acq", "rng")).reshape(acq_count, rng_count, rows, cols)
    whole = whole.transpose(0, 2, 1, 3).reshape(acq_count, rows, width)
    whole = squared(whole) / UNIT**2
    halves = whole[:, :lines].reshape(pairs, 2, 2, looks, width)
    grids = [halves.transpose(0, 2, 1, 3, 4).reshape(pairs, 2, lines, width)]
    planes = whole[:, lines:].reshape(acq_count // BLOCK, 4, 2, 2, lines, width)
    for r in range(1, ROUNDS):
        quads = sorted((pair, quad) for quad, (found, pair) in enumerate(WHOLE) if found == r)
        grid = jnp.stack([planes[:, quad] for _, quad in quads], axis=1)
        grids.append(grid.reshape(pairs, 2, lines, width))
    gamma = jnp.stack(grids)
    padded = jnp.pad(gamma, [(0, 0)] * 4 + [(HALF_W, HALF_W)])
    smooth = jnp.zeros_like(gamma)
    for offset in range(-HALF_W, HALF_W + 1):
        weight = (HALF_W + 1 - abs(offset)) / float((HALF_W + 1) ** 2)
        smooth = smooth + weight * padded[..., HALF_W + offset : HALF_W + offset + width]
    power = smooth[:, :, 0] ** 2 + smooth[:, :, 1] ** 2 + 0.01
    filtered = smooth * (power ** (-0.25))[:, :, None]
    cells = lax.all_gather(map_cell, "rng", axis=1, tiled=True).reshape(-1, 1)
    first = (lax.axis_index("acq") * rng_count + lax.axis_index("rng")) * piece
    onehot = (cells == first + jnp.arange(piece, dtype=jnp.int32)).astype(F32)
    count = onehot.sum(axis=0)
    sums = jnp.dot(
        filtered.reshape(-1, cells.shape[0]), onehot, precision=lax.Precision.HIGHEST
    ).reshape(ROUNDS, pairs, 2, piece)
    return sums / jnp.maximum(count, 1.0)


def per_device(slc, map_cell):
    acq_count = lax.axis_size("acq")
    own = slc[:, 0]
    quarter = [(a & -BLOCK) + 2 * SEND[a % BLOCK // 2] + a % 2 for a in range(acq_count)]
    whole = lax.ppermute(own, "acq", list(enumerate(quarter)))
    half = lax.ppermute(pick(own), "acq", [(a, a ^ 1) for a in range(acq_count)])
    small = acq_count == BLOCK
    take = taking(own.shape[2])
    if small:
        blocks = MAPC // (acq_count * lax.axis_size("rng")) // WIDE
        chosen = select(blocks, map_cell, swap(map_cell))
        take, chosen = lax.optimization_barrier((take, chosen))
    first, power, mine = first_matching(own, half, take)
    packed = whole_pair(mine, whole, take, power, first)
    return gather_small(packed, chosen) if small else gather_large(packed, map_cell)


def solution(mesh):
    in_specs = (P(None, ("groups", "acq"), None, "rng"), P("groups", "rng"))
    out_specs = P(None, "groups", None, ("acq", "rng"))
    return jax.shard_map(
        per_device, mesh=mesh, in_specs=in_specs, out_specs=out_specs, check_vma=False
    )
```

```python
import functools

import jax
import jax.numpy as jnp
from jax import lax
from jax.experimental import pallas as pl
from jax.experimental.pallas import tpu as pltpu
from jax.sharding import PartitionSpec as P

LOOK_A = 8
LOOK_R = 8
HALF_W = 4
ROUNDS = 3
BLOCK = 2**ROUNDS
STEPS = ((6, 4, 2), (1,))
SEND = (2, 0, 3, 1)
WHOLE = ((1, 0), (2, 2), (2, 0), (1, 2))
MAPC = 16384
LANES = 128
WIDE = 256
UNIT = 32760.0
F32 = jnp.float32
BF16 = jnp.bfloat16

VMEM = pl.BlockSpec(memory_space=pltpu.VMEM)


def dot(left, right):
    return jnp.dot(left, right, preferred_element_type=F32)


def dot_in_two(left, right):
    rows = left.shape[0]
    high = left.astype(BF16).astype(F32)
    both = dot(jnp.concatenate([high, left - high], axis=0).astype(BF16), right)
    return both[:rows] + both[rows:]


def squared(root):
    root = root.astype(F32)
    return root * jnp.abs(root)


def pick_kernel(own, out):
    half = out.shape[1]
    upper = lax.axis_index("acq") & 1
    out[...] = own[:, pl.ds(pl.multiple_of((1 - upper) * half, half), half), :]


def pick(own):
    parts, lines, width = own.shape
    return pl.pallas_call(
        pick_kernel,
        out_shape=jax.ShapeDtypeStruct((parts, lines // 2, width), own.dtype),
        in_specs=[VMEM],
        out_specs=VMEM,
        name="pick",
        compiler_params=pltpu.CompilerParams(vmem_limit_bytes=2 * 2**20),
        cost_estimate=pl.CostEstimate(flops=2**10, bytes_accessed=2**18, transcendentals=0),
    )(own)


def look_sums(terms, take):
    sums = dot_in_two(terms, take)
    return sums.reshape(terms.shape[0] // LOOK_A, LOOK_A, take.shape[1]).sum(axis=1)


def products(mine_re, mine_im, their_re, their_im):
    return [
        mine_re * their_re + mine_im * their_im,
        mine_im * their_re - mine_re * their_im,
        their_re * their_re + their_im * their_im,
    ]


def normalised(sums, power, sign):
    looks = power.shape[0]
    inverse = lax.rsqrt(power * sums[2 * looks :] + 1e-06)
    return sums[: 2 * looks] * jnp.concatenate([inverse, inverse * sign], axis=0)


def spread(samples, part, wide, out):
    blocks, looks = wide.shape[1], out.shape[3]
    for j in range(blocks):
        wide[part, j, : samples.shape[1]] = samples[part, :, j * LANES : (j + 1) * LANES].astype(F32)
        for i in range(LOOK_A):
            out[part, j, i] = wide[part, j, pl.ds(i, looks, stride=LOOK_A), :]


def first_kernel(own, other, take, out, power, mine, wide):
    half = other.shape[1]
    looks = half // LOOK_A
    own_re, own_im = own[0].astype(F32), own[1].astype(F32)
    power[...] = look_sums(own_re * own_re + own_im * own_im, take[...])
    upper = lax.axis_index("acq") & 1
    rows = pl.ds(pl.multiple_of(upper * half, half), half)
    terms = products(own[0, rows, :].astype(F32), own[1, rows, :].astype(F32), other[0].astype(F32), other[1].astype(F32))
    sums = look_sums(jnp.concatenate(terms, axis=0), take[...])
    half_power = jnp.where(upper == 1, power[looks:], power[:looks])
    out[...] = normalised(sums, half_power, (1 - 2 * upper).astype(F32))
    for part in range(2):
        spread(own, part, wide, mine)


def first_matching(own, other, take):
    parts, lines, width = own.shape
    looks, cells = lines // LOOK_A, width // LOOK_R
    blocks = width // LANES
    shape = jax.ShapeDtypeStruct((looks, cells), F32)
    return pl.pallas_call(
        first_kernel,
        out_shape=(shape, shape, jax.ShapeDtypeStruct((parts, blocks, LOOK_A, looks, LANES), F32)),
        in_specs=[VMEM] * 3,
        out_specs=(VMEM,) * 3,
        scratch_shapes=[pltpu.VMEM((parts, blocks, lines + LOOK_A, LANES), F32)],
        name="first_matching",
        compiler_params=pltpu.CompilerParams(vmem_limit_bytes=4 * 2**20),
        cost_estimate=pl.CostEstimate(flops=2 * 2**20, bytes_accessed=2**18, transcendentals=0),
    )(own, other, take)


def whole_kernel(mine, other, take, power, first, out, wide):
    upper = (lax.axis_index("acq") >> 2) & 1
    blocks, looks = mine.shape[1], mine.shape[3]
    sums = 0.0
    for j in range(blocks):
        for part in range(2):
            wide[part, j, : other.shape[1]] = other[part, :, j * LANES : (j + 1) * LANES].astype(F32)
        total = 0.0
        for i in range(LOOK_A):
            their_re, their_im = (wide[part, j, pl.ds(i, looks, stride=LOOK_A), :] for part in range(2))
            terms = products(mine[0, j, i], mine[1, j, i], their_re, their_im)
            total = total + jnp.concatenate(terms, axis=0)
        sums = sums + dot_in_two(total, take[j * LANES : (j + 1) * LANES])
    whole = normalised(sums, power[...], (1 - 2 * upper).astype(F32))
    packed = jnp.concatenate([first[...], whole], axis=0)
    root = jnp.sqrt(jnp.abs(packed)) * UNIT
    out[...] = jnp.round(jnp.where(packed < 0, -root, root)).astype(jnp.int32).astype(jnp.int16)


def whole_pair(mine, other, take, power, first):
    rows, cells = first.shape
    parts, lines, width = other.shape
    return pl.pallas_call(
        whole_kernel,
        out_shape=jax.ShapeDtypeStruct((3 * rows, cells), jnp.int16),
        in_specs=[VMEM] * 5,
        out_specs=VMEM,
        scratch_shapes=[pltpu.VMEM((parts, width // LANES, lines + LOOK_A, LANES), F32)],
        name="whole_pair",
        compiler_params=pltpu.CompilerParams(vmem_limit_bytes=4 * 2**20),
        cost_estimate=pl.CostEstimate(flops=2 * 2**20, bytes_accessed=2**18, transcendentals=0),
    )(mine, other, take, power, first)


def take_kernel(take):
    sample = lax.broadcasted_iota(jnp.int32, take.shape, 0) // LOOK_R
    cell = lax.broadcasted_iota(jnp.int32, take.shape, 1)
    take[...] = (sample == cell).astype(F32).astype(BF16)


def taking(width):
    return pl.pallas_call(
        take_kernel,
        out_shape=jax.ShapeDtypeStruct((width, width // LOOK_R), BF16),
        out_specs=VMEM,
        name="taking",
        compiler_params=pltpu.CompilerParams(vmem_limit_bytes=2 * 2**20),
        cost_estimate=pl.CostEstimate(flops=2**17, bytes_accessed=2**18, transcendentals=0),
    )()


def select_kernel(blocks, own_cells, other_cells, band, onehot, masks, scale):
    lines, cols = own_cells.shape
    core = lax.axis_index("rng")
    first = (2 * lax.axis_index("acq") + core) * blocks
    own, other = own_cells[...], other_cells[...]
    left_core = core == 0
    halves = [jnp.where(left_core, own, other), jnp.where(left_core, other, own)]
    lane = lax.broadcasted_iota(jnp.int32, (cols, WIDE), 1).astype(F32)
    for side, cells in enumerate(halves):
        low = (cells & (WIDE - 1)).astype(F32)
        tall = jnp.concatenate([low] * (cols // lines), axis=0).T
        for line in range(lines):
            hit = tall[:, line : line + 1] == lane
            start = (line * 2 + side) * cols
            onehot[start : start + cols, :] = hit.astype(F32).astype(BF16)
    wide = jnp.concatenate(halves, axis=1) // WIDE
    mine = [(wide == first + block).astype(F32) for block in range(blocks)]
    for line in range(lines):
        for block in range(blocks):
            masks[line * blocks + block : line * blocks + block + 1, :] = mine[block][line : line + 1]
    count = jnp.zeros((blocks * lines, WIDE), F32)
    for line in range(lines):
        rows = masks[line * blocks : (line + 1) * blocks, :]
        rows = jnp.concatenate([rows] * lines, axis=0).astype(BF16)
        count = count + dot(rows, onehot[line * 2 * cols : (line + 1) * 2 * cols, :])
    scale[...] = 1.0 / jnp.maximum(count[:blocks], 1.0)
    shift = lax.broadcasted_iota(jnp.int32, (2 * cols, 2 * cols), 0)
    shift = jnp.abs(shift - lax.broadcasted_iota(jnp.int32, (2 * cols, 2 * cols), 1))
    band[...] = jnp.maximum(HALF_W + 1 - shift, 0).astype(F32).astype(BF16)


def select(blocks, own_cells, other_cells):
    lines, cols = own_cells.shape
    return pl.pallas_call(
        functools.partial(select_kernel, blocks),
        out_shape=(
            jax.ShapeDtypeStruct((2 * cols, 2 * cols), BF16),
            jax.ShapeDtypeStruct((lines * 2 * cols, WIDE), BF16),
            jax.ShapeDtypeStruct((lines * blocks, 2 * cols), F32),
            jax.ShapeDtypeStruct((blocks, WIDE), F32),
        ),
        in_specs=[VMEM, VMEM],
        out_specs=(VMEM,) * 4,
        name="select",
        compiler_params=pltpu.CompilerParams(vmem_limit_bytes=8 * 2**20),
        cost_estimate=pl.CostEstimate(flops=2 * 2**20, bytes_accessed=2**20, transcendentals=0),
    )(own_cells, other_cells)


def half_sums(held, sent, other_line, band, onehot, masks, by_quarter, grid, filt):
    looks = held.shape[1] // 6
    lines, cols = 2 * looks, held.shape[2]
    quarters = BLOCK // 2
    planes = 4 * quarters
    blocks = masks.shape[0] // lines
    rank, core = lax.axis_index("acq"), lax.axis_index("rng")
    for slot, bits in enumerate((0,) + STEPS[0]):
        quarter, side = (rank ^ bits) >> 1, core ^ (bits != 0) ^ other_line
        by_quarter[quarter, side] = squared(held[slot].astype(jnp.int32))
        by_quarter[quarter, 1 - side] = squared(sent[slot].astype(jnp.int32))
    upper = (rank & 1) ^ other_line
    none = jnp.zeros((looks, cols), F32)
    for side in range(2):
        columns = slice(side * cols, (side + 1) * cols)
        for quarter in range(quarters):
            for part in range(2):
                value = by_quarter[quarter, side, part * looks : (part + 1) * looks, :]
                row = (quarter * 2 + part) * lines
                grid[row : row + looks, columns] = jnp.where(upper == 0, value, none)
                grid[row + looks : row + lines, columns] = jnp.where(upper == 0, none, value)
            row = (planes // 2 + quarter * 2) * lines
            grid[row : row + 2 * lines, columns] = by_quarter[quarter, side, lines:, :]
    smooth = dot_in_two(grid[...], band[...]) * (1.0 / (UNIT * (HALF_W + 1)) ** 2)
    smooth = smooth.reshape(planes // 2, 2, lines, 2 * cols)
    real, imag = smooth[:, 0], smooth[:, 1]
    gain = lax.rsqrt(jnp.sqrt(real * real + imag * imag + 0.01))
    filtered = (smooth * gain[:, None]).reshape(planes * lines, 2 * cols)
    for side in range(2):
        filt[side, : planes * lines] = filtered[:, side * cols : (side + 1) * cols]
    left = []
    for line in range(lines):
        value = [filt[side, pl.ds(line, planes, stride=lines), :] for side in range(2)]
        value = jnp.concatenate(value, axis=1)
        top = value.astype(BF16).astype(F32)
        both = jnp.concatenate([top, value - top], axis=0)
        rows = [both * masks[line * blocks + block : line * blocks + block + 1, :] for block in range(blocks)]
        left.append(jnp.concatenate(rows, axis=0).astype(BF16))
    sums = dot(jnp.concatenate(left, axis=1), onehot[...])
    starts = [block * 2 * planes for block in range(blocks)]
    return [sums[start : start + planes] + sums[start + planes : start + 2 * planes] for start in starts]


def near_kernel(held, sent, band, onehot, masks, scale, out, by_quarter, grid, filt):
    for block, total in enumerate(half_sums(held, sent, 0, band, onehot, masks, by_quarter, grid, filt)):
        out[block] = total * scale[block : block + 1, :]


def far_kernel(held, sent, band, onehot, masks, scale, near, out, by_quarter, grid, filt):
    line = lax.axis_index("acq") & 1
    half = near.shape[1] // 2
    for block, total in enumerate(half_sums(held, sent, 1, band, onehot, masks, by_quarter, grid, filt)):
        total = total * scale[block : block + 1, :]
        ours = near[block]
        columns = slice(block * WIDE, (block + 1) * WIDE)
        for quarter in range(BLOCK // 2):
            rows = slice(2 * quarter, 2 * quarter + 2)
            out[0, quarter, :, columns] = ours[rows] + total[rows]
            r, pair = WHOLE[quarter]
            rows = slice(half + 2 * quarter, half + 2 * quarter + 2)
            out[r, pair + line, :, columns] = ours[rows]
            out[r, pair + 1 - line, :, columns] = total[rows]


def geocode_half(kernel, name, shape, held, sent, *rest):
    slots, rows, cols = held.shape
    lines = rows // 3
    planes = 4 * slots
    return pl.pallas_call(
        kernel,
        out_shape=jax.ShapeDtypeStruct(shape, F32),
        in_specs=[VMEM] * (2 + len(rest)),
        out_specs=VMEM,
        scratch_shapes=[
            pltpu.VMEM((slots, 2, rows, cols), F32),
            pltpu.VMEM((planes * lines, 2 * cols), F32),
            pltpu.VMEM((2, (planes + 1) * lines, cols), F32),
        ],
        name=name,
        compiler_params=pltpu.CompilerParams(vmem_limit_bytes=8 * 2**20),
        cost_estimate=pl.CostEstimate(flops=2**21, bytes_accessed=2**20, transcendentals=2**15),
    )(held, sent, *rest)


def across(value, mask):
    pairs = [(2 * a + c, 2 * (a ^ mask) + 1 - c) for a in range(BLOCK) for c in range(2)]
    return lax.ppermute(value, ("acq", "rng"), pairs)


def swap(value):
    return lax.ppermute(value, "rng", [(0, 1), (1, 0)])


def gather_small(packed, chosen):
    held = packed[None]
    held = jnp.concatenate([held] + [across(held, mask) for mask in STEPS[0]], axis=0)
    far = across(held, STEPS[1][0])
    band, onehot, masks, scale = chosen
    blocks = scale.shape[0]
    near = geocode_half(
        near_kernel, "near_line", (blocks, 2 * BLOCK, WIDE), held, swap(held), band, onehot, masks, scale
    )
    shape = (ROUNDS, BLOCK // 2, 2, blocks * WIDE)
    return geocode_half(far_kernel, "far_line", shape, far, swap(far), band, onehot, masks, scale, near)


def gather_large(packed, map_cell):
    acq_count, rng_count = lax.axis_size("acq"), lax.axis_size("rng")
    pairs, piece = acq_count // 2, MAPC // (acq_count * rng_count)
    rows, cols = packed.shape
    lines, looks, width = rows // 3, rows // 6, rng_count * cols
    whole = lax.all_gather(packed, ("acq", "rng")).reshape(acq_count, rng_count, rows, cols)
    whole = whole.transpose(0, 2, 1, 3).reshape(acq_count, rows, width)
    whole = squared(whole) / UNIT**2
    halves = whole[:, :lines].reshape(pairs, 2, 2, looks, width)
    grids = [halves.transpose(0, 2, 1, 3, 4).reshape(pairs, 2, lines, width)]
    planes = whole[:, lines:].reshape(acq_count // BLOCK, 4, 2, 2, lines, width)
    for r in range(1, ROUNDS):
        quads = sorted((pair, quad) for quad, (found, pair) in enumerate(WHOLE) if found == r)
        grid = jnp.stack([planes[:, quad] for _, quad in quads], axis=1)
        grids.append(grid.reshape(pairs, 2, lines, width))
    gamma = jnp.stack(grids)
    padded = jnp.pad(gamma, [(0, 0)] * 4 + [(HALF_W, HALF_W)])
    smooth = jnp.zeros_like(gamma)
    for offset in range(-HALF_W, HALF_W + 1):
        weight = (HALF_W + 1 - abs(offset)) / float((HALF_W + 1) ** 2)
        smooth = smooth + weight * padded[..., HALF_W + offset : HALF_W + offset + width]
    power = smooth[:, :, 0] ** 2 + smooth[:, :, 1] ** 2 + 0.01
    filtered = smooth * (power ** (-0.25))[:, :, None]
    cells = lax.all_gather(map_cell, "rng", axis=1, tiled=True).reshape(-1, 1)
    first = (lax.axis_index("acq") * rng_count + lax.axis_index("rng")) * piece
    onehot = (cells == first + jnp.arange(piece, dtype=jnp.int32)).astype(F32)
    count = onehot.sum(axis=0)
    sums = jnp.dot(
        filtered.reshape(-1, cells.shape[0]), onehot, precision=lax.Precision.HIGHEST
    ).reshape(ROUNDS, pairs, 2, piece)
    return sums / jnp.maximum(count, 1.0)


def per_device(slc, map_cell):
    acq_count = lax.axis_size("acq")
    own = slc[:, 0]
    quarter = [(a & -BLOCK) + 2 * SEND[a % BLOCK // 2] + a % 2 for a in range(acq_count)]
    whole = lax.ppermute(own, "acq", list(enumerate(quarter)))
    half = lax.ppermute(pick(own), "acq", [(a, a ^ 1) for a in range(acq_count)])
    small = acq_count == BLOCK
    take = taking(own.shape[2])
    if small:
        blocks = MAPC // (acq_count * lax.axis_size("rng")) // WIDE
        chosen = select(blocks, map_cell, swap(map_cell))
        take, chosen = lax.optimization_barrier((take, chosen))
    first, power, mine = first_matching(own, half, take)
    packed = whole_pair(mine, whole, take, power, first)
    return gather_small(packed, chosen) if small else gather_large(packed, map_cell)


def solution(mesh):
    in_specs = (P(None, ("groups", "acq"), None, "rng"), P("groups", "rng"))
    out_specs = P(None, "groups", None, ("acq", "rng"))
    return jax.shard_map(
        per_device, mesh=mesh, in_specs=in_specs, out_specs=out_specs, check_vma=False
    )
```

```python
import functools

import jax
import jax.numpy as jnp
from jax import lax
from jax.experimental import pallas as pl
from jax.experimental.pallas import tpu as pltpu
from jax.sharding import PartitionSpec as P

LOOK_A = 8
LOOK_R = 8
HALF_W = 4
ROUNDS = 3
BLOCK = 2**ROUNDS
STEPS = ((6, 4, 2), (1,))
SEND = (2, 0, 3, 1)
WHOLE = ((1, 0), (2, 2), (2, 0), (1, 2))
MAPC = 16384
LANES = 128
WIDE = 256
UNIT = 32760.0
F32 = jnp.float32
BF16 = jnp.bfloat16

VMEM = pl.BlockSpec(memory_space=pltpu.VMEM)


def dot(left, right):
    return jnp.dot(left, right, preferred_element_type=F32)


def dot_in_two(left, right):
    rows = left.shape[0]
    high = left.astype(BF16).astype(F32)
    both = dot(jnp.concatenate([high, left - high], axis=0).astype(BF16), right)
    return both[:rows] + both[rows:]


def squared(root):
    root = root.astype(F32)
    return root * jnp.abs(root)


def pick_kernel(own, out):
    half = out.shape[1]
    upper = lax.axis_index("acq") & 1
    out[...] = own[:, pl.ds(pl.multiple_of((1 - upper) * half, half), half), :]


def pick(own):
    parts, lines, width = own.shape
    return pl.pallas_call(
        pick_kernel,
        out_shape=jax.ShapeDtypeStruct((parts, lines // 2, width), own.dtype),
        in_specs=[VMEM],
        out_specs=VMEM,
        name="pick",
        compiler_params=pltpu.CompilerParams(vmem_limit_bytes=2 * 2**20),
        cost_estimate=pl.CostEstimate(flops=2**10, bytes_accessed=2**18, transcendentals=0),
    )(own)


def look_sums(terms, take):
    sums = dot_in_two(terms, take)
    return sums.reshape(terms.shape[0] // LOOK_A, LOOK_A, take.shape[1]).sum(axis=1)


def products(mine_re, mine_im, their_re, their_im):
    return [
        mine_re * their_re + mine_im * their_im,
        mine_im * their_re - mine_re * their_im,
        their_re * their_re + their_im * their_im,
    ]


def normalised(sums, power, sign):
    looks = power.shape[0]
    inverse = lax.rsqrt(power * sums[2 * looks :] + 1e-06)
    return sums[: 2 * looks] * jnp.concatenate([inverse, inverse * sign], axis=0)


def spread(samples, part, wide, out):
    blocks, looks = wide.shape[1], out.shape[3]
    for j in range(blocks):
        wide[part, j, : samples.shape[1]] = samples[part, :, j * LANES : (j + 1) * LANES].astype(F32)
        for i in range(LOOK_A):
            out[part, j, i] = wide[part, j, pl.ds(i, looks, stride=LOOK_A), :]


def first_kernel(own, other, take, out, power, mine, wide):
    half = other.shape[1]
    looks = half // LOOK_A
    own_re, own_im = own[0].astype(F32), own[1].astype(F32)
    power[...] = look_sums(own_re * own_re + own_im * own_im, take[...])
    upper = lax.axis_index("acq") & 1
    rows = pl.ds(pl.multiple_of(upper * half, half), half)
    terms = products(own[0, rows, :].astype(F32), own[1, rows, :].astype(F32), other[0].astype(F32), other[1].astype(F32))
    sums = look_sums(jnp.concatenate(terms, axis=0), take[...])
    half_power = jnp.where(upper == 1, power[looks:], power[:looks])
    out[...] = normalised(sums, half_power, (1 - 2 * upper).astype(F32))
    for part in range(2):
        spread(own, part, wide, mine)


def first_matching(own, other, take):
    parts, lines, width = own.shape
    looks, cells = lines // LOOK_A, width // LOOK_R
    blocks = width // LANES
    shape = jax.ShapeDtypeStruct((looks, cells), F32)
    return pl.pallas_call(
        first_kernel,
        out_shape=(shape, shape, jax.ShapeDtypeStruct((parts, blocks, LOOK_A, looks, LANES), F32)),
        in_specs=[VMEM] * 3,
        out_specs=(VMEM,) * 3,
        scratch_shapes=[pltpu.VMEM((parts, blocks, lines + LOOK_A, LANES), F32)],
        name="first_matching",
        compiler_params=pltpu.CompilerParams(vmem_limit_bytes=4 * 2**20),
        cost_estimate=pl.CostEstimate(flops=2 * 2**20, bytes_accessed=2**18, transcendentals=0),
    )(own, other, take)


def whole_kernel(mine, other, take, power, first, out, wide):
    upper = (lax.axis_index("acq") >> 2) & 1
    blocks, looks = mine.shape[1], mine.shape[3]
    sums = 0.0
    for j in range(blocks):
        for part in range(2):
            wide[part, j, : other.shape[1]] = other[part, :, j * LANES : (j + 1) * LANES].astype(F32)
        total = 0.0
        for i in range(LOOK_A):
            their_re, their_im = (wide[part, j, pl.ds(i, looks, stride=LOOK_A), :] for part in range(2))
            terms = products(mine[0, j, i], mine[1, j, i], their_re, their_im)
            total = total + jnp.concatenate(terms, axis=0)
        sums = sums + dot_in_two(total, take[j * LANES : (j + 1) * LANES])
    whole = normalised(sums, power[...], (1 - 2 * upper).astype(F32))
    packed = jnp.concatenate([first[...], whole], axis=0)
    root = jnp.sqrt(jnp.abs(packed)) * UNIT
    out[...] = jnp.round(jnp.where(packed < 0, -root, root)).astype(jnp.int32).astype(jnp.int16)


def whole_pair(mine, other, take, power, first):
    rows, cells = first.shape
    parts, lines, width = other.shape
    return pl.pallas_call(
        whole_kernel,
        out_shape=jax.ShapeDtypeStruct((3 * rows, cells), jnp.int16),
        in_specs=[VMEM] * 5,
        out_specs=VMEM,
        scratch_shapes=[pltpu.VMEM((parts, width // LANES, lines + LOOK_A, LANES), F32)],
        name="whole_pair",
        compiler_params=pltpu.CompilerParams(vmem_limit_bytes=4 * 2**20),
        cost_estimate=pl.CostEstimate(flops=2 * 2**20, bytes_accessed=2**18, transcendentals=0),
    )(mine, other, take, power, first)


def take_kernel(take):
    sample = lax.broadcasted_iota(jnp.int32, take.shape, 0) // LOOK_R
    cell = lax.broadcasted_iota(jnp.int32, take.shape, 1)
    take[...] = (sample == cell).astype(F32).astype(BF16)


def taking(width):
    return pl.pallas_call(
        take_kernel,
        out_shape=jax.ShapeDtypeStruct((width, width // LOOK_R), BF16),
        out_specs=VMEM,
        name="taking",
        compiler_params=pltpu.CompilerParams(vmem_limit_bytes=2 * 2**20),
        cost_estimate=pl.CostEstimate(flops=2**17, bytes_accessed=2**18, transcendentals=0),
    )()


def select_kernel(blocks, own_cells, other_cells, band, onehot, masks, scale):
    lines, cols = own_cells.shape
    core = lax.axis_index("rng")
    first = (2 * lax.axis_index("acq") + core) * blocks
    own, other = own_cells[...], other_cells[...]
    left_core = core == 0
    halves = [jnp.where(left_core, own, other), jnp.where(left_core, other, own)]
    lane = lax.broadcasted_iota(jnp.int32, (cols, WIDE), 1).astype(F32)
    for side, cells in enumerate(halves):
        low = (cells & (WIDE - 1)).astype(F32)
        tall = jnp.concatenate([low] * (cols // lines), axis=0).T
        for line in range(lines):
            hit = tall[:, line : line + 1] == lane
            start = (line * 2 + side) * cols
            onehot[start : start + cols, :] = hit.astype(F32).astype(BF16)
    wide = jnp.concatenate(halves, axis=1) // WIDE
    mine = [(wide == first + block).astype(F32) for block in range(blocks)]
    for line in range(lines):
        for block in range(blocks):
            masks[line * blocks + block : line * blocks + block + 1, :] = mine[block][line : line + 1]
    count = jnp.zeros((blocks * lines, WIDE), F32)
    for line in range(lines):
        rows = masks[line * blocks : (line + 1) * blocks, :]
        rows = jnp.concatenate([rows] * lines, axis=0).astype(BF16)
        count = count + dot(rows, onehot[line * 2 * cols : (line + 1) * 2 * cols, :])
    scale[...] = 1.0 / jnp.maximum(count[:blocks], 1.0)
    shift = lax.broadcasted_iota(jnp.int32, (2 * cols, 2 * cols), 0)
    shift = jnp.abs(shift - lax.broadcasted_iota(jnp.int32, (2 * cols, 2 * cols), 1))
    band[...] = jnp.maximum(HALF_W + 1 - shift, 0).astype(F32).astype(BF16)


def select(blocks, own_cells, other_cells):
    lines, cols = own_cells.shape
    return pl.pallas_call(
        functools.partial(select_kernel, blocks),
        out_shape=(
            jax.ShapeDtypeStruct((2 * cols, 2 * cols), BF16),
            jax.ShapeDtypeStruct((lines * 2 * cols, WIDE), BF16),
            jax.ShapeDtypeStruct((lines * blocks, 2 * cols), F32),
            jax.ShapeDtypeStruct((blocks, WIDE), F32),
        ),
        in_specs=[VMEM, VMEM],
        out_specs=(VMEM,) * 4,
        name="select",
        compiler_params=pltpu.CompilerParams(vmem_limit_bytes=8 * 2**20),
        cost_estimate=pl.CostEstimate(flops=2 * 2**20, bytes_accessed=2**20, transcendentals=0),
    )(own_cells, other_cells)


def half_sums(held, sent, other_line, band, onehot, masks, by_quarter, grid, filt):
    looks = held.shape[1] // 6
    lines, cols = 2 * looks, held.shape[2]
    quarters = BLOCK // 2
    planes = 4 * quarters
    blocks = masks.shape[0] // lines
    rank, core = lax.axis_index("acq"), lax.axis_index("rng")
    for slot, bits in enumerate((0,) + STEPS[0]):
        quarter, side = (rank ^ bits) >> 1, core ^ (bits != 0) ^ other_line
        by_quarter[quarter, side] = squared(held[slot].astype(jnp.int32))
        by_quarter[quarter, 1 - side] = squared(sent[slot].astype(jnp.int32))
    upper = (rank & 1) ^ other_line
    none = jnp.zeros((looks, cols), F32)
    for side in range(2):
        columns = slice(side * cols, (side + 1) * cols)
        for quarter in range(quarters):
            for part in range(2):
                value = by_quarter[quarter, side, part * looks : (part + 1) * looks, :]
                row = (quarter * 2 + part) * lines
                grid[row : row + looks, columns] = jnp.where(upper == 0, value, none)
                grid[row + looks : row + lines, columns] = jnp.where(upper == 0, none, value)
            row = (planes // 2 + quarter * 2) * lines
            grid[row : row + 2 * lines, columns] = by_quarter[quarter, side, lines:, :]
    smooth = dot_in_two(grid[...], band[...]) * (1.0 / (UNIT * (HALF_W + 1)) ** 2)
    smooth = smooth.reshape(planes // 2, 2, lines, 2 * cols)
    real, imag = smooth[:, 0], smooth[:, 1]
    gain = lax.rsqrt(jnp.sqrt(real * real + imag * imag + 0.01))
    filtered = (smooth * gain[:, None]).reshape(planes * lines, 2 * cols)
    for side in range(2):
        filt[side, : planes * lines] = filtered[:, side * cols : (side + 1) * cols]
    left = []
    for line in range(lines):
        value = [filt[side, pl.ds(line, planes, stride=lines), :] for side in range(2)]
        value = jnp.concatenate(value, axis=1)
        top = value.astype(BF16).astype(F32)
        both = jnp.concatenate([top, value - top], axis=0)
        rows = [both * masks[line * blocks + block : line * blocks + block + 1, :] for block in range(blocks)]
        left.append(jnp.concatenate(rows, axis=0).astype(BF16))
    middle = lines // 2
    sums = dot(jnp.concatenate(left[:middle], axis=1), onehot[: middle * 2 * cols, :])
    sums = sums + dot(jnp.concatenate(left[middle:], axis=1), onehot[middle * 2 * cols :, :])
    starts = [block * 2 * planes for block in range(blocks)]
    return [sums[start : start + planes] + sums[start + planes : start + 2 * planes] for start in starts]


def near_kernel(held, sent, band, onehot, masks, scale, out, by_quarter, grid, filt):
    for block, total in enumerate(half_sums(held, sent, 0, band, onehot, masks, by_quarter, grid, filt)):
        out[block] = total * scale[block : block + 1, :]


def far_kernel(held, sent, band, onehot, masks, scale, near, out, by_quarter, grid, filt):
    line = lax.axis_index("acq") & 1
    half = near.shape[1] // 2
    for block, total in enumerate(half_sums(held, sent, 1, band, onehot, masks, by_quarter, grid, filt)):
        total = total * scale[block : block + 1, :]
        ours = near[block]
        columns = slice(block * WIDE, (block + 1) * WIDE)
        for quarter in range(BLOCK // 2):
            rows = slice(2 * quarter, 2 * quarter + 2)
            out[0, quarter, :, columns] = ours[rows] + total[rows]
            r, pair = WHOLE[quarter]
            rows = slice(half + 2 * quarter, half + 2 * quarter + 2)
            out[r, pair + line, :, columns] = ours[rows]
            out[r, pair + 1 - line, :, columns] = total[rows]


def geocode_half(kernel, name, shape, held, sent, *rest):
    slots, rows, cols = held.shape
    lines = rows // 3
    planes = 4 * slots
    return pl.pallas_call(
        kernel,
        out_shape=jax.ShapeDtypeStruct(shape, F32),
        in_specs=[VMEM] * (2 + len(rest)),
        out_specs=VMEM,
        scratch_shapes=[
            pltpu.VMEM((slots, 2, rows, cols), F32),
            pltpu.VMEM((planes * lines, 2 * cols), F32),
            pltpu.VMEM((2, (planes + 1) * lines, cols), F32),
        ],
        name=name,
        compiler_params=pltpu.CompilerParams(vmem_limit_bytes=8 * 2**20),
        cost_estimate=pl.CostEstimate(flops=2**21, bytes_accessed=2**20, transcendentals=2**15),
    )(held, sent, *rest)


def across(value, mask):
    pairs = [(2 * a + c, 2 * (a ^ mask) + 1 - c) for a in range(BLOCK) for c in range(2)]
    return lax.ppermute(value, ("acq", "rng"), pairs)


def swap(value):
    return lax.ppermute(value, "rng", [(0, 1), (1, 0)])


def gather_small(packed, chosen):
    held = packed[None]
    held = jnp.concatenate([held] + [across(held, mask) for mask in STEPS[0]], axis=0)
    far = across(held, STEPS[1][0])
    band, onehot, masks, scale = chosen
    blocks = scale.shape[0]
    near = geocode_half(
        near_kernel, "near_line", (blocks, 2 * BLOCK, WIDE), held, swap(held), band, onehot, masks, scale
    )
    shape = (ROUNDS, BLOCK // 2, 2, blocks * WIDE)
    return geocode_half(far_kernel, "far_line", shape, far, swap(far), band, onehot, masks, scale, near)


def gather_large(packed, map_cell):
    acq_count, rng_count = lax.axis_size("acq"), lax.axis_size("rng")
    pairs, piece = acq_count // 2, MAPC // (acq_count * rng_count)
    rows, cols = packed.shape
    lines, looks, width = rows // 3, rows // 6, rng_count * cols
    whole = lax.all_gather(packed, ("acq", "rng")).reshape(acq_count, rng_count, rows, cols)
    whole = whole.transpose(0, 2, 1, 3).reshape(acq_count, rows, width)
    whole = squared(whole) / UNIT**2
    halves = whole[:, :lines].reshape(pairs, 2, 2, looks, width)
    grids = [halves.transpose(0, 2, 1, 3, 4).reshape(pairs, 2, lines, width)]
    planes = whole[:, lines:].reshape(acq_count // BLOCK, 4, 2, 2, lines, width)
    for r in range(1, ROUNDS):
        quads = sorted((pair, quad) for quad, (found, pair) in enumerate(WHOLE) if found == r)
        grid = jnp.stack([planes[:, quad] for _, quad in quads], axis=1)
        grids.append(grid.reshape(pairs, 2, lines, width))
    gamma = jnp.stack(grids)
    padded = jnp.pad(gamma, [(0, 0)] * 4 + [(HALF_W, HALF_W)])
    smooth = jnp.zeros_like(gamma)
    for offset in range(-HALF_W, HALF_W + 1):
        weight = (HALF_W + 1 - abs(offset)) / float((HALF_W + 1) ** 2)
        smooth = smooth + weight * padded[..., HALF_W + offset : HALF_W + offset + width]
    power = smooth[:, :, 0] ** 2 + smooth[:, :, 1] ** 2 + 0.01
    filtered = smooth * (power ** (-0.25))[:, :, None]
    cells = lax.all_gather(map_cell, "rng", axis=1, tiled=True).reshape(-1, 1)
    first = (lax.axis_index("acq") * rng_count + lax.axis_index("rng")) * piece
    onehot = (cells == first + jnp.arange(piece, dtype=jnp.int32)).astype(F32)
    count = onehot.sum(axis=0)
    sums = jnp.dot(
        filtered.reshape(-1, cells.shape[0]), onehot, precision=lax.Precision.HIGHEST
    ).reshape(ROUNDS, pairs, 2, piece)
    return sums / jnp.maximum(count, 1.0)


def per_device(slc, map_cell):
    acq_count = lax.axis_size("acq")
    own = slc[:, 0]
    quarter = [(a & -BLOCK) + 2 * SEND[a % BLOCK // 2] + a % 2 for a in range(acq_count)]
    whole = lax.ppermute(own, "acq", list(enumerate(quarter)))
    half = lax.ppermute(pick(own), "acq", [(a, a ^ 1) for a in range(acq_count)])
    small = acq_count == BLOCK
    take = taking(own.shape[2])
    if small:
        blocks = MAPC // (acq_count * lax.axis_size("rng")) // WIDE
        chosen = select(blocks, map_cell, swap(map_cell))
        take, chosen = lax.optimization_barrier((take, chosen))
    first, power, mine = first_matching(own, half, take)
    packed = whole_pair(mine, whole, take, power, first)
    return gather_small(packed, chosen) if small else gather_large(packed, map_cell)


def solution(mesh):
    in_specs = (P(None, ("groups", "acq"), None, "rng"), P("groups", "rng"))
    out_specs = P(None, "groups", None, ("acq", "rng"))
    return jax.shard_map(
        per_device, mesh=mesh, in_specs=in_specs, out_specs=out_specs, check_vma=False
    )
```

```python
import functools

import jax
import jax.numpy as jnp
from jax import lax
from jax.experimental import pallas as pl
from jax.experimental.pallas import tpu as pltpu
from jax.sharding import PartitionSpec as P

LOOK_A = 8
LOOK_R = 8
HALF_W = 4
ROUNDS = 3
BLOCK = 2**ROUNDS
STEPS = ((1,), (6, 4, 2))
SEND = (2, 0, 3, 1)
WHOLE = ((1, 0), (2, 2), (2, 0), (1, 2))
MAPC = 16384
LANES = 128
WIDE = 256
UNIT = 32760.0
F32 = jnp.float32
BF16 = jnp.bfloat16

VMEM = pl.BlockSpec(memory_space=pltpu.VMEM)


def dot(left, right):
    return jnp.dot(left, right, preferred_element_type=F32)


def dot_in_two(left, right):
    rows = left.shape[0]
    high = left.astype(BF16).astype(F32)
    both = dot(jnp.concatenate([high, left - high], axis=0).astype(BF16), right)
    return both[:rows] + both[rows:]


def squared(root):
    root = root.astype(F32)
    return root * jnp.abs(root)


def pick_kernel(own, out):
    half = out.shape[1]
    upper = lax.axis_index("acq") & 1
    out[...] = own[:, pl.ds(pl.multiple_of((1 - upper) * half, half), half), :]


def pick(own):
    parts, lines, width = own.shape
    return pl.pallas_call(
        pick_kernel,
        out_shape=jax.ShapeDtypeStruct((parts, lines // 2, width), own.dtype),
        in_specs=[VMEM],
        out_specs=VMEM,
        name="pick",
        compiler_params=pltpu.CompilerParams(vmem_limit_bytes=2 * 2**20),
        cost_estimate=pl.CostEstimate(flops=2**10, bytes_accessed=2**18, transcendentals=0),
    )(own)


def look_sums(terms, take):
    sums = dot_in_two(terms, take)
    return sums.reshape(terms.shape[0] // LOOK_A, LOOK_A, take.shape[1]).sum(axis=1)


def products(mine_re, mine_im, their_re, their_im):
    return [
        mine_re * their_re + mine_im * their_im,
        mine_im * their_re - mine_re * their_im,
        their_re * their_re + their_im * their_im,
    ]


def normalised(sums, power, sign):
    looks = power.shape[0]
    inverse = lax.rsqrt(power * sums[2 * looks :] + 1e-06)
    return sums[: 2 * looks] * jnp.concatenate([inverse, inverse * sign], axis=0)


def spread(samples, part, wide, out):
    blocks, looks = wide.shape[1], out.shape[3]
    for j in range(blocks):
        wide[part, j, : samples.shape[1]] = samples[part, :, j * LANES : (j + 1) * LANES].astype(F32)
        for i in range(LOOK_A):
            out[part, j, i] = wide[part, j, pl.ds(i, looks, stride=LOOK_A), :]


def first_kernel(own, other, take, out, power, mine, wide):
    half = other.shape[1]
    looks = half // LOOK_A
    own_re, own_im = own[0].astype(F32), own[1].astype(F32)
    power[...] = look_sums(own_re * own_re + own_im * own_im, take[...])
    upper = lax.axis_index("acq") & 1
    rows = pl.ds(pl.multiple_of(upper * half, half), half)
    terms = products(own[0, rows, :].astype(F32), own[1, rows, :].astype(F32), other[0].astype(F32), other[1].astype(F32))
    sums = look_sums(jnp.concatenate(terms, axis=0), take[...])
    half_power = jnp.where(upper == 1, power[looks:], power[:looks])
    out[...] = normalised(sums, half_power, (1 - 2 * upper).astype(F32))
    for part in range(2):
        spread(own, part, wide, mine)


def first_matching(own, other, take):
    parts, lines, width = own.shape
    looks, cells = lines // LOOK_A, width // LOOK_R
    blocks = width // LANES
    shape = jax.ShapeDtypeStruct((looks, cells), F32)
    return pl.pallas_call(
        first_kernel,
        out_shape=(shape, shape, jax.ShapeDtypeStruct((parts, blocks, LOOK_A, looks, LANES), F32)),
        in_specs=[VMEM] * 3,
        out_specs=(VMEM,) * 3,
        scratch_shapes=[pltpu.VMEM((parts, blocks, lines + LOOK_A, LANES), F32)],
        name="first_matching",
        compiler_params=pltpu.CompilerParams(vmem_limit_bytes=4 * 2**20),
        cost_estimate=pl.CostEstimate(flops=2 * 2**20, bytes_accessed=2**18, transcendentals=0),
    )(own, other, take)


def whole_kernel(mine, other, take, power, first, out, wide):
    upper = (lax.axis_index("acq") >> 2) & 1
    blocks, looks = mine.shape[1], mine.shape[3]
    sums = 0.0
    for j in range(blocks):
        for part in range(2):
            wide[part, j, : other.shape[1]] = other[part, :, j * LANES : (j + 1) * LANES].astype(F32)
        total = 0.0
        for i in range(LOOK_A):
            their_re, their_im = (wide[part, j, pl.ds(i, looks, stride=LOOK_A), :] for part in range(2))
            terms = products(mine[0, j, i], mine[1, j, i], their_re, their_im)
            total = total + jnp.concatenate(terms, axis=0)
        sums = sums + dot_in_two(total, take[j * LANES : (j + 1) * LANES])
    whole = normalised(sums, power[...], (1 - 2 * upper).astype(F32))
    packed = jnp.concatenate([first[...], whole], axis=0)
    root = jnp.sqrt(jnp.abs(packed)) * UNIT
    out[...] = jnp.round(jnp.where(packed < 0, -root, root)).astype(jnp.int32).astype(jnp.int16)


def whole_pair(mine, other, take, power, first):
    rows, cells = first.shape
    parts, lines, width = other.shape
    return pl.pallas_call(
        whole_kernel,
        out_shape=jax.ShapeDtypeStruct((3 * rows, cells), jnp.int16),
        in_specs=[VMEM] * 5,
        out_specs=VMEM,
        scratch_shapes=[pltpu.VMEM((parts, width // LANES, lines + LOOK_A, LANES), F32)],
        name="whole_pair",
        compiler_params=pltpu.CompilerParams(vmem_limit_bytes=4 * 2**20),
        cost_estimate=pl.CostEstimate(flops=2 * 2**20, bytes_accessed=2**18, transcendentals=0),
    )(mine, other, take, power, first)


def take_kernel(take):
    sample = lax.broadcasted_iota(jnp.int32, take.shape, 0) // LOOK_R
    cell = lax.broadcasted_iota(jnp.int32, take.shape, 1)
    take[...] = (sample == cell).astype(F32).astype(BF16)


def taking(width):
    return pl.pallas_call(
        take_kernel,
        out_shape=jax.ShapeDtypeStruct((width, width // LOOK_R), BF16),
        out_specs=VMEM,
        name="taking",
        compiler_params=pltpu.CompilerParams(vmem_limit_bytes=2 * 2**20),
        cost_estimate=pl.CostEstimate(flops=2**17, bytes_accessed=2**18, transcendentals=0),
    )()


def select_kernel(blocks, own_cells, other_cells, band, onehot, masks, scale):
    lines, cols = own_cells.shape
    core = lax.axis_index("rng")
    first = (2 * lax.axis_index("acq") + core) * blocks
    own, other = own_cells[...], other_cells[...]
    left_core = core == 0
    halves = [jnp.where(left_core, own, other), jnp.where(left_core, other, own)]
    lane = lax.broadcasted_iota(jnp.int32, (cols, WIDE), 1).astype(F32)
    for side, cells in enumerate(halves):
        low = (cells & (WIDE - 1)).astype(F32)
        tall = jnp.concatenate([low] * (cols // lines), axis=0).T
        for line in range(lines):
            hit = tall[:, line : line + 1] == lane
            start = (line * 2 + side) * cols
            onehot[start : start + cols, :] = hit.astype(F32).astype(BF16)
    wide = jnp.concatenate(halves, axis=1) // WIDE
    mine = [(wide == first + block).astype(F32) for block in range(blocks)]
    for line in range(lines):
        for block in range(blocks):
            masks[line * blocks + block : line * blocks + block + 1, :] = mine[block][line : line + 1]
    count = jnp.zeros((blocks * lines, WIDE), F32)
    for line in range(lines):
        rows = masks[line * blocks : (line + 1) * blocks, :]
        rows = jnp.concatenate([rows] * lines, axis=0).astype(BF16)
        count = count + dot(rows, onehot[line * 2 * cols : (line + 1) * 2 * cols, :])
    scale[...] = 1.0 / jnp.maximum(count[:blocks], 1.0)
    shift = lax.broadcasted_iota(jnp.int32, (2 * cols, 2 * cols), 0)
    shift = jnp.abs(shift - lax.broadcasted_iota(jnp.int32, (2 * cols, 2 * cols), 1))
    band[...] = jnp.maximum(HALF_W + 1 - shift, 0).astype(F32).astype(BF16)


def select(blocks, own_cells, other_cells):
    lines, cols = own_cells.shape
    return pl.pallas_call(
        functools.partial(select_kernel, blocks),
        out_shape=(
            jax.ShapeDtypeStruct((2 * cols, 2 * cols), BF16),
            jax.ShapeDtypeStruct((lines * 2 * cols, WIDE), BF16),
            jax.ShapeDtypeStruct((lines * blocks, 2 * cols), F32),
            jax.ShapeDtypeStruct((blocks, WIDE), F32),
        ),
        in_specs=[VMEM, VMEM],
        out_specs=(VMEM,) * 4,
        name="select",
        compiler_params=pltpu.CompilerParams(vmem_limit_bytes=8 * 2**20),
        cost_estimate=pl.CostEstimate(flops=2 * 2**20, bytes_accessed=2**20, transcendentals=0),
    )(own_cells, other_cells)


def geocode_kernel(held, sent, band, onehot, masks, scale, out, by_acq, grid, filt):
    pairs = BLOCK // 2
    looks = held.shape[1] // 6
    lines, cols = 2 * looks, held.shape[2]
    planes = ROUNDS * pairs * 2
    blocks = scale.shape[0]
    rank, core = lax.axis_index("acq"), lax.axis_index("rng")
    origins = [(0, 0)]
    for step in STEPS:
        origins = origins + [(bits ^ mask, 1 - other) for mask in step for bits, other in origins]
    for slot, (bits, other) in enumerate(origins):
        acq, side = rank ^ bits, core ^ other
        by_acq[acq, side] = squared(held[slot].astype(jnp.int32))
        by_acq[acq, 1 - side] = squared(sent[slot].astype(jnp.int32))
    for side in range(2):
        columns = slice(side * cols, (side + 1) * cols)
        for acq in range(BLOCK):
            for part in range(2):
                row = (acq // 2 * 2 + part) * lines + (acq & 1) * looks
                grid[row : row + looks, columns] = by_acq[acq, side, part * looks : (part + 1) * looks, :]
            r, pair = WHOLE[acq >> 1]
            row = (r * pairs + pair + (acq & 1)) * 2 * lines
            grid[row : row + 2 * lines, columns] = by_acq[acq, side, lines:, :]
    smooth = dot_in_two(grid[...], band[...]) * (1.0 / (UNIT * (HALF_W + 1)) ** 2)
    smooth = smooth.reshape(planes // 2, 2, lines, 2 * cols)
    real, imag = smooth[:, 0], smooth[:, 1]
    gain = lax.rsqrt(jnp.sqrt(real * real + imag * imag + 0.01))
    filtered = (smooth * gain[:, None]).reshape(planes * lines, 2 * cols)
    for side in range(2):
        filt[side, : planes * lines] = filtered[:, side * cols : (side + 1) * cols]
    left = []
    for line in range(lines):
        value = [filt[side, pl.ds(line, planes, stride=lines), :] for side in range(2)]
        value = jnp.concatenate(value, axis=1)
        top = value.astype(BF16).astype(F32)
        both = jnp.concatenate([top, value - top], axis=0)
        rows = [both * masks[line * blocks + block : line * blocks + block + 1, :] for block in range(blocks)]
        left.append(jnp.concatenate(rows, axis=0).astype(BF16))
    sums = dot(jnp.concatenate(left, axis=1), onehot[...])
    for block in range(blocks):
        start = block * 2 * planes
        total = sums[start : start + planes] + sums[start + planes : start + 2 * planes]
        total = total * scale[block : block + 1, :]
        for plane in range(0, planes, 2):
            r, pair = plane // (2 * pairs), plane // 2 % pairs
            out[r, pair, :, block * WIDE : (block + 1) * WIDE] = total[plane : plane + 2]


def geocode(held, sent, band, onehot, masks, scale):
    pairs, blocks = BLOCK // 2, scale.shape[0]
    _, rows, cols = held.shape
    lines = rows // 3
    return pl.pallas_call(
        geocode_kernel,
        out_shape=jax.ShapeDtypeStruct((ROUNDS, pairs, 2, blocks * WIDE), F32),
        in_specs=[VMEM] * 6,
        out_specs=VMEM,
        scratch_shapes=[
            pltpu.VMEM((BLOCK, 2, rows, cols), F32),
            pltpu.VMEM((ROUNDS * pairs * 2 * lines, 2 * cols), F32),
            pltpu.VMEM((2, (ROUNDS * pairs * 2 + 1) * lines, cols), F32),
        ],
        name="geocode",
        compiler_params=pltpu.CompilerParams(vmem_limit_bytes=8 * 2**20),
        cost_estimate=pl.CostEstimate(flops=2**28, bytes_accessed=2**21, transcendentals=2**16),
    )(held, sent, band, onehot, masks, scale)


def across(value, mask):
    pairs = [(2 * a + c, 2 * (a ^ mask) + 1 - c) for a in range(BLOCK) for c in range(2)]
    return lax.ppermute(value, ("acq", "rng"), pairs)


def swap(value):
    return lax.ppermute(value, "rng", [(0, 1), (1, 0)])


def gather_small(packed, chosen):
    held = packed[None]
    for step in STEPS[:-1]:
        held = jnp.concatenate([held] + [across(held, mask) for mask in step], axis=0)
    last = [across(held, mask) for mask in STEPS[-1]]
    early = swap(jnp.concatenate([held] + last[:1], axis=0))
    late = swap(jnp.concatenate(last[1:], axis=0))
    return geocode(jnp.concatenate([held] + last, axis=0), jnp.concatenate([early, late], axis=0), *chosen)


def gather_large(packed, map_cell):
    acq_count, rng_count = lax.axis_size("acq"), lax.axis_size("rng")
    pairs, piece = acq_count // 2, MAPC // (acq_count * rng_count)
    rows, cols = packed.shape
    lines, looks, width = rows // 3, rows // 6, rng_count * cols
    whole = lax.all_gather(packed, ("acq", "rng")).reshape(acq_count, rng_count, rows, cols)
    whole = whole.transpose(0, 2, 1, 3).reshape(acq_count, rows, width)
    whole = squared(whole) / UNIT**2
    halves = whole[:, :lines].reshape(pairs, 2, 2, looks, width)
    grids = [halves.transpose(0, 2, 1, 3, 4).reshape(pairs, 2, lines, width)]
    planes = whole[:, lines:].reshape(acq_count // BLOCK, 4, 2, 2, lines, width)
    for r in range(1, ROUNDS):
        quads = sorted((pair, quad) for quad, (found, pair) in enumerate(WHOLE) if found == r)
        grid = jnp.stack([planes[:, quad] for _, quad in quads], axis=1)
        grids.append(grid.reshape(pairs, 2, lines, width))
    gamma = jnp.stack(grids)
    padded = jnp.pad(gamma, [(0, 0)] * 4 + [(HALF_W, HALF_W)])
    smooth = jnp.zeros_like(gamma)
    for offset in range(-HALF_W, HALF_W + 1):
        weight = (HALF_W + 1 - abs(offset)) / float((HALF_W + 1) ** 2)
        smooth = smooth + weight * padded[..., HALF_W + offset : HALF_W + offset + width]
    power = smooth[:, :, 0] ** 2 + smooth[:, :, 1] ** 2 + 0.01
    filtered = smooth * (power ** (-0.25))[:, :, None]
    cells = lax.all_gather(map_cell, "rng", axis=1, tiled=True).reshape(-1, 1)
    first = (lax.axis_index("acq") * rng_count + lax.axis_index("rng")) * piece
    onehot = (cells == first + jnp.arange(piece, dtype=jnp.int32)).astype(F32)
    count = onehot.sum(axis=0)
    sums = jnp.dot(
        filtered.reshape(-1, cells.shape[0]), onehot, precision=lax.Precision.HIGHEST
    ).reshape(ROUNDS, pairs, 2, piece)
    return sums / jnp.maximum(count, 1.0)


def per_device(slc, map_cell):
    acq_count = lax.axis_size("acq")
    own = slc[:, 0]
    quarter = [(a & -BLOCK) + 2 * SEND[a % BLOCK // 2] + a % 2 for a in range(acq_count)]
    whole = lax.ppermute(own, "acq", list(enumerate(quarter)))
    half = lax.ppermute(pick(own), "acq", [(a, a ^ 1) for a in range(acq_count)])
    small = acq_count == BLOCK
    take = taking(own.shape[2])
    if small:
        blocks = MAPC // (acq_count * lax.axis_size("rng")) // WIDE
        chosen = select(blocks, map_cell, swap(map_cell))
        take, chosen = lax.optimization_barrier((take, chosen))
    first, power, mine = first_matching(own, half, take)
    packed = whole_pair(mine, whole, take, power, first)
    return gather_small(packed, chosen) if small else gather_large(packed, map_cell)


def solution(mesh):
    in_specs = (P(None, ("groups", "acq"), None, "rng"), P("groups", "rng"))
    out_specs = P(None, "groups", None, ("acq", "rng"))
    return jax.shard_map(
        per_device, mesh=mesh, in_specs=in_specs, out_specs=out_specs, check_vma=False
    )
```

```python
import functools

import jax
import jax.numpy as jnp
from jax import lax
from jax.experimental import pallas as pl
from jax.experimental.pallas import tpu as pltpu
from jax.sharding import PartitionSpec as P

LOOK_A = 8
LOOK_R = 8
HALF_W = 4
ROUNDS = 3
BLOCK = 2**ROUNDS
STEPS = ((1,), (6, 4, 2))
SEND = (2, 0, 3, 1)
WHOLE = ((1, 0), (2, 2), (2, 0), (1, 2))
MAPC = 16384
LANES = 128
WIDE = 256
UNIT = 32760.0
F32 = jnp.float32
BF16 = jnp.bfloat16

VMEM = pl.BlockSpec(memory_space=pltpu.VMEM)


def dot(left, right):
    return jnp.dot(left, right, preferred_element_type=F32)


def dot_in_two(left, right):
    rows = left.shape[0]
    high = left.astype(BF16).astype(F32)
    both = dot(jnp.concatenate([high, left - high], axis=0).astype(BF16), right)
    return both[:rows] + both[rows:]


def squared(root):
    root = root.astype(F32)
    return root * jnp.abs(root)


def pick_kernel(own, out):
    half = out.shape[1]
    upper = lax.axis_index("acq") & 1
    out[...] = own[:, pl.ds(pl.multiple_of((1 - upper) * half, half), half), :]


def pick(own):
    parts, lines, width = own.shape
    return pl.pallas_call(
        pick_kernel,
        out_shape=jax.ShapeDtypeStruct((parts, lines // 2, width), own.dtype),
        in_specs=[VMEM],
        out_specs=VMEM,
        name="pick",
        compiler_params=pltpu.CompilerParams(vmem_limit_bytes=2 * 2**20),
        cost_estimate=pl.CostEstimate(flops=2**10, bytes_accessed=2**18, transcendentals=0),
    )(own)


def look_sums(terms, take):
    sums = dot_in_two(terms, take)
    return sums.reshape(terms.shape[0] // LOOK_A, LOOK_A, take.shape[1]).sum(axis=1)


def products(mine_re, mine_im, their_re, their_im):
    return [
        mine_re * their_re + mine_im * their_im,
        mine_im * their_re - mine_re * their_im,
        their_re * their_re + their_im * their_im,
    ]


def normalised(sums, power, sign):
    looks = power.shape[0]
    inverse = lax.rsqrt(power * sums[2 * looks :] + 1e-06)
    return sums[: 2 * looks] * jnp.concatenate([inverse, inverse * sign], axis=0)


def spread(samples, part, wide, out):
    blocks, looks = wide.shape[1], out.shape[3]
    for j in range(blocks):
        wide[part, j, : samples.shape[1]] = samples[part, :, j * LANES : (j + 1) * LANES].astype(F32)
        for i in range(LOOK_A):
            out[part, j, i] = wide[part, j, pl.ds(i, looks, stride=LOOK_A), :]


def first_kernel(own, other, take, out, power, mine, wide):
    half = other.shape[1]
    looks = half // LOOK_A
    own_re, own_im = own[0].astype(F32), own[1].astype(F32)
    power[...] = look_sums(own_re * own_re + own_im * own_im, take[...])
    upper = lax.axis_index("acq") & 1
    rows = pl.ds(pl.multiple_of(upper * half, half), half)
    terms = products(own[0, rows, :].astype(F32), own[1, rows, :].astype(F32), other[0].astype(F32), other[1].astype(F32))
    sums = look_sums(jnp.concatenate(terms, axis=0), take[...])
    half_power = jnp.where(upper == 1, power[looks:], power[:looks])
    out[...] = normalised(sums, half_power, (1 - 2 * upper).astype(F32))
    for part in range(2):
        spread(own, part, wide, mine)


def first_matching(own, other, take):
    parts, lines, width = own.shape
    looks, cells = lines // LOOK_A, width // LOOK_R
    blocks = width // LANES
    shape = jax.ShapeDtypeStruct((looks, cells), F32)
    return pl.pallas_call(
        first_kernel,
        out_shape=(shape, shape, jax.ShapeDtypeStruct((parts, blocks, LOOK_A, looks, LANES), F32)),
        in_specs=[VMEM] * 3,
        out_specs=(VMEM,) * 3,
        scratch_shapes=[pltpu.VMEM((parts, blocks, lines + LOOK_A, LANES), F32)],
        name="first_matching",
        compiler_params=pltpu.CompilerParams(vmem_limit_bytes=4 * 2**20),
        cost_estimate=pl.CostEstimate(flops=2 * 2**20, bytes_accessed=2**18, transcendentals=0),
    )(own, other, take)


def whole_kernel(mine, other, take, power, first, out, wide):
    upper = (lax.axis_index("acq") >> 2) & 1
    blocks, looks = mine.shape[1], mine.shape[3]
    sums = 0.0
    for j in range(blocks):
        for part in range(2):
            wide[part, j, : other.shape[1]] = other[part, :, j * LANES : (j + 1) * LANES].astype(F32)
        total = 0.0
        for i in range(LOOK_A):
            their_re, their_im = (wide[part, j, pl.ds(i, looks, stride=LOOK_A), :] for part in range(2))
            terms = products(mine[0, j, i], mine[1, j, i], their_re, their_im)
            total = total + jnp.concatenate(terms, axis=0)
        sums = sums + dot_in_two(total, take[j * LANES : (j + 1) * LANES])
    whole = normalised(sums, power[...], (1 - 2 * upper).astype(F32))
    packed = jnp.concatenate([first[...], whole], axis=0)
    root = jnp.sqrt(jnp.abs(packed)) * UNIT
    out[...] = jnp.round(jnp.where(packed < 0, -root, root)).astype(jnp.int32).astype(jnp.int16)


def whole_pair(mine, other, take, power, first):
    rows, cells = first.shape
    parts, lines, width = other.shape
    return pl.pallas_call(
        whole_kernel,
        out_shape=jax.ShapeDtypeStruct((3 * rows, cells), jnp.int16),
        in_specs=[VMEM] * 5,
        out_specs=VMEM,
        scratch_shapes=[pltpu.VMEM((parts, width // LANES, lines + LOOK_A, LANES), F32)],
        name="whole_pair",
        compiler_params=pltpu.CompilerParams(vmem_limit_bytes=4 * 2**20),
        cost_estimate=pl.CostEstimate(flops=2 * 2**20, bytes_accessed=2**18, transcendentals=0),
    )(mine, other, take, power, first)


def take_kernel(take):
    sample = lax.broadcasted_iota(jnp.int32, take.shape, 0) // LOOK_R
    cell = lax.broadcasted_iota(jnp.int32, take.shape, 1)
    take[...] = (sample == cell).astype(F32).astype(BF16)


def taking(width):
    return pl.pallas_call(
        take_kernel,
        out_shape=jax.ShapeDtypeStruct((width, width // LOOK_R), BF16),
        out_specs=VMEM,
        name="taking",
        compiler_params=pltpu.CompilerParams(vmem_limit_bytes=2 * 2**20),
        cost_estimate=pl.CostEstimate(flops=2**17, bytes_accessed=2**18, transcendentals=0),
    )()


def select_kernel(blocks, own_cells, other_cells, band, onehot, masks, scale):
    lines, cols = own_cells.shape
    core = lax.axis_index("rng")
    first = (2 * lax.axis_index("acq") + core) * blocks
    own, other = own_cells[...], other_cells[...]
    left_core = core == 0
    halves = [jnp.where(left_core, own, other), jnp.where(left_core, other, own)]
    lane = lax.broadcasted_iota(jnp.int32, (cols, WIDE), 1).astype(F32)
    for side, cells in enumerate(halves):
        low = (cells & (WIDE - 1)).astype(F32)
        tall = jnp.concatenate([low] * (cols // lines), axis=0).T
        for line in range(lines):
            hit = tall[:, line : line + 1] == lane
            start = (line * 2 + side) * cols
            onehot[start : start + cols, :] = hit.astype(F32).astype(BF16)
    wide = jnp.concatenate(halves, axis=1) // WIDE
    mine = [(wide == first + block).astype(F32) for block in range(blocks)]
    for line in range(lines):
        for block in range(blocks):
            masks[line * blocks + block : line * blocks + block + 1, :] = mine[block][line : line + 1]
    count = jnp.zeros((blocks * lines, WIDE), F32)
    for line in range(lines):
        rows = masks[line * blocks : (line + 1) * blocks, :]
        rows = jnp.concatenate([rows] * lines, axis=0).astype(BF16)
        count = count + dot(rows, onehot[line * 2 * cols : (line + 1) * 2 * cols, :])
    scale[...] = 1.0 / jnp.maximum(count[:blocks], 1.0)
    shift = lax.broadcasted_iota(jnp.int32, (2 * cols, 2 * cols), 0)
    shift = jnp.abs(shift - lax.broadcasted_iota(jnp.int32, (2 * cols, 2 * cols), 1))
    band[...] = jnp.maximum(HALF_W + 1 - shift, 0).astype(F32).astype(BF16)


def select(blocks, own_cells, other_cells):
    lines, cols = own_cells.shape
    return pl.pallas_call(
        functools.partial(select_kernel, blocks),
        out_shape=(
            jax.ShapeDtypeStruct((2 * cols, 2 * cols), BF16),
            jax.ShapeDtypeStruct((lines * 2 * cols, WIDE), BF16),
            jax.ShapeDtypeStruct((lines * blocks, 2 * cols), F32),
            jax.ShapeDtypeStruct((blocks, WIDE), F32),
        ),
        in_specs=[VMEM, VMEM],
        out_specs=(VMEM,) * 4,
        name="select",
        compiler_params=pltpu.CompilerParams(vmem_limit_bytes=8 * 2**20),
        cost_estimate=pl.CostEstimate(flops=2 * 2**20, bytes_accessed=2**20, transcendentals=0),
    )(own_cells, other_cells)


def geocode_kernel(held, sent, band, onehot, masks, scale, out, by_acq, grid, filt):
    pairs = BLOCK // 2
    looks = held.shape[1] // 6
    lines, cols = 2 * looks, held.shape[2]
    planes = ROUNDS * pairs * 2
    blocks = scale.shape[0]
    rank, core = lax.axis_index("acq"), lax.axis_index("rng")
    origins = [(0, 0)]
    for step in STEPS:
        origins = origins + [(bits ^ mask, 1 - other) for mask in step for bits, other in origins]
    for slot, (bits, other) in enumerate(origins):
        acq, side = rank ^ bits, core ^ other
        by_acq[acq, side] = squared(held[slot].astype(jnp.int32))
        by_acq[acq, 1 - side] = squared(sent[slot].astype(jnp.int32))
    for side in range(2):
        columns = slice(side * cols, (side + 1) * cols)
        for acq in range(BLOCK):
            for part in range(2):
                row = (acq // 2 * 2 + part) * lines + (acq & 1) * looks
                grid[row : row + looks, columns] = by_acq[acq, side, part * looks : (part + 1) * looks, :]
            r, pair = WHOLE[acq >> 1]
            row = (r * pairs + pair + (acq & 1)) * 2 * lines
            grid[row : row + 2 * lines, columns] = by_acq[acq, side, lines:, :]
    smooth = dot_in_two(grid[...], band[...]) * (1.0 / (UNIT * (HALF_W + 1)) ** 2)
    smooth = smooth.reshape(planes // 2, 2, lines, 2 * cols)
    real, imag = smooth[:, 0], smooth[:, 1]
    gain = lax.rsqrt(jnp.sqrt(real * real + imag * imag + 0.01))
    filtered = (smooth * gain[:, None]).reshape(planes * lines, 2 * cols)
    for side in range(2):
        filt[side, : planes * lines] = filtered[:, side * cols : (side + 1) * cols]
    left = []
    for line in range(lines):
        value = [filt[side, pl.ds(line, planes, stride=lines), :] for side in range(2)]
        value = jnp.concatenate(value, axis=1)
        top = value.astype(BF16).astype(F32)
        both = jnp.concatenate([top, value - top], axis=0)
        rows = [both * masks[line * blocks + block : line * blocks + block + 1, :] for block in range(blocks)]
        left.append(jnp.concatenate(rows, axis=0).astype(BF16))
    middle = lines // 2
    sums = dot(jnp.concatenate(left[:middle], axis=1), onehot[: middle * 2 * cols, :])
    sums = sums + dot(jnp.concatenate(left[middle:], axis=1), onehot[middle * 2 * cols :, :])
    for block in range(blocks):
        start = block * 2 * planes
        total = sums[start : start + planes] + sums[start + planes : start + 2 * planes]
        total = total * scale[block : block + 1, :]
        for plane in range(0, planes, 2):
            r, pair = plane // (2 * pairs), plane // 2 % pairs
            out[r, pair, :, block * WIDE : (block + 1) * WIDE] = total[plane : plane + 2]


def geocode(held, sent, band, onehot, masks, scale):
    pairs, blocks = BLOCK // 2, scale.shape[0]
    _, rows, cols = held.shape
    lines = rows // 3
    return pl.pallas_call(
        geocode_kernel,
        out_shape=jax.ShapeDtypeStruct((ROUNDS, pairs, 2, blocks * WIDE), F32),
        in_specs=[VMEM] * 6,
        out_specs=VMEM,
        scratch_shapes=[
            pltpu.VMEM((BLOCK, 2, rows, cols), F32),
            pltpu.VMEM((ROUNDS * pairs * 2 * lines, 2 * cols), F32),
            pltpu.VMEM((2, (ROUNDS * pairs * 2 + 1) * lines, cols), F32),
        ],
        name="geocode",
        compiler_params=pltpu.CompilerParams(vmem_limit_bytes=8 * 2**20),
        cost_estimate=pl.CostEstimate(flops=2**28, bytes_accessed=2**21, transcendentals=2**16),
    )(held, sent, band, onehot, masks, scale)


def across(value, mask):
    pairs = [(2 * a + c, 2 * (a ^ mask) + 1 - c) for a in range(BLOCK) for c in range(2)]
    return lax.ppermute(value, ("acq", "rng"), pairs)


def swap(value):
    return lax.ppermute(value, "rng", [(0, 1), (1, 0)])


def gather_small(packed, chosen):
    held = packed[None]
    for step in STEPS[:-1]:
        held = jnp.concatenate([held] + [across(held, mask) for mask in step], axis=0)
    last = [across(held, mask) for mask in STEPS[-1]]
    early = swap(jnp.concatenate([held] + last[:1], axis=0))
    late = swap(jnp.concatenate(last[1:], axis=0))
    return geocode(jnp.concatenate([held] + last, axis=0), jnp.concatenate([early, late], axis=0), *chosen)


def gather_large(packed, map_cell):
    acq_count, rng_count = lax.axis_size("acq"), lax.axis_size("rng")
    pairs, piece = acq_count // 2, MAPC // (acq_count * rng_count)
    rows, cols = packed.shape
    lines, looks, width = rows // 3, rows // 6, rng_count * cols
    whole = lax.all_gather(packed, ("acq", "rng")).reshape(acq_count, rng_count, rows, cols)
    whole = whole.transpose(0, 2, 1, 3).reshape(acq_count, rows, width)
    whole = squared(whole) / UNIT**2
    halves = whole[:, :lines].reshape(pairs, 2, 2, looks, width)
    grids = [halves.transpose(0, 2, 1, 3, 4).reshape(pairs, 2, lines, width)]
    planes = whole[:, lines:].reshape(acq_count // BLOCK, 4, 2, 2, lines, width)
    for r in range(1, ROUNDS):
        quads = sorted((pair, quad) for quad, (found, pair) in enumerate(WHOLE) if found == r)
        grid = jnp.stack([planes[:, quad] for _, quad in quads], axis=1)
        grids.append(grid.reshape(pairs, 2, lines, width))
    gamma = jnp.stack(grids)
    padded = jnp.pad(gamma, [(0, 0)] * 4 + [(HALF_W, HALF_W)])
    smooth = jnp.zeros_like(gamma)
    for offset in range(-HALF_W, HALF_W + 1):
        weight = (HALF_W + 1 - abs(offset)) / float((HALF_W + 1) ** 2)
        smooth = smooth + weight * padded[..., HALF_W + offset : HALF_W + offset + width]
    power = smooth[:, :, 0] ** 2 + smooth[:, :, 1] ** 2 + 0.01
    filtered = smooth * (power ** (-0.25))[:, :, None]
    cells = lax.all_gather(map_cell, "rng", axis=1, tiled=True).reshape(-1, 1)
    first = (lax.axis_index("acq") * rng_count + lax.axis_index("rng")) * piece
    onehot = (cells == first + jnp.arange(piece, dtype=jnp.int32)).astype(F32)
    count = onehot.sum(axis=0)
    sums = jnp.dot(
        filtered.reshape(-1, cells.shape[0]), onehot, precision=lax.Precision.HIGHEST
    ).reshape(ROUNDS, pairs, 2, piece)
    return sums / jnp.maximum(count, 1.0)


def per_device(slc, map_cell):
    acq_count = lax.axis_size("acq")
    own = slc[:, 0]
    quarter = [(a & -BLOCK) + 2 * SEND[a % BLOCK // 2] + a % 2 for a in range(acq_count)]
    whole = lax.ppermute(own, "acq", list(enumerate(quarter)))
    half = lax.ppermute(pick(own), "acq", [(a, a ^ 1) for a in range(acq_count)])
    small = acq_count == BLOCK
    take = taking(own.shape[2])
    if small:
        blocks = MAPC // (acq_count * lax.axis_size("rng")) // WIDE
        chosen = select(blocks, map_cell, swap(map_cell))
        take, chosen = lax.optimization_barrier((take, chosen))
    first, power, mine = first_matching(own, half, take)
    packed = whole_pair(mine, whole, take, power, first)
    return gather_small(packed, chosen) if small else gather_large(packed, map_cell)


def solution(mesh):
    in_specs = (P(None, ("groups", "acq"), None, "rng"), P("groups", "rng"))
    out_specs = P(None, "groups", None, ("acq", "rng"))
    return jax.shard_map(
        per_device, mesh=mesh, in_specs=in_specs, out_specs=out_specs, check_vma=False
    )
```

```python
import functools

import jax
import jax.numpy as jnp
from jax import lax
from jax.experimental import pallas as pl
from jax.experimental.pallas import tpu as pltpu
from jax.sharding import PartitionSpec as P

LOOK_A = 8
LOOK_R = 8
HALF_W = 4
ROUNDS = 3
BLOCK = 2**ROUNDS
STEPS = ((4,), (3, 2, 1))
SEND = (2, 0, 3, 1)
WHOLE = ((1, 0), (2, 2), (2, 0), (1, 2))
MAPC = 16384
LANES = 128
WIDE = 256
UNIT = 32760.0
F32 = jnp.float32
BF16 = jnp.bfloat16

VMEM = pl.BlockSpec(memory_space=pltpu.VMEM)


def dot(left, right):
    return jnp.dot(left, right, preferred_element_type=F32)


def dot_in_two(left, right):
    rows = left.shape[0]
    high = left.astype(BF16).astype(F32)
    both = dot(jnp.concatenate([high, left - high], axis=0).astype(BF16), right)
    return both[:rows] + both[rows:]


def squared(root):
    root = root.astype(F32)
    return root * jnp.abs(root)


def pick_kernel(own, out):
    half = out.shape[1]
    upper = lax.axis_index("acq") & 1
    out[...] = own[:, pl.ds(pl.multiple_of((1 - upper) * half, half), half), :]


def pick(own):
    parts, lines, width = own.shape
    return pl.pallas_call(
        pick_kernel,
        out_shape=jax.ShapeDtypeStruct((parts, lines // 2, width), own.dtype),
        in_specs=[VMEM],
        out_specs=VMEM,
        name="pick",
        compiler_params=pltpu.CompilerParams(vmem_limit_bytes=2 * 2**20),
        cost_estimate=pl.CostEstimate(flops=2**10, bytes_accessed=2**18, transcendentals=0),
    )(own)


def look_sums(terms, take):
    sums = dot_in_two(terms, take)
    return sums.reshape(terms.shape[0] // LOOK_A, LOOK_A, take.shape[1]).sum(axis=1)


def products(mine_re, mine_im, their_re, their_im):
    return [
        mine_re * their_re + mine_im * their_im,
        mine_im * their_re - mine_re * their_im,
        their_re * their_re + their_im * their_im,
    ]


def normalised(sums, power, sign):
    looks = power.shape[0]
    inverse = lax.rsqrt(power * sums[2 * looks :] + 1e-06)
    return sums[: 2 * looks] * jnp.concatenate([inverse, inverse * sign], axis=0)


def spread(samples, part, wide, out):
    blocks, looks = wide.shape[1], out.shape[3]
    for j in range(blocks):
        wide[part, j, : samples.shape[1]] = samples[part, :, j * LANES : (j + 1) * LANES].astype(F32)
        for i in range(LOOK_A):
            out[part, j, i] = wide[part, j, pl.ds(i, looks, stride=LOOK_A), :]


def first_kernel(own, other, take, out, power, mine, wide):
    half = other.shape[1]
    looks = half // LOOK_A
    own_re, own_im = own[0].astype(F32), own[1].astype(F32)
    power[...] = look_sums(own_re * own_re + own_im * own_im, take[...])
    upper = lax.axis_index("acq") & 1
    rows = pl.ds(pl.multiple_of(upper * half, half), half)
    terms = products(own[0, rows, :].astype(F32), own[1, rows, :].astype(F32), other[0].astype(F32), other[1].astype(F32))
    sums = look_sums(jnp.concatenate(terms, axis=0), take[...])
    half_power = jnp.where(upper == 1, power[looks:], power[:looks])
    out[...] = normalised(sums, half_power, (1 - 2 * upper).astype(F32))
    for part in range(2):
        spread(own, part, wide, mine)


def first_matching(own, other, take):
    parts, lines, width = own.shape
    looks, cells = lines // LOOK_A, width // LOOK_R
    blocks = width // LANES
    shape = jax.ShapeDtypeStruct((looks, cells), F32)
    return pl.pallas_call(
        first_kernel,
        out_shape=(shape, shape, jax.ShapeDtypeStruct((parts, blocks, LOOK_A, looks, LANES), F32)),
        in_specs=[VMEM] * 3,
        out_specs=(VMEM,) * 3,
        scratch_shapes=[pltpu.VMEM((parts, blocks, lines + LOOK_A, LANES), F32)],
        name="first_matching",
        compiler_params=pltpu.CompilerParams(vmem_limit_bytes=4 * 2**20),
        cost_estimate=pl.CostEstimate(flops=2 * 2**20, bytes_accessed=2**18, transcendentals=0),
    )(own, other, take)


def whole_kernel(mine, other, take, power, first, out, wide):
    upper = (lax.axis_index("acq") >> 2) & 1
    blocks, looks = mine.shape[1], mine.shape[3]
    sums = 0.0
    for j in range(blocks):
        for part in range(2):
            wide[part, j, : other.shape[1]] = other[part, :, j * LANES : (j + 1) * LANES].astype(F32)
        total = 0.0
        for i in range(LOOK_A):
            their_re, their_im = (wide[part, j, pl.ds(i, looks, stride=LOOK_A), :] for part in range(2))
            terms = products(mine[0, j, i], mine[1, j, i], their_re, their_im)
            total = total + jnp.concatenate(terms, axis=0)
        sums = sums + dot_in_two(total, take[j * LANES : (j + 1) * LANES])
    whole = normalised(sums, power[...], (1 - 2 * upper).astype(F32))
    packed = jnp.concatenate([first[...], whole], axis=0)
    root = jnp.sqrt(jnp.abs(packed)) * UNIT
    out[...] = jnp.round(jnp.where(packed < 0, -root, root)).astype(jnp.int32).astype(jnp.int16)


def whole_pair(mine, other, take, power, first):
    rows, cells = first.shape
    parts, lines, width = other.shape
    return pl.pallas_call(
        whole_kernel,
        out_shape=jax.ShapeDtypeStruct((3 * rows, cells), jnp.int16),
        in_specs=[VMEM] * 5,
        out_specs=VMEM,
        scratch_shapes=[pltpu.VMEM((parts, width // LANES, lines + LOOK_A, LANES), F32)],
        name="whole_pair",
        compiler_params=pltpu.CompilerParams(vmem_limit_bytes=4 * 2**20),
        cost_estimate=pl.CostEstimate(flops=2 * 2**20, bytes_accessed=2**18, transcendentals=0),
    )(mine, other, take, power, first)


def take_kernel(take):
    sample = lax.broadcasted_iota(jnp.int32, take.shape, 0) // LOOK_R
    cell = lax.broadcasted_iota(jnp.int32, take.shape, 1)
    take[...] = (sample == cell).astype(F32).astype(BF16)


def taking(width):
    return pl.pallas_call(
        take_kernel,
        out_shape=jax.ShapeDtypeStruct((width, width // LOOK_R), BF16),
        out_specs=VMEM,
        name="taking",
        compiler_params=pltpu.CompilerParams(vmem_limit_bytes=2 * 2**20),
        cost_estimate=pl.CostEstimate(flops=2**17, bytes_accessed=2**18, transcendentals=0),
    )()


def select_kernel(blocks, own_cells, other_cells, band, onehot, masks, scale):
    lines, cols = own_cells.shape
    core = lax.axis_index("rng")
    first = (2 * lax.axis_index("acq") + core) * blocks
    own, other = own_cells[...], other_cells[...]
    left_core = core == 0
    halves = [jnp.where(left_core, own, other), jnp.where(left_core, other, own)]
    lane = lax.broadcasted_iota(jnp.int32, (cols, WIDE), 1).astype(F32)
    for side, cells in enumerate(halves):
        low = (cells & (WIDE - 1)).astype(F32)
        tall = jnp.concatenate([low] * (cols // lines), axis=0).T
        for line in range(lines):
            hit = tall[:, line : line + 1] == lane
            start = (line * 2 + side) * cols
            onehot[start : start + cols, :] = hit.astype(F32).astype(BF16)
    wide = jnp.concatenate(halves, axis=1) // WIDE
    mine = [(wide == first + block).astype(F32) for block in range(blocks)]
    for line in range(lines):
        for block in range(blocks):
            masks[line * blocks + block : line * blocks + block + 1, :] = mine[block][line : line + 1]
    count = jnp.zeros((blocks * lines, WIDE), F32)
    for line in range(lines):
        rows = masks[line * blocks : (line + 1) * blocks, :]
        rows = jnp.concatenate([rows] * lines, axis=0).astype(BF16)
        count = count + dot(rows, onehot[line * 2 * cols : (line + 1) * 2 * cols, :])
    scale[...] = 1.0 / jnp.maximum(count[:blocks], 1.0)
    shift = lax.broadcasted_iota(jnp.int32, (2 * cols, 2 * cols), 0)
    shift = jnp.abs(shift - lax.broadcasted_iota(jnp.int32, (2 * cols, 2 * cols), 1))
    band[...] = jnp.maximum(HALF_W + 1 - shift, 0).astype(F32).astype(BF16)


def select(blocks, own_cells, other_cells):
    lines, cols = own_cells.shape
    return pl.pallas_call(
        functools.partial(select_kernel, blocks),
        out_shape=(
            jax.ShapeDtypeStruct((2 * cols, 2 * cols), BF16),
            jax.ShapeDtypeStruct((lines * 2 * cols, WIDE), BF16),
            jax.ShapeDtypeStruct((lines * blocks, 2 * cols), F32),
            jax.ShapeDtypeStruct((blocks, WIDE), F32),
        ),
        in_specs=[VMEM, VMEM],
        out_specs=(VMEM,) * 4,
        name="select",
        compiler_params=pltpu.CompilerParams(vmem_limit_bytes=8 * 2**20),
        cost_estimate=pl.CostEstimate(flops=2 * 2**20, bytes_accessed=2**20, transcendentals=0),
    )(own_cells, other_cells)


def geocode_kernel(held, sent, band, onehot, masks, scale, out, by_acq, grid, filt):
    pairs = BLOCK // 2
    looks = held.shape[1] // 6
    lines, cols = 2 * looks, held.shape[2]
    planes = ROUNDS * pairs * 2
    blocks = scale.shape[0]
    rank, core = lax.axis_index("acq"), lax.axis_index("rng")
    origins = [(0, 0)]
    for step in STEPS:
        origins = origins + [(bits ^ mask, 1 - other) for mask in step for bits, other in origins]
    for slot, (bits, other) in enumerate(origins):
        acq, side = rank ^ bits, core ^ other
        by_acq[acq, side] = squared(held[slot].astype(jnp.int32))
        by_acq[acq, 1 - side] = squared(sent[slot].astype(jnp.int32))
    for side in range(2):
        columns = slice(side * cols, (side + 1) * cols)
        for acq in range(BLOCK):
            for part in range(2):
                row = (acq // 2 * 2 + part) * lines + (acq & 1) * looks
                grid[row : row + looks, columns] = by_acq[acq, side, part * looks : (part + 1) * looks, :]
            r, pair = WHOLE[acq >> 1]
            row = (r * pairs + pair + (acq & 1)) * 2 * lines
            grid[row : row + 2 * lines, columns] = by_acq[acq, side, lines:, :]
    smooth = dot_in_two(grid[...], band[...]) * (1.0 / (UNIT * (HALF_W + 1)) ** 2)
    smooth = smooth.reshape(planes // 2, 2, lines, 2 * cols)
    real, imag = smooth[:, 0], smooth[:, 1]
    gain = lax.rsqrt(jnp.sqrt(real * real + imag * imag + 0.01))
    filtered = (smooth * gain[:, None]).reshape(planes * lines, 2 * cols)
    for side in range(2):
        filt[side, : planes * lines] = filtered[:, side * cols : (side + 1) * cols]
    left = []
    for line in range(lines):
        value = [filt[side, pl.ds(line, planes, stride=lines), :] for side in range(2)]
        value = jnp.concatenate(value, axis=1)
        top = value.astype(BF16).astype(F32)
        both = jnp.concatenate([top, value - top], axis=0)
        rows = [both * masks[line * blocks + block : line * blocks + block + 1, :] for block in range(blocks)]
        left.append(jnp.concatenate(rows, axis=0).astype(BF16))
    sums = dot(jnp.concatenate(left, axis=1), onehot[...])
    for block in range(blocks):
        start = block * 2 * planes
        total = sums[start : start + planes] + sums[start + planes : start + 2 * planes]
        total = total * scale[block : block + 1, :]
        for plane in range(0, planes, 2):
            r, pair = plane // (2 * pairs), plane // 2 % pairs
            out[r, pair, :, block * WIDE : (block + 1) * WIDE] = total[plane : plane + 2]


def geocode(held, sent, band, onehot, masks, scale):
    pairs, blocks = BLOCK // 2, scale.shape[0]
    _, rows, cols = held.shape
    lines = rows // 3
    return pl.pallas_call(
        geocode_kernel,
        out_shape=jax.ShapeDtypeStruct((ROUNDS, pairs, 2, blocks * WIDE), F32),
        in_specs=[VMEM] * 6,
        out_specs=VMEM,
        scratch_shapes=[
            pltpu.VMEM((BLOCK, 2, rows, cols), F32),
            pltpu.VMEM((ROUNDS * pairs * 2 * lines, 2 * cols), F32),
            pltpu.VMEM((2, (ROUNDS * pairs * 2 + 1) * lines, cols), F32),
        ],
        name="geocode",
        compiler_params=pltpu.CompilerParams(vmem_limit_bytes=8 * 2**20),
        cost_estimate=pl.CostEstimate(flops=2**28, bytes_accessed=2**21, transcendentals=2**16),
    )(held, sent, band, onehot, masks, scale)


def across(value, mask):
    pairs = [(2 * a + c, 2 * (a ^ mask) + 1 - c) for a in range(BLOCK) for c in range(2)]
    return lax.ppermute(value, ("acq", "rng"), pairs)


def swap(value):
    return lax.ppermute(value, "rng", [(0, 1), (1, 0)])


def gather_small(packed, chosen):
    held = packed[None]
    for step in STEPS[:-1]:
        held = jnp.concatenate([held] + [across(held, mask) for mask in step], axis=0)
    last = [across(held, mask) for mask in STEPS[-1]]
    early = swap(jnp.concatenate([held] + last[:1], axis=0))
    late = swap(jnp.concatenate(last[1:], axis=0))
    return geocode(jnp.concatenate([held] + last, axis=0), jnp.concatenate([early, late], axis=0), *chosen)


def gather_large(packed, map_cell):
    acq_count, rng_count = lax.axis_size("acq"), lax.axis_size("rng")
    pairs, piece = acq_count // 2, MAPC // (acq_count * rng_count)
    rows, cols = packed.shape
    lines, looks, width = rows // 3, rows // 6, rng_count * cols
    whole = lax.all_gather(packed, ("acq", "rng")).reshape(acq_count, rng_count, rows, cols)
    whole = whole.transpose(0, 2, 1, 3).reshape(acq_count, rows, width)
    whole = squared(whole) / UNIT**2
    halves = whole[:, :lines].reshape(pairs, 2, 2, looks, width)
    grids = [halves.transpose(0, 2, 1, 3, 4).reshape(pairs, 2, lines, width)]
    planes = whole[:, lines:].reshape(acq_count // BLOCK, 4, 2, 2, lines, width)
    for r in range(1, ROUNDS):
        quads = sorted((pair, quad) for quad, (found, pair) in enumerate(WHOLE) if found == r)
        grid = jnp.stack([planes[:, quad] for _, quad in quads], axis=1)
        grids.append(grid.reshape(pairs, 2, lines, width))
    gamma = jnp.stack(grids)
    padded = jnp.pad(gamma, [(0, 0)] * 4 + [(HALF_W, HALF_W)])
    smooth = jnp.zeros_like(gamma)
    for offset in range(-HALF_W, HALF_W + 1):
        weight = (HALF_W + 1 - abs(offset)) / float((HALF_W + 1) ** 2)
        smooth = smooth + weight * padded[..., HALF_W + offset : HALF_W + offset + width]
    power = smooth[:, :, 0] ** 2 + smooth[:, :, 1] ** 2 + 0.01
    filtered = smooth * (power ** (-0.25))[:, :, None]
    cells = lax.all_gather(map_cell, "rng", axis=1, tiled=True).reshape(-1, 1)
    first = (lax.axis_index("acq") * rng_count + lax.axis_index("rng")) * piece
    onehot = (cells == first + jnp.arange(piece, dtype=jnp.int32)).astype(F32)
    count = onehot.sum(axis=0)
    sums = jnp.dot(
        filtered.reshape(-1, cells.shape[0]), onehot, precision=lax.Precision.HIGHEST
    ).reshape(ROUNDS, pairs, 2, piece)
    return sums / jnp.maximum(count, 1.0)


def per_device(slc, map_cell):
    acq_count = lax.axis_size("acq")
    own = slc[:, 0]
    quarter = [(a & -BLOCK) + 2 * SEND[a % BLOCK // 2] + a % 2 for a in range(acq_count)]
    whole = lax.ppermute(own, "acq", list(enumerate(quarter)))
    half = lax.ppermute(pick(own), "acq", [(a, a ^ 1) for a in range(acq_count)])
    small = acq_count == BLOCK
    take = taking(own.shape[2])
    if small:
        blocks = MAPC // (acq_count * lax.axis_size("rng")) // WIDE
        chosen = select(blocks, map_cell, swap(map_cell))
        take, chosen = lax.optimization_barrier((take, chosen))
    first, power, mine = first_matching(own, half, take)
    packed = whole_pair(mine, whole, take, power, first)
    return gather_small(packed, chosen) if small else gather_large(packed, map_cell)


def solution(mesh):
    in_specs = (P(None, ("groups", "acq"), None, "rng"), P("groups", "rng"))
    out_specs = P(None, "groups", None, ("acq", "rng"))
    return jax.shard_map(
        per_device, mesh=mesh, in_specs=in_specs, out_specs=out_specs, check_vma=False
    )
```
